32 devices in a mesh: shard: 4 (over y, x), context: 4 (over z), tensor: 2 (over core).
Axes of the slice: x: 2, y: 2, z: 4, core: 2. Of those that a mesh axis runs over, the one named last changes fastest.
Arguments:
- hidden_in: bfloat16 [4, 8, 1024, 768], P(None, 'shard', 'context'), may hold values from -6 to 6
- out_grad: bfloat16 [4, 8, 1024, 768], P(None, 'shard', 'context'), may hold values from -6 to 6
- doc_start: int32 [4, 8, 1024], P(None, 'shard', 'context'), may hold values from 0 to 964, as said below
- norm_in: float32 [768], replicated, may hold values from 0.5 to 1.5
- w_z: bfloat16 [768, 1536], P(('shard', 'context'), 'tensor'), may hold values from -0.21875 to 0.21875
- w_x: bfloat16 [768, 1536], P(('shard', 'context'), 'tensor'), may hold values from -0.21875 to 0.21875
- w_bc: bfloat16 [768, 256], P(('shard', 'context'), 'tensor'), may hold values from -0.21875 to 0.21875
- w_dt: bfloat16 [768, 24], P(('shard', 'context'), 'tensor'), may hold values from -0.21875 to 0.21875
- conv_x: float32 [5, 1536], P(None, 'tensor'), may hold values from -0.5 to 0.5
- conv_bc: float32 [5, 256], P(None, 'tensor'), may hold values from -0.5 to 0.5
- dt_bias: float32 [24], P('tensor'), may hold values from -6 to -2
- a_log: float32 [24], P('tensor'), may hold values from -2 to 1
- skip_d: float32 [24], P('tensor'), may hold values from 0.5 to 1.5
- norm_gate: float32 [1536], P('tensor'), may hold values from 0.5 to 1.5
- w_out: bfloat16 [1536, 768], P('tensor', ('shard', 'context')), may hold values from -0.15625 to 0.15625
Outputs:
- out_hidden: bfloat16 [4, 8, 1024, 768], P(None, 'shard', 'context')
- in_grad: bfloat16 [4, 8, 1024, 768], P(None, 'shard', 'context')
- grad_norm_in: float32 [768], replicated
- grad_w_z: float32 [768, 1536], P(('shard', 'context'), 'tensor')
- grad_w_x: float32 [768, 1536], P(('shard', 'context'), 'tensor')
- grad_w_bc: float32 [768, 256], P(('shard', 'context'), 'tensor')
- grad_w_dt: float32 [768, 24], P(('shard', 'context'), 'tensor')
- grad_conv_x: float32 [5, 1536], P(None, 'tensor')
- grad_conv_bc: float32 [5, 256], P(None, 'tensor')
- grad_dt_bias: float32 [24], P('tensor')
- grad_a_log: float32 [24], P('tensor')
- grad_skip_d: float32 [24], P('tensor')
- grad_norm_gate: float32 [1536], P('tensor')
- grad_w_out: float32 [1536, 768], P('tensor', ('shard', 'context'))
The draws below stay inside these ranges and needn't reach their ends.
Inputs may be any that keep to these rules, and one draw needn't show every extreme that they name: doc_start[m, s, t] is the first position of the document that holds position t of sequence s; documents follow one another up to the sequence's end, the last one exactly 60 positions long and the others 60 to 800, except the first, which the sequence's start may cut; in each micro-batch, one sequence of each aligned group of 2 instead holds three documents: a first one of 60 to 255 positions, then one that runs up to position 963, then the last one of 60 positions.
All inputs are finite; a program needn't handle non-finite values.
Results may differ from the reference program's by a relative error of at most 0.0083.
Values may be sent and summed in bfloat16 or wider, within the bound.
A program may use at most 256 MiB of HBM per device.

```python
import jax
import jax.numpy as jnp
from jax import lax

D = 768
HEADS = 24
HEAD = 64
STATE = 128
CONV = 4
PIECE = 256
SEQ_DEV = 2
MB = 4
MIN_DOC = 60
MAX_DOC = 800
INNER = 1536
LENGTH = 1024
SEQS = 8


def draw_doc_start(key, part):
    key = jax.random.fold_in(key, 11)
    key_lengths, key_whole, key_cut = jax.random.split(key, 3)
    slots = LENGTH // MIN_DOC + 2
    doc_lengths = jax.random.randint(key_lengths, (MB, SEQS, slots), MIN_DOC, MAX_DOC + 1).astype(jnp.int32)
    first_slot = jnp.arange(slots, dtype=jnp.int32) == 0
    doc_lengths = jnp.where(first_slot[None, None, :], MIN_DOC, doc_lengths).astype(jnp.int32)
    bounds = jnp.maximum(LENGTH - jnp.cumsum(doc_lengths, -1), 0).astype(jnp.int32)
    position = jnp.arange(LENGTH, dtype=jnp.int32)
    reached = bounds[:, :, None, :] <= position[None, None, :, None]
    starts = jnp.max(jnp.where(reached, bounds[:, :, None, :], 0), -1)
    cut = jax.random.randint(key_cut, (MB, SEQS), MIN_DOC, PIECE).astype(jnp.int32)
    last_start = LENGTH - MIN_DOC
    spanning = jnp.where(position[None, None, :] < cut[:, :, None], 0, jnp.where(position[None, None, :] < last_start, cut[:, :, None], last_start)).astype(jnp.int32)
    group_count = SEQS // SEQ_DEV
    chosen = jax.random.randint(key_whole, (MB, group_count), 0, SEQ_DEV).astype(jnp.int32)
    within = jnp.arange(SEQS, dtype=jnp.int32) % SEQ_DEV
    picked = jnp.repeat(chosen, SEQ_DEV, axis=1) == within[None, :]
    return jnp.where(picked[:, :, None], spanning, starts).astype(jnp.int32)


def block_levels(rng, extent, cuts, smallest, largest):
    def one(axis_at, shards_of):
        draws = jax.random.uniform(jax.random.fold_in(jax.random.fold_in(rng, 6), axis_at), (shards_of,), jnp.float32, smallest / len(cuts), largest / len(cuts))
        return jnp.repeat(jnp.exp(draws), extent[axis_at] // shards_of).reshape((-1,) + (1,) * (len(extent) - axis_at - 1))

    gain = one(*cuts[0])
    for cut in cuts[1:]:
        gain = gain * one(*cut)
    return gain


def gaussian(rng, dims, scale, bound, shards=(), kind=jnp.bfloat16):
    factor_of = block_levels(rng, dims, shards, -0.22, 0.18) if shards else 1.0
    values = jax.random.normal(rng, dims, jnp.float32) * scale * factor_of
    return jnp.minimum(jnp.maximum(values, -bound), bound).astype(kind)


def setup_inputs(seed: int = 0) -> dict:
    key_list = jax.random.split(jax.random.key(seed), 16)
    return {
        "hidden_in": gaussian(key_list[0], (MB, SEQS, LENGTH, D), 1.0, 6.0, ((1, 4), (2, 4))),
        "out_grad": gaussian(key_list[1], (MB, SEQS, LENGTH, D), 1.0, 6.0, ((1, 4), (2, 4))),
        "doc_start": draw_doc_start(jax.random.fold_in(key_list[15], 71), 0),
        "norm_in": jnp.clip(1.0 + 0.1 * jax.random.normal(key_list[3], (D,), jnp.float32), 0.5, 1.5),
        "w_z": gaussian(key_list[4], (D, INNER), D ** -0.5, 0.21875, ((0, 16), (1, 2))),
        "w_x": gaussian(key_list[5], (D, INNER), D ** -0.5, 0.21875, ((0, 16), (1, 2))),
        "w_bc": gaussian(key_list[6], (D, 2 * STATE), D ** -0.5, 0.21875, ((0, 16), (1, 2))),
        "w_dt": gaussian(key_list[7], (D, HEADS), D ** -0.5, 0.21875, ((0, 16), (1, 2))),
        "conv_x": jnp.clip(jax.random.uniform(key_list[8], (CONV + 1, INNER), jnp.float32, -0.5, 0.5) * block_levels(key_list[8], (CONV + 1, INNER), ((1, 2),), -0.4, 0.0), -0.5, 0.5),
        "conv_bc": jnp.clip(jax.random.uniform(key_list[9], (CONV + 1, 2 * STATE), jnp.float32, -0.5, 0.5) * block_levels(key_list[9], (CONV + 1, 2 * STATE), ((1, 2),), -0.4, 0.0), -0.5, 0.5),
        "dt_bias": jnp.clip(-6.0 + 4.0 * jax.random.uniform(key_list[10], (HEADS,), jnp.float32) ** block_levels(key_list[10], (HEADS,), ((0, 2),), -0.2, 0.2), -6.0, -2.0),
        "a_log": jnp.clip(-2.0 + 3.0 * jax.random.uniform(key_list[11], (HEADS,), jnp.float32) ** block_levels(key_list[11], (HEADS,), ((0, 2),), -0.2, 0.2), -2.0, 1.0),
        "skip_d": jnp.clip(0.5 + 1.0 * jax.random.uniform(key_list[12], (HEADS,), jnp.float32) ** block_levels(key_list[12], (HEADS,), ((0, 2),), -0.2, 0.2), 0.5, 1.5),
        "norm_gate": jnp.clip(1.0 + 0.1 * jax.random.normal(key_list[13], (INNER,), jnp.float32), 0.5, 1.5),
        "w_out": gaussian(key_list[14], (INNER, D), INNER ** -0.5, 0.15625, ((0, 2), (1, 16))),
    }


EPSILON = 1e-05
HIGHEST = lax.Precision.HIGHEST

@jax.custom_vjp
def low(v):
    return lax.optimization_barrier(v.astype(jnp.bfloat16)).astype(jnp.float32)

@jax.custom_vjp
def low_back(v):
    return v

def low_keep(v):
    return (low(v), None)

def low_pass(kept, grad):
    return (grad,)

def back_keep(v):
    return (v, None)

def back_low(kept, grad):
    return (low(grad),)
low.defvjp(low_keep, low_pass)
low_back.defvjp(back_keep, back_low)

def matmul(left, right):
    return jnp.dot(left, right, precision=HIGHEST, preferred_element_type=jnp.float32)

def flag(condition):
    return jnp.where(condition, 1.0, 0.0).astype(jnp.float32)

def conv_block(channels, weights, starts):
    length = channels.shape[0]
    position = jnp.arange(length, dtype=jnp.int32)
    running = jnp.zeros_like(channels) + weights[4]
    for lag_count in range(4):
        tapped = jnp.concatenate([jnp.zeros((lag_count, channels.shape[1]), jnp.float32), channels[:length - lag_count]], 0)
        keep_tap = (position - lag_count >= starts)[:, None]
        running = running + weights[lag_count] * jnp.where(keep_tap, tapped, 0.0)
    return jax.nn.silu(running)

def piece_setup(conv_x_out, conv_bc_out, dt_raw, dt_bias, a_log):
    step_size = jax.nn.softplus(dt_raw + dt_bias)
    cumulative = jnp.cumsum(-jnp.exp(a_log) * step_size, 0).T
    length, head_count = dt_raw.shape
    values = conv_x_out.reshape(length, head_count, -1).transpose(1, 0, 2)
    half_width = conv_bc_out.shape[1] // 2
    return (step_size.T, cumulative, values, conv_bc_out[:, :half_width], conv_bc_out[:, half_width:])

def state_part(conv_x_out, conv_bc_out, dt_raw, dt_bias, a_log, starts, offset):
    step_size, cumulative, values, inputs_b, readout = piece_setup(conv_x_out, conv_bc_out, dt_raw, dt_bias, a_log)
    position = offset + jnp.arange(dt_raw.shape[0], dtype=jnp.int32)
    weight_end = jnp.exp(cumulative[:, -1:] - cumulative) * flag(position >= starts[-1])[None, :] * step_size
    local_state = jnp.einsum('hjp,jn->hpn', values * weight_end[:, :, None], inputs_b, precision=HIGHEST)
    decay_total = jnp.exp(cumulative[:, -1]) * flag(starts[-1] < offset)
    return (decay_total, local_state)

def output_part(conv_x_out, conv_bc_out, dt_raw, dt_bias, a_log, skip_d, state_in, starts, offset):
    step_size, cumulative, values, inputs_b, readout = piece_setup(conv_x_out, conv_bc_out, dt_raw, dt_bias, a_log)
    length = dt_raw.shape[0]
    position = offset + jnp.arange(length, dtype=jnp.int32)
    row_index = jnp.arange(length, dtype=jnp.int32)[:, None]
    col_index = jnp.arange(length, dtype=jnp.int32)[None, :]
    causal = (col_index <= row_index) & (position[None, :] >= starts[:, None])
    spread = cumulative[:, :, None] - cumulative[:, None, :]
    decay_mat = jnp.where(causal[None], jnp.exp(jnp.minimum(spread, 0.0)), 0.0)
    intersection = jnp.einsum('in,jn->ij', readout, inputs_b, precision=HIGHEST)
    mixing = intersection[None] * decay_mat * step_size[:, None, :]
    within = jnp.einsum('hij,hjp->hip', mixing, values, precision=HIGHEST)
    carried_in = jnp.exp(cumulative) * flag(starts < offset)[None, :]
    across = carried_in[:, :, None] * jnp.einsum('in,hpn->hip', readout, state_in, precision=HIGHEST)
    result = within + across + skip_d[:, None, None] * values
    return result.transpose(1, 0, 2).reshape(length, -1)

def sequence(hidden, starts, params):
    norm_in, w_z, w_x, w_bc, w_dt, conv_x, conv_bc, dt_bias, a_log, skip_d, norm_gate, w_out = params
    scale_in = lax.rsqrt(lax.optimization_barrier(jnp.mean(hidden * hidden, -1, keepdims=True)) + EPSILON)
    normed = low(hidden * scale_in * norm_in)
    gate_raw = low_back(matmul(normed, w_z))
    x_raw = low_back(matmul(normed, w_x))
    bc_raw = low_back(matmul(normed, w_bc))
    dt_raw = low_back(matmul(normed, w_dt))
    convolved_output = conv_block(jnp.concatenate([x_raw, bc_raw], 1), jnp.concatenate([conv_x, conv_bc], 1), starts)
    inner_width = x_raw.shape[1]
    conv_x_out = convolved_output[:, :inner_width]
    conv_bc_out = convolved_output[:, inner_width:]
    piece_count = LENGTH // PIECE
    offsets = jnp.arange(piece_count, dtype=jnp.int32) * PIECE

    def advance(state_in, piece_item):
        part_x, part_bc, part_dt, part_starts, offset = piece_item
        mixing_out = output_part(part_x, part_bc, part_dt, dt_bias, a_log, skip_d, state_in, part_starts, offset)
        decay_total, local_state = state_part(part_x, part_bc, part_dt, dt_bias, a_log, part_starts, offset)
        return (decay_total[:, None, None] * state_in + local_state, mixing_out)
    start_state = jnp.zeros((HEADS, HEAD, STATE), jnp.float32)
    unused, pieces = lax.scan(jax.checkpoint(advance), start_state, (conv_x_out.reshape(piece_count, PIECE, -1), conv_bc_out.reshape(piece_count, PIECE, -1), dt_raw.reshape(piece_count, PIECE, -1), starts.reshape(piece_count, PIECE), offsets))
    mixer = pieces.reshape(LENGTH, -1)
    gated_out = mixer * jax.nn.silu(gate_raw)
    scale_gate = lax.rsqrt(lax.optimization_barrier(jnp.mean(gated_out * gated_out, -1, keepdims=True)) + EPSILON)
    branch = matmul(low(gated_out * scale_gate * norm_gate), w_out)
    return hidden + branch

def reference(hidden_in, out_grad, doc_start, norm_in, w_z, w_x, w_bc, w_dt, conv_x, conv_bc, dt_bias, a_log, skip_d, norm_gate, w_out):
    params = tuple((array.astype(jnp.float32) for array in (norm_in, w_z, w_x, w_bc, w_dt, conv_x, conv_bc, dt_bias, a_log, skip_d, norm_gate, w_out)))
    sequences = hidden_in.astype(jnp.float32).reshape(-1, LENGTH, D)
    starts_all = doc_start.reshape(-1, LENGTH).astype(jnp.int32)

    def whole(inputs_all, weights_all):
        return lax.map(lambda pair_item: jax.checkpoint(sequence)(pair_item[0], pair_item[1], weights_all), (inputs_all, starts_all))
    output, pullback = jax.vjp(whole, sequences, params)
    input_grad, weight_grads = pullback(out_grad.astype(jnp.float32).reshape(-1, LENGTH, D))
    shape_full = hidden_in.shape
    return (output.reshape(shape_full).astype(jnp.bfloat16), input_grad.reshape(shape_full).astype(jnp.bfloat16), weight_grads[0], weight_grads[1], weight_grads[2], weight_grads[3], weight_grads[4], weight_grads[5], weight_grads[6], weight_grads[7], weight_grads[8], weight_grads[9], weight_grads[10], weight_grads[11])
```

```python
import functools

import jax
import jax.numpy as jnp
import numpy as np
from jax import lax
from jax.experimental import pallas as pl
from jax.experimental.pallas import tpu as pltpu
from jax.sharding import PartitionSpec as P

EPSILON = 1e-05
F32, BF16 = jnp.float32, jnp.bfloat16
HEAD = 64
LANES = 128
HALO = 16
GONE = -1e30
VMEM_BYTES = 60 * 1024 * 1024


def mm(left, right):
    return jnp.dot(left, right, preferred_element_type=F32)


def mm_nt(left, right):
    return lax.dot_general(left, right, (((1,), (1,)), ((), ())), preferred_element_type=F32)


def mm_tn(left, right):
    return lax.dot_general(left, right, (((0,), (0,)), ((), ())), preferred_element_type=F32)


def parts_of(value, count):
    parts = []
    for _ in range(count - 1):
        parts.append(value.astype(BF16))
        value = value - parts[-1].astype(F32)
    return parts + [value.astype(BF16)]


def pick(value, ones, count=2):
    return sum(mm(part, ones) for part in parts_of(value, count))


def pick_left(ones, value, count=3):
    return sum(mm(ones, part) for part in parts_of(value, count))


def softplus(value):
    return jnp.maximum(value, 0.0) + jnp.log1p(jnp.exp(-jnp.abs(value)))


def sigmoid(value):
    return 1.0 / (1.0 + jnp.exp(-value))


def column_blocks(width):
    return [(at, min(LANES, width - at)) for at in range(0, width, LANES)]


def row_index(length):
    return lax.broadcasted_iota(jnp.int32, (length, LANES), 0).astype(F32)


def is_first_step():
    return pl.program_id(0) == 0


def is_last_step():
    return pl.program_id(0) == pl.num_programs(0) - 1


def half_masks(width):
    lane = lax.broadcasted_iota(jnp.int32, (1, width), 1)
    return [(lane // HEAD) == k for k in range(width // HEAD)]


def normalised(hidden, gain):
    scale = lax.rsqrt(jnp.mean(hidden * hidden, -1, keepdims=True) + EPSILON)
    return hidden * scale * gain, scale


def forward_local(hid, halo, age, norm_in, w_in, taps, heads, spread, tri,
                  normed, raw, pre, dt_raw, cum, local, decay, act):
    length = hid.shape[1]
    channels = taps.shape[1]
    bc_width = 2 * LANES
    normed[0, :HALO] = normalised(halo[0].astype(F32), norm_in[...])[0].astype(BF16)
    for at in range(0, length, 64):
        rows = normalised(hid[0, at : at + 64].astype(F32), norm_in[...])[0]
        normed[0, HALO + at : HALO + at + 64] = rows.astype(BF16)
    raw[0, :, :bc_width] = mm(normed[0], w_in[:, :bc_width])
    raw[0, :, bc_width:] = mm(normed[0], w_in[:, bc_width + LANES :])
    dt_raw[0] = mm(normed[0, HALO:], w_in[:, bc_width : bc_width + LANES])
    for at, width in column_blocks(channels):
        cols = slice(at, at + width)
        running = jnp.broadcast_to(taps[4:5, cols], (length, width))
        for lag in range(4):
            tapped = raw[0, HALO - lag : HALO - lag + length, cols]
            if lag:
                tapped = jnp.where(age[0, :, :width] >= lag, tapped, 0.0)
            running = running + taps[lag : lag + 1, cols] * tapped
        pre[0, :, cols] = running
        act[:, cols] = running * sigmoid(running)
    step = softplus(dt_raw[0] + heads[0:1])
    total = pick_left(tri[...], -jnp.exp(heads[1:2]) * step)
    cum[0] = total
    last, age_last = total[length - 1 :], age[0, length - 1 :]
    open_end = row_index(length) - (length - 1) + age_last >= 0
    weight = jnp.where(open_end, jnp.exp(last - total), 0.0) * step
    weighted = (act[:, bc_width:] * pick(weight, spread[...])).astype(BF16)
    local[0] = mm_tn(act[:, :LANES].astype(BF16), weighted).astype(BF16)
    kept = jnp.where(age_last > length - 1, jnp.exp(last), 0.0)
    decay[0] = pick(jnp.broadcast_to(kept, (8, LANES)), spread[...], 3)


def forward_mix(pre, dt_raw, cum, age, state_in, normed, out_grad, w_z, w_out_t, norm_gate, skip, heads, spread,
                mixer, gate, grad_gn, part, stats, near, seg, pair, carried, step_x, gated_low):
    length, inner = mixer.shape[1:]
    bc_width = 2 * LANES
    readout = pre[0, :, LANES:bc_width]
    readout = (readout * sigmoid(readout)).astype(BF16)
    inputs_b = pre[0, :, :LANES]
    inputs_b = (inputs_b * sigmoid(inputs_b)).astype(BF16)
    gate[0] = mm(normed[0, HALO:], w_z[...])
    grad_gn[0] = mm(out_grad[0], w_out_t[...])
    pair[...] = mm_nt(readout, inputs_b)
    row = lax.broadcasted_iota(jnp.int32, (length, length), 0)
    col = lax.broadcasted_iota(jnp.int32, (length, length), 1)
    back = (row - col).astype(F32)
    seg[...] = jnp.where((back >= 0) & (back <= age[0][:, :1]), 0.0, GONE)
    total = cum[0]
    total_t = total.T
    step = softplus(dt_raw[0] + heads[0:1])
    step_x[...] = pick(step, spread[...])
    open_start = age[0] > row_index(length)
    carried[...] = pick(jnp.where(open_start, jnp.exp(total), 0.0), spread[...])
    carried[...] = carried[...] * mm(readout, state_in[0])
    squares = jnp.zeros((length, 1), F32)
    products = jnp.zeros((length, 1), F32)
    for at, width in column_blocks(inner):
        cols = slice(at, at + width)
        x_pre = pre[0, :, bc_width + at : bc_width + at + width]
        values = x_pre * sigmoid(x_pre)
        fed = (values * step_x[:, cols]).astype(BF16)
        masks = half_masks(width)
        near[:, :width] = carried[:, cols] + skip[:, cols] * values
        for start in range(0, length, LANES):
            stop = start + LANES
            found = near[start:stop, :width]
            for k, mask in enumerate(masks):
                head = at // HEAD + k
                spread_log = total[start:stop, head : head + 1] - total_t[head : head + 1, :stop]
                mixing = pair[start:stop, :stop] * jnp.exp(spread_log + seg[start:stop, :stop])
                found = found + mm(mixing.astype(BF16), jnp.where(mask, fed[:stop], 0))
            near[start:stop, :width] = found
        mixed = near[:, :width]
        mixer[0, :, cols] = mixed
        raw_gate = gate[0, :, cols]
        gated = mixed * (raw_gate * sigmoid(raw_gate))
        weighted = gated * norm_gate[:, cols]
        gated_low[:, cols] = weighted.astype(BF16)
        squares = squares + jnp.sum(gated * gated, 1, keepdims=True)
        products = products + jnp.sum(grad_gn[0, :, cols] * weighted, 1, keepdims=True)
    part[0] = mm_nt(gated_low[...], w_out_t[...]).astype(BF16)
    lane = lax.broadcasted_iota(jnp.int32, (length, LANES), 1)
    stats[0] = jnp.where(lane == 0, squares, jnp.where(lane == 1, products, 0.0))


def backward_local(inner_all, mixer, gate, grad_gn, stats, pre, dt_raw, cum, age, age_row, state_in, normed, out_grad,
                   norm_gate, skip, heads, spread, gather,
                   grad_fed, grad_mix, grad_gate, grad_cum, grad_bc, grad_state, grad_wz, grad_wo, sums,
                   sum_z, sum_o, near, seg, pair, grad_pair, carried, step_x, gated_low, from_state):
    length, inner = mixer.shape[1:]
    bc_width = 2 * LANES

    @pl.when(is_first_step())
    def _():
        sum_z[...] = jnp.zeros_like(sum_z)
        sum_o[...] = jnp.zeros_like(sum_o)
        sums[...] = jnp.zeros_like(sums)

    readout = pre[0, :, LANES:bc_width]
    readout = (readout * sigmoid(readout)).astype(BF16)
    inputs_b = pre[0, :, :LANES]
    inputs_b = (inputs_b * sigmoid(inputs_b)).astype(BF16)
    pair[...] = mm_nt(inputs_b, readout)
    grad_pair[...] = jnp.zeros_like(grad_pair)
    row = lax.broadcasted_iota(jnp.int32, (length, length), 0)
    col = lax.broadcasted_iota(jnp.int32, (length, length), 1)
    back = (col - row).astype(F32)
    seg[...] = jnp.where((back >= 0) & (back <= age_row[0][:1]), 0.0, GONE)
    total = cum[0]
    total_t = total.T
    step = softplus(dt_raw[0] + heads[0:1])
    step_x[...] = pick(step, spread[...])
    open_start = age[0] > row_index(length)
    carried[...] = pick(jnp.where(open_start, jnp.exp(total), 0.0), spread[...])
    scale = lax.rsqrt(stats[0][:, :1] / inner_all + EPSILON)
    pull = scale * scale * scale * (stats[0][:, 1:2] / inner_all)
    rows_sum = jnp.zeros((length, LANES), F32)
    for at, width in column_blocks(inner):
        cols = slice(at, at + width)
        x_pre = pre[0, :, bc_width + at : bc_width + at + width]
        values = x_pre * sigmoid(x_pre)
        fed = (values * step_x[:, cols]).astype(BF16)
        mixed = mixer[0, :, cols]
        raw_gate = gate[0, :, cols]
        logistic = sigmoid(raw_gate)
        acted = raw_gate * logistic
        gated = mixed * acted
        grad_out = grad_gn[0, :, cols]
        gated_scaled = gated * scale
        gated_low[:, cols] = (gated_scaled * norm_gate[:, cols]).astype(BF16)
        grad_gated = scale * (grad_out * norm_gate[:, cols]) - gated * pull
        grad_gate[0, :, cols] = (grad_gated * mixed * (logistic * (1.0 + raw_gate * (1.0 - logistic)))).astype(BF16)
        mix_low = (grad_gated * acted).astype(BF16)
        grad_mix[0, :, cols] = mix_low
        mix_wide = mix_low.astype(F32)
        sums[0:1, cols] += jnp.sum(grad_out * gated_scaled, 0, keepdims=True)
        sums[1:2, cols] += jnp.sum(mix_wide * values, 0, keepdims=True)
        rows_sum = rows_sum + pick(mix_wide * (mixed - skip[:, cols] * values), gather[cols])
        from_state[:, cols] = (carried[:, cols] * mix_wide).astype(BF16)
        masks = half_masks(width)
        for start in range(0, length, LANES):
            stop = start + LANES
            found = jnp.zeros((LANES, width), F32)
            for k, mask in enumerate(masks):
                head = at // HEAD + k
                spread_log = total_t[head : head + 1, start:] - total[start:stop, head : head + 1]
                decayed = jnp.exp(spread_log + seg[start:stop, start:])
                mixing = (pair[start:stop, start:] * decayed).astype(BF16)
                grad_mixing = mm_nt(jnp.where(mask, fed[start:stop], 0), mix_low[start:])
                grad_pair[start:stop, start:] += grad_mixing * decayed
                found = found + mm(mixing, jnp.where(mask, mix_low[start:], 0))
            near[start:stop, :width] = found
        grad_fed[0, :, cols] = near[:, :width]
        rows_sum = rows_sum - pick(near[:, :width] * fed.astype(F32), gather[cols])
    grad_cum[0] = rows_sum
    pair_low = grad_pair[...].astype(BF16)
    grad_bc[0, :, :LANES] = mm(pair_low, readout)
    grad_bc[0, :, LANES:] = mm_tn(pair_low, inputs_b) + mm_nt(from_state[...], state_in[0])
    grad_state[0] = mm_tn(readout, from_state[...]).astype(BF16)
    sum_z[...] += mm_tn(normed[0, HALO:], grad_gate[0])
    sum_o[...] += mm_tn(out_grad[0], gated_low[...])

    @pl.when(is_last_step())
    def _():
        grad_wz[...] = sum_z[...].astype(BF16)
        grad_wo[...] = sum_o[...].astype(BF16)


def backward_finish(grad_later, state_in, pre, raw, dt_raw, cum, age, grad_fed, grad_mix, grad_cum, grad_bc, grad_gate,
                    normed, hid, halo, w_in, w_z, taps, skip, norm_in, heads, spread, gather, tri_up,
                    grad_normed, grad_halo, grad_w, conv_sums, head_sums, norm_sums,
                    sum_w, step_x, open_x, from_state, fed_state, slope, age_long, grad_in, wide):
    length, inner = grad_fed.shape[1:]
    channels = taps.shape[1]
    bc_width = 2 * LANES
    lead = HALO + length

    @pl.when(is_first_step())
    def _():
        sum_w[...] = jnp.zeros_like(sum_w)
        conv_sums[...] = jnp.zeros_like(conv_sums)
        head_sums[...] = jnp.zeros_like(head_sums)
        norm_sums[...] = jnp.zeros_like(norm_sums)
        slope[:HALO] = jnp.zeros((HALO, channels), F32)
        slope[lead:] = jnp.zeros((8, channels), F32)
        age_long[:HALO] = jnp.zeros((HALO, LANES), F32)
        age_long[lead:] = jnp.zeros((8, LANES), F32)
        grad_in[:HALO, bc_width : bc_width + LANES] = jnp.zeros((HALO, LANES), BF16)

    age_long[HALO:lead] = age[0]
    total = cum[0]
    step_raw = dt_raw[0] + heads[0:1]
    step = softplus(step_raw)
    rate = -jnp.exp(heads[1:2])
    step_x[...] = pick(step, spread[...])
    last, age_last = total[length - 1 :], age[0, length - 1 :]
    open_end = row_index(length) - (length - 1) + age_last >= 0
    open_x[...] = pick(jnp.where(open_end, jnp.exp(last - total), 0.0), spread[...])
    b_pre = pre[0, :, :LANES]
    inputs_b = (b_pre * sigmoid(b_pre)).astype(BF16)
    from_state[...] = open_x[...] * mm(inputs_b, grad_later[0])
    state_sum = jnp.zeros((length, LANES), F32)
    step_sum = jnp.zeros((length, LANES), F32)
    for at, width in column_blocks(inner):
        cols = slice(at, at + width)
        x_pre = pre[0, :, bc_width + at : bc_width + at + width]
        logistic = sigmoid(x_pre)
        values = x_pre * logistic
        fed = values * step_x[:, cols]
        fed_state[:, cols] = (fed * open_x[:, cols]).astype(BF16)
        arrived = from_state[:, cols]
        grad = grad_fed[0, :, cols] + arrived
        state_sum = state_sum + pick(fed * arrived, gather[cols])
        step_sum = step_sum + pick(values * grad, gather[cols])
        grad_values = grad * step_x[:, cols] + skip[:, cols] * grad_mix[0, :, cols].astype(F32)
        slope[HALO:lead, bc_width + at : bc_width + at + width] = grad_values * (
            logistic * (1.0 + x_pre * (1.0 - logistic))
        )
    for at, extra in ((0, mm_nt(fed_state[...], grad_later[0])), (LANES, 0.0)):
        cols = slice(at, at + LANES)
        bc_pre = pre[0, :, cols]
        logistic = sigmoid(bc_pre)
        slope[HALO:lead, cols] = (grad_bc[0, :, cols] + extra) * (logistic * (1.0 + bc_pre * (1.0 - logistic)))
    kept = jnp.where(age_last > length - 1, jnp.exp(last), 0.0)
    met = jnp.sum(grad_later[0].astype(F32) * state_in[0].astype(F32), 0, keepdims=True)
    met = pick(jnp.broadcast_to(met, (8, inner)), gather[...], 3)[:1]
    end = met * kept + jnp.sum(state_sum, 0, keepdims=True)
    grad_a = pick_left(tri_up[...], grad_cum[0] - state_sum) + end
    head_sums[1:2] += jnp.sum(grad_a * rate * step, 0, keepdims=True)
    grad_step = (step_sum + grad_a * rate) * sigmoid(step_raw)
    head_sums[0:1] += jnp.sum(grad_step, 0, keepdims=True)
    grad_in[HALO:, bc_width : bc_width + LANES] = grad_step.astype(BF16)
    for at, width in column_blocks(channels):
        cols = slice(at, at + width)
        shifted = at if at < bc_width else at + LANES
        own = slope[HALO:lead, cols]
        total_in = taps[0:1, cols] * slope[:lead, cols]
        conv_sums[0:1, cols] += jnp.sum(own * raw[0, HALO:, cols], 0, keepdims=True)
        for lag in range(1, 4):
            kept_lag = jnp.where(age[0, :, :width] >= lag, own, 0.0)
            conv_sums[lag : lag + 1, cols] += jnp.sum(
                kept_lag * raw[0, HALO - lag : lead - lag, cols], 0, keepdims=True
            )
            later = jnp.where(age_long[lag : lead + lag, :width] >= lag, slope[lag : lead + lag, cols], 0.0)
            total_in = total_in + taps[lag : lag + 1, cols] * later
        conv_sums[4:5, cols] += jnp.sum(own, 0, keepdims=True)
        grad_in[:, shifted : shifted + width] = total_in.astype(BF16)
    wide[...] = mm_nt(grad_in[...], w_in[...])
    wide[HALO:] += mm_nt(grad_gate[0], w_z[...])
    hidden = halo[0].astype(F32)
    scale = normalised(hidden, 1.0)[1]
    norm_sums[0:1] += jnp.sum(wide[:HALO] * hidden * scale, 0, keepdims=True)
    for at in range(0, length, 64):
        hidden = hid[0, at : at + 64].astype(F32)
        scale = normalised(hidden, 1.0)[1]
        norm_sums[0:1] += jnp.sum(wide[HALO + at : HALO + at + 64] * hidden * scale, 0, keepdims=True)
    grad_halo[0] = wide[:HALO].astype(BF16)
    grad_normed[0] = wide[HALO:].astype(BF16)
    sum_w[...] += mm_tn(normed[0], grad_in[...])

    @pl.when(is_last_step())
    def _():
        grad_w[...] = sum_w[...].astype(BF16)


def finish(inner_all, hid, out_grad, stats, norm_in, own_part, other_part, own_grad, other_grad, own_tail, other_tail,
           out, in_grad, total):
    length = hid.shape[1]

    def added(own, others, rows):
        found = own[0, rows].astype(F32)
        for k in range(others.shape[0]):
            found = found + others[k, 0, rows].astype(F32)
        return found

    everything = slice(None)
    total[...] = added(own_grad, other_grad, everything)
    total[length - HALO :] += added(own_tail, other_tail, everything)
    for at in range(0, length, 64):
        rows = slice(at, at + 64)
        hidden = hid[0, rows].astype(F32)
        scale_gate = lax.rsqrt(stats[0, rows, :1] / inner_all + EPSILON)
        out[0, rows] = (hidden + scale_gate * added(own_part, other_part, rows)).astype(BF16)
        scale = normalised(hidden, 1.0)[1]
        weighted = total[rows] * norm_in[...]
        inner_mean = jnp.mean(weighted * hidden, -1, keepdims=True)
        in_grad[0, rows] = (
            out_grad[0, rows].astype(F32) + scale * weighted - hidden * (scale * scale * scale * inner_mean)
        ).astype(BF16)


def by_piece(array):
    rest = array.shape[1:]
    return pl.BlockSpec((1,) + rest, lambda i: (i,) + (0,) * len(rest))


def by_piece_second(array):
    rest = array.shape[2:]
    return pl.BlockSpec((array.shape[0], 1) + rest, lambda i: (0, i) + (0,) * len(rest))


def fixed(array):
    return pl.BlockSpec(array.shape, lambda i: (0,) * len(array.shape))


def call(kernel, pieces, inputs, outputs, scratch, name):
    return pl.pallas_call(
        kernel,
        grid=(pieces,),
        in_specs=[cut(array) for array, cut in inputs],
        out_specs=[cut(shape) for shape, cut in outputs],
        out_shape=[shape for shape, _ in outputs],
        scratch_shapes=[pltpu.VMEM(shape, kind) for shape, kind in scratch],
        compiler_params=pltpu.CompilerParams(vmem_limit_bytes=VMEM_BYTES),
        name=name,
    )(*[array for array, _ in inputs])


def shaped(kind, *dims):
    return jax.ShapeDtypeStruct(dims, kind)


def gather_rows(rows):
    return lax.all_gather(rows, ("shard", "context"), axis=0, tiled=True)


def scatter_rows(rows):
    return lax.psum_scatter(rows.astype(F32), ("shard", "context"), scatter_dimension=0, tiled=True)


def passed_along(value, by):
    length = lax.axis_size("context")
    return lax.ppermute(value, "context", [(i, i + by) for i in range(length) if 0 <= i + by < length])


def chain(local, decay, by):
    arrived = jnp.zeros_like(local)
    for _ in range(lax.axis_size("context") - 1):
        leaving = decay[:, :1] * arrived.astype(F32) + local.astype(F32)
        arrived = passed_along(leaving.astype(BF16), by)
    return arrived


def exchange(value):
    everything = lax.all_gather(value, "tensor")
    return everything[0], everything[1:]


def shards(inner_all, hidden_in, out_grad, doc_start, norm_in, w_z, w_x, w_bc, w_dt, conv_x, conv_bc, dt_bias, a_log,
           skip_d, norm_gate, w_out):
    micro, per_device, length, model = hidden_in.shape
    pieces = micro * per_device
    inner = w_z.shape[1]
    head_count = w_dt.shape[1]
    bc_width = w_bc.shape[1] * lax.axis_size("tensor")
    channels = bc_width + inner
    in_width = channels + LANES
    lead = HALO + length
    offset = lax.axis_index("context") * length

    head_of = np.arange(inner) // HEAD
    gather = jnp.asarray(head_of[:, None] == np.arange(LANES)[None], BF16)
    spread = jnp.asarray(head_of[None] == np.arange(LANES)[:, None], BF16)
    tri = jnp.asarray(np.tril(np.ones((length, length))), BF16)
    tri_up = jnp.asarray(np.triu(np.ones((length, length))), BF16)

    def head_row(row):
        return jnp.pad(row, (0, LANES - head_count))

    heads = jnp.stack([head_row(dt_bias), head_row(a_log)] + [jnp.zeros((LANES,), F32)] * 6)
    skip = jnp.repeat(skip_d, HEAD)[None]
    norm_in, norm_gate = norm_in[None], norm_gate[None]
    conv_bc_all = lax.all_gather(conv_bc, "tensor", axis=1, tiled=True)
    taps = jnp.pad(jnp.concatenate([conv_bc_all, conv_x], 1), ((0, 3), (0, 0)))
    w_bc_all = lax.all_gather(w_bc, "tensor", axis=1, tiled=True)
    w_dt_wide = jnp.pad(w_dt, ((0, 0), (0, LANES - head_count)))
    w_in = gather_rows(jnp.concatenate([w_bc_all, w_dt_wide, w_x], 1))
    w_z_all = gather_rows(w_z)
    w_out_t = gather_rows(w_out.T)

    hid = hidden_in.reshape(pieces, length, model)
    seed = out_grad.reshape(pieces, length, model)
    halo = passed_along(hid[:, length - HALO :], 1)
    ages = (offset + jnp.arange(length, dtype=jnp.int32) - doc_start.reshape(pieces, length)).astype(F32)
    age = jnp.broadcast_to(ages[:, :, None], (pieces, length, LANES))
    age_row = jnp.broadcast_to(ages[:, None, :], (pieces, 8, length))

    token = functools.partial(shaped, F32, pieces, length)
    token_low = functools.partial(shaped, BF16, pieces, length)
    state = shaped(BF16, pieces, LANES, inner)
    normed, raw, pre, dt_raw, cum, local, decay = call(
        forward_local, pieces,
        [(hid, by_piece), (halo, by_piece), (age, by_piece), (norm_in, fixed), (w_in, fixed), (taps, fixed),
         (heads, fixed), (spread, fixed), (tri, fixed)],
        [(shaped(BF16, pieces, lead, model), by_piece), (shaped(F32, pieces, lead, channels), by_piece),
         (token(channels), by_piece), (token(LANES), by_piece), (token(LANES), by_piece), (state, by_piece),
         (shaped(F32, pieces, 8, inner), by_piece)],
        [((length, channels), F32)], "forward_local",
    )

    state_in = chain(local, decay, 1)

    square = ((length, length), F32)
    token_wide = ((length, inner), F32)
    token_narrow = ((length, inner), BF16)
    mixer, gate, grad_gn, part, stats = call(
        forward_mix, pieces,
        [(pre, by_piece), (dt_raw, by_piece), (cum, by_piece), (age, by_piece), (state_in, by_piece), (normed, by_piece),
         (seed, by_piece), (w_z_all, fixed), (w_out_t, fixed), (norm_gate, fixed), (skip, fixed), (heads, fixed),
         (spread, fixed)],
        [(token(inner), by_piece), (token(inner), by_piece), (token(inner), by_piece), (token_low(model), by_piece),
         (token(LANES), by_piece)],
        [((length, LANES), F32), square, square, token_wide, token_wide, token_narrow], "forward_mix",
    )

    stats = lax.psum(stats, "tensor")

    grad_fed, grad_mix, grad_gate, grad_cum, grad_bc, grad_state, grad_wz, grad_wo, sums = call(
        functools.partial(backward_local, inner_all), pieces,
        [(mixer, by_piece), (gate, by_piece), (grad_gn, by_piece), (stats, by_piece), (pre, by_piece),
         (dt_raw, by_piece), (cum, by_piece), (age, by_piece), (age_row, by_piece), (state_in, by_piece),
         (normed, by_piece), (seed, by_piece), (norm_gate, fixed), (skip, fixed), (heads, fixed), (spread, fixed),
         (gather, fixed)],
        [(token(inner), by_piece), (token_low(inner), by_piece), (token_low(inner), by_piece), (token(LANES), by_piece),
         (token(bc_width), by_piece), (state, by_piece), (shaped(BF16, model, inner), fixed),
         (shaped(BF16, model, inner), fixed), (shaped(F32, 8, inner), fixed)],
        [((model, inner), F32), ((model, inner), F32), ((length, LANES), F32), square, square, square, token_wide,
         token_wide, token_narrow, token_narrow], "backward_local",
    )

    grad_later = chain(grad_state, decay, -1)

    grad_normed, grad_halo, grad_w, conv_sums, head_sums, norm_sums = call(
        backward_finish, pieces,
        [(grad_later, by_piece), (state_in, by_piece), (pre, by_piece), (raw, by_piece), (dt_raw, by_piece),
         (cum, by_piece), (age, by_piece), (grad_fed, by_piece), (grad_mix, by_piece), (grad_cum, by_piece),
         (grad_bc, by_piece), (grad_gate, by_piece), (normed, by_piece), (hid, by_piece), (halo, by_piece),
         (w_in, fixed), (w_z_all, fixed), (taps, fixed), (skip, fixed), (norm_in, fixed), (heads, fixed),
         (spread, fixed), (gather, fixed), (tri_up, fixed)],
        [(token_low(model), by_piece), (shaped(BF16, pieces, HALO, model), by_piece),
         (shaped(BF16, model, in_width), fixed), (shaped(F32, 8, channels), fixed), (shaped(F32, 8, LANES), fixed),
         (shaped(F32, 8, model), fixed)],
        [((model, in_width), F32), token_wide, token_wide, token_wide, token_narrow,
         ((lead + 8, channels), F32), ((lead + 8, LANES), F32), ((lead, in_width), BF16), ((lead, model), F32)],
        "backward_finish",
    )

    own_part, other_part = exchange(part)
    own_grad, other_grad = exchange(grad_normed)
    own_tail, other_tail = exchange(passed_along(grad_halo, -1))
    out, in_grad = call(
        functools.partial(finish, inner_all), pieces,
        [(hid, by_piece), (seed, by_piece), (stats, by_piece), (norm_in, fixed), (own_part, by_piece),
         (other_part, by_piece_second), (own_grad, by_piece), (other_grad, by_piece_second), (own_tail, by_piece),
         (other_tail, by_piece_second)],
        [(token_low(model), by_piece), (token_low(model), by_piece)],
        [((length, model), F32)], "finish",
    )

    mine = lax.axis_index("tensor")
    own_bc = w_bc.shape[1]
    grad_w = scatter_rows(grad_w)
    grad_w_bc = lax.psum_scatter(grad_w[:, :bc_width], "tensor", scatter_dimension=1, tiled=True)
    norm_sums, conv_bc_sums = lax.psum((norm_sums[0], conv_sums[:5, :bc_width]), ("shard", "context", "tensor"))
    conv_x_sums, head_sums, sums = lax.psum((conv_sums[:5, bc_width:], head_sums[:2], sums[:2]), ("shard", "context"))
    return (
        out.reshape(hidden_in.shape),
        in_grad.reshape(hidden_in.shape),
        norm_sums,
        scatter_rows(grad_wz),
        grad_w[:, bc_width + LANES :],
        grad_w_bc,
        grad_w[:, bc_width : bc_width + head_count],
        conv_x_sums,
        lax.dynamic_slice_in_dim(conv_bc_sums, mine * own_bc, own_bc, 1),
        head_sums[0, :head_count],
        head_sums[1, :head_count],
        jnp.sum(sums[1].reshape(head_count, HEAD), 1),
        sums[0],
        scatter_rows(grad_wo).T,
    )


def solution(mesh):
    whole = P(None, "shard", "context", None)
    rows = P(("shard", "context"), "tensor")
    lanes = P(None, "tensor")
    heads = P("tensor")
    w_out = P("tensor", ("shard", "context"))
    inputs = (whole, whole, P(None, "shard", "context"), P(), rows, rows, rows, rows, lanes, lanes, heads, heads, heads, heads, w_out)
    outputs = (whole, whole, P(), rows, rows, rows, rows, lanes, lanes, heads, heads, heads, heads, w_out)

    def placed(*arrays):
        inner_all = arrays[4].shape[1]
        return jax.shard_map(
            functools.partial(shards, inner_all), mesh=mesh, in_specs=inputs, out_specs=outputs, check_vma=False
        )(*arrays)

    return placed
```

```python
import functools

import jax
import jax.numpy as jnp
import numpy as np
from jax import lax
from jax.experimental import pallas as pl
from jax.experimental.pallas import tpu as pltpu
from jax.sharding import PartitionSpec as P

EPSILON = 1e-05
F32, BF16 = jnp.float32, jnp.bfloat16
HEAD = 64
LANES = 128
HALO = 16
GONE = -1e30
VMEM_BYTES = 60 * 1024 * 1024


def mm(left, right):
    return jnp.dot(left, right, preferred_element_type=F32)


def mm_nt(left, right):
    return lax.dot_general(left, right, (((1,), (1,)), ((), ())), preferred_element_type=F32)


def mm_tn(left, right):
    return lax.dot_general(left, right, (((0,), (0,)), ((), ())), preferred_element_type=F32)


def parts_of(value, count):
    parts = []
    for _ in range(count - 1):
        parts.append(value.astype(BF16))
        value = value - parts[-1].astype(F32)
    return parts + [value.astype(BF16)]


def pick(value, ones, count=2):
    return sum(mm(part, ones) for part in parts_of(value, count))


def pick_left(ones, value, count=3):
    return sum(mm(ones, part) for part in parts_of(value, count))


def softplus(value):
    return jnp.maximum(value, 0.0) + jnp.log1p(jnp.exp(-jnp.abs(value)))


def sigmoid(value):
    return 1.0 / (1.0 + jnp.exp(-value))


def column_blocks(width):
    return [(at, min(LANES, width - at)) for at in range(0, width, LANES)]


def row_index(length):
    return lax.broadcasted_iota(jnp.int32, (length, LANES), 0).astype(F32)


def is_first_step():
    return pl.program_id(0) == 0


def is_last_step():
    return pl.program_id(0) == pl.num_programs(0) - 1


def half_masks(width):
    lane = lax.broadcasted_iota(jnp.int32, (1, width), 1)
    return [(lane // HEAD) == k for k in range(width // HEAD)]


def normalised(hidden, gain):
    scale = lax.rsqrt(jnp.mean(hidden * hidden, -1, keepdims=True) + EPSILON)
    return hidden * scale * gain, scale


def forward_local(hid, halo, age, norm_in, w_in, taps, heads, spread, tri,
                  normed, raw, pre, dt_raw, cum, local, decay, act):
    length = hid.shape[1]
    channels = taps.shape[1]
    bc_width = 2 * LANES
    normed[0, :HALO] = normalised(halo[0].astype(F32), norm_in[...])[0].astype(BF16)
    for at in range(0, length, 64):
        rows = normalised(hid[0, at : at + 64].astype(F32), norm_in[...])[0]
        normed[0, HALO + at : HALO + at + 64] = rows.astype(BF16)
    raw[0, :, :bc_width] = mm(normed[0], w_in[:, :bc_width])
    raw[0, :, bc_width:] = mm(normed[0], w_in[:, bc_width + LANES :])
    dt_raw[0] = mm(normed[0, HALO:], w_in[:, bc_width : bc_width + LANES])
    for at, width in column_blocks(channels):
        cols = slice(at, at + width)
        running = jnp.broadcast_to(taps[4:5, cols], (length, width))
        for lag in range(4):
            tapped = raw[0, HALO - lag : HALO - lag + length, cols]
            if lag:
                tapped = jnp.where(age[0, :, :width] >= lag, tapped, 0.0)
            running = running + taps[lag : lag + 1, cols] * tapped
        pre[0, :, cols] = running
        act[:, cols] = running * sigmoid(running)
    step = softplus(dt_raw[0] + heads[0:1])
    total = pick_left(tri[...], -jnp.exp(heads[1:2]) * step)
    cum[0] = total
    last, age_last = total[length - 1 :], age[0, length - 1 :]
    open_end = row_index(length) - (length - 1) + age_last >= 0
    weight = jnp.where(open_end, jnp.exp(last - total), 0.0) * step
    weighted = (act[:, bc_width:] * pick(weight, spread[...])).astype(BF16)
    local[0] = mm_tn(act[:, :LANES].astype(BF16), weighted).astype(BF16)
    kept = jnp.where(age_last > length - 1, jnp.exp(last), 0.0)
    decay[0] = pick(jnp.broadcast_to(kept, (8, LANES)), spread[...], 3)


def forward_mix(pre, dt_raw, cum, age, state_in, normed, out_grad, w_z, w_out_t, norm_gate, skip, heads, spread,
                mixer, gate, grad_gn, part, stats, near, seg, pair, carried, step_x, gated_low):
    length, inner = mixer.shape[1:]
    bc_width = 2 * LANES
    readout = pre[0, :, LANES:bc_width]
    readout = (readout * sigmoid(readout)).astype(BF16)
    inputs_b = pre[0, :, :LANES]
    inputs_b = (inputs_b * sigmoid(inputs_b)).astype(BF16)
    gate[0] = mm(normed[0, HALO:], w_z[...])
    grad_gn[0] = mm(out_grad[0], w_out_t[...])
    pair[...] = mm_nt(readout, inputs_b)
    row = lax.broadcasted_iota(jnp.int32, (length, length), 0)
    col = lax.broadcasted_iota(jnp.int32, (length, length), 1)
    back = (row - col).astype(F32)
    seg[...] = jnp.where((back >= 0) & (back <= age[0][:, :1]), 0.0, GONE)
    total = cum[0]
    total_t = total.T
    step = softplus(dt_raw[0] + heads[0:1])
    step_x[...] = pick(step, spread[...])
    open_start = age[0] > row_index(length)
    carried[...] = pick(jnp.where(open_start, jnp.exp(total), 0.0), spread[...])
    carried[...] = carried[...] * mm(readout, state_in[0])
    squares = jnp.zeros((length, 1), F32)
    products = jnp.zeros((length, 1), F32)
    for at, width in column_blocks(inner):
        cols = slice(at, at + width)
        x_pre = pre[0, :, bc_width + at : bc_width + at + width]
        values = x_pre * sigmoid(x_pre)
        fed = (values * step_x[:, cols]).astype(BF16)
        masks = half_masks(width)
        near[:, :width] = carried[:, cols] + skip[:, cols] * values
        for start in range(0, length, LANES):
            stop = start + LANES
            found = near[start:stop, :width]
            for k, mask in enumerate(masks):
                head = at // HEAD + k
                spread_log = total[start:stop, head : head + 1] - total_t[head : head + 1, :stop]
                mixing = pair[start:stop, :stop] * jnp.exp(spread_log + seg[start:stop, :stop])
                found = found + mm(mixing.astype(BF16), jnp.where(mask, fed[:stop], 0))
            near[start:stop, :width] = found
        mixed = near[:, :width]
        mixer[0, :, cols] = mixed
        raw_gate = gate[0, :, cols]
        gated = mixed * (raw_gate * sigmoid(raw_gate))
        weighted = gated * norm_gate[:, cols]
        gated_low[:, cols] = weighted.astype(BF16)
        squares = squares + jnp.sum(gated * gated, 1, keepdims=True)
        products = products + jnp.sum(grad_gn[0, :, cols] * weighted, 1, keepdims=True)
    part[0] = mm_nt(gated_low[...], w_out_t[...]).astype(BF16)
    lane = lax.broadcasted_iota(jnp.int32, (length, LANES), 1)
    columns = jnp.where(lane == 0, squares, jnp.where(lane == 1, products, 0.0))
    stats[0] = columns.T[:8]


def backward_local(inner_all, mixer, gate, grad_gn, stats, pre, dt_raw, cum, age, age_row, state_in, normed, out_grad,
                   norm_gate, skip, heads, spread, gather,
                   grad_fed, grad_mix, grad_gate, grad_cum, grad_bc, grad_state, grad_wz, grad_wo, sums,
                   sum_z, sum_o, near, seg, pair, grad_pair, carried, step_x, gated_low, from_state):
    length, inner = mixer.shape[1:]
    bc_width = 2 * LANES

    @pl.when(is_first_step())
    def _():
        sum_z[...] = jnp.zeros_like(sum_z)
        sum_o[...] = jnp.zeros_like(sum_o)
        sums[...] = jnp.zeros_like(sums)

    readout = pre[0, :, LANES:bc_width]
    readout = (readout * sigmoid(readout)).astype(BF16)
    inputs_b = pre[0, :, :LANES]
    inputs_b = (inputs_b * sigmoid(inputs_b)).astype(BF16)
    pair[...] = mm_nt(inputs_b, readout)
    grad_pair[...] = jnp.zeros_like(grad_pair)
    row = lax.broadcasted_iota(jnp.int32, (length, length), 0)
    col = lax.broadcasted_iota(jnp.int32, (length, length), 1)
    back = (col - row).astype(F32)
    seg[...] = jnp.where((back >= 0) & (back <= age_row[0][:1]), 0.0, GONE)
    total = cum[0]
    total_t = total.T
    step = softplus(dt_raw[0] + heads[0:1])
    step_x[...] = pick(step, spread[...])
    open_start = age[0] > row_index(length)
    carried[...] = pick(jnp.where(open_start, jnp.exp(total), 0.0), spread[...])
    means = stats[0].T / inner_all
    scale = lax.rsqrt(means[:, :1] + EPSILON)
    pull = scale * scale * scale * means[:, 1:2]
    rows_sum = jnp.zeros((length, LANES), F32)
    for at, width in column_blocks(inner):
        cols = slice(at, at + width)
        x_pre = pre[0, :, bc_width + at : bc_width + at + width]
        values = x_pre * sigmoid(x_pre)
        fed = (values * step_x[:, cols]).astype(BF16)
        mixed = mixer[0, :, cols]
        raw_gate = gate[0, :, cols]
        logistic = sigmoid(raw_gate)
        acted = raw_gate * logistic
        gated = mixed * acted
        grad_out = grad_gn[0, :, cols]
        gated_scaled = gated * scale
        gated_low[:, cols] = (gated_scaled * norm_gate[:, cols]).astype(BF16)
        grad_gated = scale * (grad_out * norm_gate[:, cols]) - gated * pull
        grad_gate[0, :, cols] = (grad_gated * mixed * (logistic * (1.0 + raw_gate * (1.0 - logistic)))).astype(BF16)
        mix_low = (grad_gated * acted).astype(BF16)
        grad_mix[0, :, cols] = mix_low
        mix_wide = mix_low.astype(F32)
        sums[0:1, cols] += jnp.sum(grad_out * gated_scaled, 0, keepdims=True)
        sums[1:2, cols] += jnp.sum(mix_wide * values, 0, keepdims=True)
        rows_sum = rows_sum + pick(mix_wide * (mixed - skip[:, cols] * values), gather[cols])
        from_state[:, cols] = (carried[:, cols] * mix_wide).astype(BF16)
        masks = half_masks(width)
        for start in range(0, length, LANES):
            stop = start + LANES
            found = jnp.zeros((LANES, width), F32)
            for k, mask in enumerate(masks):
                head = at // HEAD + k
                spread_log = total_t[head : head + 1, start:] - total[start:stop, head : head + 1]
                decayed = jnp.exp(spread_log + seg[start:stop, start:])
                mixing = (pair[start:stop, start:] * decayed).astype(BF16)
                grad_mixing = mm_nt(jnp.where(mask, fed[start:stop], 0), mix_low[start:])
                grad_pair[start:stop, start:] += grad_mixing * decayed
                found = found + mm(mixing, jnp.where(mask, mix_low[start:], 0))
            near[start:stop, :width] = found
        grad_fed[0, :, cols] = near[:, :width]
        rows_sum = rows_sum - pick(near[:, :width] * fed.astype(F32), gather[cols])
    grad_cum[0] = rows_sum
    pair_low = grad_pair[...].astype(BF16)
    grad_bc[0, :, :LANES] = mm(pair_low, readout)
    grad_bc[0, :, LANES:] = mm_tn(pair_low, inputs_b) + mm_nt(from_state[...], state_in[0])
    grad_state[0] = mm_tn(readout, from_state[...]).astype(BF16)
    sum_z[...] += mm_tn(normed[0, HALO:], grad_gate[0])
    sum_o[...] += mm_tn(out_grad[0], gated_low[...])

    @pl.when(is_last_step())
    def _():
        grad_wz[...] = sum_z[...].astype(BF16)
        grad_wo[...] = sum_o[...].astype(BF16)


def backward_finish(grad_later, state_in, pre, raw, dt_raw, cum, age, grad_fed, grad_mix, grad_cum, grad_bc, grad_gate,
                    normed, hid, halo, w_in, w_z, taps, skip, norm_in, heads, spread, gather, tri_up,
                    grad_normed, grad_halo, grad_w, conv_sums, head_sums, norm_sums,
                    sum_w, step_x, open_x, from_state, fed_state, slope, age_long, grad_in, wide):
    length, inner = grad_fed.shape[1:]
    channels = taps.shape[1]
    bc_width = 2 * LANES
    lead = HALO + length

    @pl.when(is_first_step())
    def _():
        sum_w[...] = jnp.zeros_like(sum_w)
        conv_sums[...] = jnp.zeros_like(conv_sums)
        head_sums[...] = jnp.zeros_like(head_sums)
        norm_sums[...] = jnp.zeros_like(norm_sums)
        slope[:HALO] = jnp.zeros((HALO, channels), F32)
        slope[lead:] = jnp.zeros((8, channels), F32)
        age_long[:HALO] = jnp.zeros((HALO, LANES), F32)
        age_long[lead:] = jnp.zeros((8, LANES), F32)
        grad_in[:HALO, bc_width : bc_width + LANES] = jnp.zeros((HALO, LANES), BF16)

    age_long[HALO:lead] = age[0]
    total = cum[0]
    step_raw = dt_raw[0] + heads[0:1]
    step = softplus(step_raw)
    rate = -jnp.exp(heads[1:2])
    step_x[...] = pick(step, spread[...])
    last, age_last = total[length - 1 :], age[0, length - 1 :]
    open_end = row_index(length) - (length - 1) + age_last >= 0
    open_x[...] = pick(jnp.where(open_end, jnp.exp(last - total), 0.0), spread[...])
    b_pre = pre[0, :, :LANES]
    inputs_b = (b_pre * sigmoid(b_pre)).astype(BF16)
    from_state[...] = open_x[...] * mm(inputs_b, grad_later[0])
    state_sum = jnp.zeros((length, LANES), F32)
    step_sum = jnp.zeros((length, LANES), F32)
    for at, width in column_blocks(inner):
        cols = slice(at, at + width)
        x_pre = pre[0, :, bc_width + at : bc_width + at + width]
        logistic = sigmoid(x_pre)
        values = x_pre * logistic
        fed = values * step_x[:, cols]
        fed_state[:, cols] = (fed * open_x[:, cols]).astype(BF16)
        arrived = from_state[:, cols]
        grad = grad_fed[0, :, cols] + arrived
        state_sum = state_sum + pick(fed * arrived, gather[cols])
        step_sum = step_sum + pick(values * grad, gather[cols])
        grad_values = grad * step_x[:, cols] + skip[:, cols] * grad_mix[0, :, cols].astype(F32)
        slope[HALO:lead, bc_width + at : bc_width + at + width] = grad_values * (
            logistic * (1.0 + x_pre * (1.0 - logistic))
        )
    for at, extra in ((0, mm_nt(fed_state[...], grad_later[0])), (LANES, 0.0)):
        cols = slice(at, at + LANES)
        bc_pre = pre[0, :, cols]
        logistic = sigmoid(bc_pre)
        slope[HALO:lead, cols] = (grad_bc[0, :, cols] + extra) * (logistic * (1.0 + bc_pre * (1.0 - logistic)))
    kept = jnp.where(age_last > length - 1, jnp.exp(last), 0.0)
    met = jnp.sum(grad_later[0].astype(F32) * state_in[0].astype(F32), 0, keepdims=True)
    met = pick(jnp.broadcast_to(met, (8, inner)), gather[...], 3)[:1]
    end = met * kept + jnp.sum(state_sum, 0, keepdims=True)
    grad_a = pick_left(tri_up[...], grad_cum[0] - state_sum) + end
    head_sums[1:2] += jnp.sum(grad_a * rate * step, 0, keepdims=True)
    grad_step = (step_sum + grad_a * rate) * sigmoid(step_raw)
    head_sums[0:1] += jnp.sum(grad_step, 0, keepdims=True)
    grad_in[HALO:, bc_width : bc_width + LANES] = grad_step.astype(BF16)
    for at, width in column_blocks(channels):
        cols = slice(at, at + width)
        shifted = at if at < bc_width else at + LANES
        own = slope[HALO:lead, cols]
        total_in = taps[0:1, cols] * slope[:lead, cols]
        conv_sums[0:1, cols] += jnp.sum(own * raw[0, HALO:, cols], 0, keepdims=True)
        for lag in range(1, 4):
            kept_lag = jnp.where(age[0, :, :width] >= lag, own, 0.0)
            conv_sums[lag : lag + 1, cols] += jnp.sum(
                kept_lag * raw[0, HALO - lag : lead - lag, cols], 0, keepdims=True
            )
            later = jnp.where(age_long[lag : lead + lag, :width] >= lag, slope[lag : lead + lag, cols], 0.0)
            total_in = total_in + taps[lag : lag + 1, cols] * later
        conv_sums[4:5, cols] += jnp.sum(own, 0, keepdims=True)
        grad_in[:, shifted : shifted + width] = total_in.astype(BF16)
    wide[...] = mm_nt(grad_in[...], w_in[...])
    wide[HALO:] += mm_nt(grad_gate[0], w_z[...])
    hidden = halo[0].astype(F32)
    scale = normalised(hidden, 1.0)[1]
    norm_sums[0:1] += jnp.sum(wide[:HALO] * hidden * scale, 0, keepdims=True)
    for at in range(0, length, 64):
        hidden = hid[0, at : at + 64].astype(F32)
        scale = normalised(hidden, 1.0)[1]
        norm_sums[0:1] += jnp.sum(wide[HALO + at : HALO + at + 64] * hidden * scale, 0, keepdims=True)
    grad_halo[0] = wide[:HALO].astype(BF16)
    grad_normed[0] = wide[HALO:].astype(BF16)
    sum_w[...] += mm_tn(normed[0], grad_in[...])

    @pl.when(is_last_step())
    def _():
        grad_w[...] = sum_w[...].astype(BF16)


def finish(inner_all, hid, out_grad, stats, norm_in, own_part, other_part, own_grad, other_grad, own_tail, other_tail,
           sums_zo, sums_w, conv_sums, norm_sums, head_sums, inner_sums, gather,
           out, in_grad, grad_wz, grad_wx, grad_wbc, grad_wdt, grad_wo, grad_conv_x, grad_conv_bc, grad_dt_bias,
           grad_a_log, grad_skip, grad_norm_gate, grad_norm_in, total):
    length = hid.shape[1]

    def added(own, others, rows):
        found = own[0, rows].astype(F32)
        for k in range(others.shape[0]):
            found = found + others[k, 0, rows].astype(F32)
        return found

    everything = slice(None)
    total[...] = added(own_grad, other_grad, everything)
    total[length - HALO :] += added(own_tail, other_tail, everything)
    scales = lax.rsqrt(stats[0].T[:, :1] / inner_all + EPSILON)
    for at in range(0, length, 64):
        rows = slice(at, at + 64)
        hidden = hid[0, rows].astype(F32)
        out[0, rows] = (hidden + scales[rows] * added(own_part, other_part, rows)).astype(BF16)
        scale = normalised(hidden, 1.0)[1]
        weighted = total[rows] * norm_in[...]
        inner_mean = jnp.mean(weighted * hidden, -1, keepdims=True)
        in_grad[0, rows] = (
            out_grad[0, rows].astype(F32) + scale * weighted - hidden * (scale * scale * scale * inner_mean)
        ).astype(BF16)

    @pl.when(is_last_step())
    def _():
        inner, own_bc, head_count = grad_wz.shape[1], grad_wbc.shape[1], grad_wdt.shape[1]
        grad_wz[...] = sums_zo[:, :inner]
        grad_wo[...] = sums_zo[:, inner:].T
        grad_wbc[...] = sums_w[:, :own_bc]
        grad_wdt[...] = sums_w[:, own_bc : own_bc + head_count]
        grad_wx[...] = sums_w[:, own_bc + LANES :]
        grad_conv_bc[...] = conv_sums[:5, :own_bc]
        grad_conv_x[...] = conv_sums[:5, own_bc:]
        grad_dt_bias[...] = head_sums[0:1, :head_count]
        grad_a_log[...] = head_sums[1:2, :head_count]
        grad_norm_in[...] = norm_sums[0:1]
        grad_norm_gate[...] = inner_sums[0:1]
        grad_skip[...] = pick(inner_sums[...], gather[...], 3)[1:2, :head_count]


def by_piece(array):
    rest = array.shape[1:]
    return pl.BlockSpec((1,) + rest, lambda i: (i,) + (0,) * len(rest))


def by_piece_second(array):
    rest = array.shape[2:]
    return pl.BlockSpec((array.shape[0], 1) + rest, lambda i: (0, i) + (0,) * len(rest))


def fixed(array):
    return pl.BlockSpec(array.shape, lambda i: (0,) * len(array.shape))


def call(kernel, pieces, inputs, outputs, scratch, name):
    return pl.pallas_call(
        kernel,
        grid=(pieces,),
        in_specs=[cut(array) for array, cut in inputs],
        out_specs=[cut(shape) for shape, cut in outputs],
        out_shape=[shape for shape, _ in outputs],
        scratch_shapes=[pltpu.VMEM(shape, kind) for shape, kind in scratch],
        compiler_params=pltpu.CompilerParams(vmem_limit_bytes=VMEM_BYTES),
        name=name,
    )(*[array for array, _ in inputs])


def shaped(kind, *dims):
    return jax.ShapeDtypeStruct(dims, kind)


MESH = pl.DeviceIdType.MESH
UP, DOWN, NEXT_X, NEXT_Y = range(4)


def coordinates():
    return lax.axis_index("shard"), lax.axis_index("context"), lax.axis_index("tensor")


def greet(partners):
    barrier = pltpu.get_barrier_semaphore()
    count = 0
    for there, device in partners:
        if there is True:
            pl.semaphore_signal(barrier, inc=1, device_id=device, device_id_type=MESH)
            count = count + 1
        else:
            pl.when(there)(
                functools.partial(pl.semaphore_signal, barrier, inc=1, device_id=device, device_id_type=MESH)
            )
            count = count + there.astype(jnp.int32)
    pl.semaphore_wait(barrier, count)


class Copies:
    def __init__(self, send):
        self.send, self.used, self.started = send, 0, []

    def make(self, source, target, received, device, send=0):
        return pltpu.make_async_remote_copy(
            src_ref=source, dst_ref=target, send_sem=self.send.at[send], recv_sem=received,
            device_id=device, device_id_type=MESH,
        )

    def start(self, source, target, received, device, there=True):
        copy = self.make(source, target, received, device, self.used)
        self.used += 1
        self.started.append((there, copy))
        if there is True:
            copy.start()
        else:
            pl.when(there)(copy.start)

    def arrived(self, target, received, there=True):
        copy = self.make(target, target, received, {"tensor": 1 - lax.axis_index("tensor")})
        if there is True:
            copy.wait_recv()
        else:
            pl.when(there)(copy.wait_recv)

    def finish(self):
        for there, copy in self.started:
            if there is True:
                copy.wait_send()
            else:
                pl.when(there)(copy.wait_send)


def neighbours(place):
    shard, context, _ = place
    count = lax.axis_size("context")
    return [
        (context + 1 < count, {"context": context + 1}),
        (context > 0, {"context": context - 1}),
        (True, {"shard": shard ^ 1}),
        (True, {"shard": shard ^ 2}),
    ]


def gather_blocks(copies, place, stage, out, received, own):
    shard, context, _ = place
    count = lax.axis_size("context")
    up, down, next_x, next_y = neighbours(place)
    mine, beside_x, beside_y, across = [(shard ^ k) * count for k in (0, 1, 2, 3)]

    def pass_on(source, slot, to, there=True):
        if to[0] is not True:
            there = to[0] if there is True else there & to[0]
        copies.start(source, out.at[slot], received.at[slot], to[1], there)

    local = pltpu.make_async_copy(stage, out.at[mine + context], own)
    local.start()
    for to in (up, down, next_x, next_y):
        pass_on(stage, mine + context, to)
    yield
    for distance in range(1, count):
        for at, there, to in ((context - distance, context >= distance, up),
                              (context + distance, context + distance < count, down)):
            slot = mine + jnp.clip(at, 0, count - 1)
            copies.arrived(out.at[slot], received.at[slot], there)
            for target in (to, next_x, next_y):
                pass_on(out.at[slot], slot, target, there)
        yield
    for distance in range(count):
        for at, there in ((context - distance, context >= distance),
                          (context + distance, context + distance < count))[: 2 if distance else 1]:
            at = jnp.clip(at, 0, count - 1)
            low = at < count // 2
            copies.arrived(out.at[beside_x + at], received.at[beside_x + at], there)
            pass_on(out.at[beside_x + at], beside_x + at, next_y, there & low)
            copies.arrived(out.at[beside_y + at], received.at[beside_y + at], there)
            pass_on(out.at[beside_y + at], beside_y + at, next_x, there & (at >= count // 2))
        yield
    for at in range(count):
        copies.arrived(out.at[across + at], received.at[across + at])
    local.wait()


GATHER_COPIES = 64


def scatter_scratch(rows, width):
    block = pltpu.VMEM((4, rows, width), BF16)
    return [block, block, block, block, block, block, block, block, pltpu.VMEM((4, rows, width), F32),
            pltpu.SemaphoreType.DMA((5, 4))]


SCATTER_COPIES = 20


def scatter_blocks(copies, place, blocks, out, first, from_x, from_y, from_up, from_down, to_first, to_up, to_down,
                   column, received):
    shard, context, _ = place
    count = lax.axis_size("context")
    up, down, next_x, next_y = neighbours(place)
    mine, beside_x, beside_y, across = [(shard ^ k) * count for k in (0, 1, 2, 3)]
    low, high = range(count // 2), range(count // 2, count)
    for at in range(count // 2):
        for k, to in ((at, next_y), (at + count // 2, next_x)):
            copies.start(blocks.at[across + k], first.at[k], received.at[0, k], to[1])
    for k in reversed(high):
        copies.start(blocks.at[beside_x + k], from_x.at[k], received.at[1, k], next_x[1])
    for k in low:
        copies.start(blocks.at[beside_y + k], from_y.at[k], received.at[2, k], next_y[1])
    yield
    for at in range(count // 2):
        for k, beside, buffers, row, to in ((at, beside_x, from_x, 1, next_x), (count - 1 - at, beside_y, from_y, 2, next_y)):
            copies.arrived(first.at[k], received.at[0, k])
            to_first[k] = (blocks[beside + k].astype(F32) + first[k].astype(F32)).astype(BF16)
            copies.start(to_first.at[k], buffers.at[k], received.at[row, k], to[1])
        yield
    for at in range(count):
        k = count - 1 - at // 2 if at % 2 == 0 else at // 2
        copies.arrived(from_x.at[k], received.at[1, k])
        copies.arrived(from_y.at[k], received.at[2, k])
        column[k] = blocks[mine + k].astype(F32) + from_x[k].astype(F32) + from_y[k].astype(F32)
        yield
    for at in range(count - 1):
        k = count - 1 - at

        @pl.when(context < k)
        def _(k=k):
            @pl.when(context > 0)
            def _():
                copies.arrived(from_down.at[k], received.at[3, k])
                to_up[k] = (column[k] + from_down[k].astype(F32)).astype(BF16)

            @pl.when(context == 0)
            def _():
                to_up[k] = column[k].astype(BF16)

        copies.start(to_up.at[k], from_down.at[k], received.at[3, k], up[1], context < k)
        k = at

        @pl.when(context > k)
        def _(k=k):
            @pl.when(context < count - 1)
            def _():
                copies.arrived(from_up.at[k], received.at[4, k])
                to_down[k] = (column[k] + from_up[k].astype(F32)).astype(BF16)

            @pl.when(context == count - 1)
            def _():
                to_down[k] = column[k].astype(BF16)

        copies.start(to_down.at[k], from_up.at[k], received.at[4, k], down[1], context > k)
        yield
    out[...] = column[context]

    @pl.when(context > 0)
    def _():
        copies.arrived(from_down.at[context], received.at[3, context])
        out[...] += from_down[context].astype(F32)

    @pl.when(context < count - 1)
    def _():
        copies.arrived(from_up.at[context], received.at[4, context])
        out[...] += from_up[context].astype(F32)


def gather_inputs(w_bc, w_dt, w_x, conv_bc, conv_x, hid, out, halo, taps, stage, send, received, others, own):
    place = shard, context, tensor = coordinates()
    length = hid.shape[1]
    own_bc, head_count = w_bc.shape[1], w_dt.shape[1]
    bc_width = 2 * LANES
    partner = {"tensor": 1 - tensor}
    around = neighbours(place)
    stage[:, bc_width : bc_width + LANES] = jnp.zeros((stage.shape[0], LANES), BF16)
    stage[:, bc_width : bc_width + head_count] = w_dt[...]
    stage[:, bc_width + LANES :] = w_x[...]
    cols = pl.ds(pl.multiple_of(tensor * own_bc, LANES), own_bc)
    other_cols = pl.ds(pl.multiple_of((1 - tensor) * own_bc, LANES), own_bc)
    stage[:, cols] = w_bc[...]
    taps[...] = jnp.zeros_like(taps)
    taps[:5, cols] = conv_bc[...]
    taps[:5, bc_width:] = conv_x[...]
    greet(around + [(True, partner)])
    copies = Copies(send)
    copies.start(stage.at[:, cols], stage.at[:, cols], others.at[0], partner)
    copies.start(taps.at[:, cols], taps.at[:, cols], others.at[1], partner)
    tail = pl.ds(length - HALO, HALO)
    copies.start(hid.at[:, tail], halo, others.at[2], around[UP][1], around[UP][0])
    copies.arrived(stage.at[:, other_cols], others.at[0])
    for _ in gather_blocks(copies, place, stage, out, received, own):
        pass
    copies.arrived(taps.at[:, other_cols], others.at[1])
    copies.arrived(halo, others.at[2], context > 0)

    @pl.when(context == 0)
    def _():
        clear = pltpu.make_async_copy(hid.at[:, tail], halo, others.at[2])
        clear.start()
        clear.wait()

    copies.finish()


def chain_states(copies, place, local, decay, arrived, leaving, received, by):
    _, context, _ = place
    count = lax.axis_size("context")
    first = context == (0 if by > 0 else count - 1)
    last = context == (count - 1 if by > 0 else 0)
    to = {"context": context + by}
    pieces = local.shape[0]

    def sent(i):
        return pltpu.make_async_remote_copy(
            src_ref=leaving.at[i], dst_ref=arrived.at[i], send_sem=received.at[1, i], recv_sem=received.at[0, i],
            device_id=to, device_id_type=MESH,
        )

    for i in range(pieces):

        @pl.when(first)
        def _(i=i):
            arrived[i] = jnp.zeros_like(arrived[i])
            leaving[i] = local[i]

        @pl.when(jnp.logical_not(first))
        def _(i=i):
            copies.arrived(arrived.at[i], received.at[0, i])

        @pl.when(jnp.logical_not(first | last))
        def _(i=i):
            leaving[i] = (decay[i, :1] * arrived[i].astype(F32) + local[i].astype(F32)).astype(BF16)

        pl.when(jnp.logical_not(last))(sent(i).start)
        yield
    for i in range(pieces):
        pl.when(jnp.logical_not(last))(sent(i).wait_send)


def in_turn(*steps):
    steps = list(steps)
    while steps:
        for one in list(steps):
            try:
                next(one)
            except StopIteration:
                steps.remove(one)


def states_up(local, decay, w_z, w_out, arrived, out, stage, leaving, send, received, own, states):
    place = coordinates()
    inner = w_z.shape[1]
    stage[:, :inner] = w_z[...]
    stage[:, inner:] = w_out[...].astype(F32).T.astype(BF16)
    greet(neighbours(place))
    copies = Copies(send)
    in_turn(
        gather_blocks(copies, place, stage, out, received, own),
        chain_states(copies, place, local, decay, arrived, leaving, states, 1),
    )
    copies.finish()


def add_over_cores(own, out, other, send, received):
    _, _, tensor = coordinates()
    partner = {"tensor": 1 - tensor}
    greet([(True, partner)])
    copies = Copies(send)
    copies.start(own, other, received.at[0], partner)
    copies.arrived(other, received.at[0])
    out[...] = own[...] + other[...]
    copies.finish()


def states_down(local, decay, grad_wz, grad_wo, part, arrived, out, other_part, stage, leaving, send, others, states,
                *buffers):
    place = _, _, tensor = coordinates()
    inner = grad_wz.shape[2]
    stage[:, :, :inner] = grad_wz[...]
    stage[:, :, inner:] = grad_wo[...]
    partner = {"tensor": 1 - tensor}
    greet(neighbours(place) + [(True, partner)])
    copies = Copies(send)
    copies.start(part, other_part.at[0], others.at[0], partner)
    in_turn(
        scatter_blocks(copies, place, stage, out, *buffers),
        chain_states(copies, place, local, decay, arrived, leaving, states, -1),
    )
    copies.arrived(other_part.at[0], others.at[0])
    copies.finish()


def last_sums(grad_w, grad_normed, grad_halo, conv_sums, norm_sums, head_sums, inner_sums,
              out, other_grad, own_tail, other_tail, conv_out, norm_out, head_out, inner_out,
              stage, half, small, seen, tails, send, others, *buffers):
    place = shard, context, tensor = coordinates()
    count = lax.axis_size("context")
    bc_width = 2 * LANES
    own_bc = bc_width // 2
    inner, model = inner_sums.shape[1], norm_sums.shape[1]
    partner = {"tensor": 1 - tensor}
    around = neighbours(place)
    cols = pl.ds(pl.multiple_of(tensor * own_bc, LANES), own_bc)
    other_cols = pl.ds(pl.multiple_of((1 - tensor) * own_bc, LANES), own_bc)
    small[0, :5] = conv_sums[:5]
    small[0, 5:6, :model] = norm_sums[:1]
    small[0, 5:6, model : model + LANES] = head_sums[:1]
    small[0, 5:6, model + LANES :] = head_sums[1:2]
    small[0, 6:8, :inner] = inner_sums[:2]
    small[0, 6:8, inner:] = jnp.zeros((2, small.shape[2] - inner), F32)
    below, above = (around[DOWN][0], around[UP][0])
    greet(around + [(True, partner), (True, {"context": context ^ 2}),
                    (above, {"context": context + 1, "tensor": 1 - tensor}),
                    (below, {"context": context - 1, "tensor": 1 - tensor})])
    copies = Copies(send)
    copies.start(small.at[0], seen.at[0], others.at[4], partner)
    copies.start(grad_w.at[:, :, other_cols], half, others.at[0], partner)
    copies.start(grad_normed, other_grad.at[0], others.at[1], partner)
    copies.start(grad_halo, own_tail, others.at[2], around[DOWN][1], below)
    copies.start(grad_halo, other_tail.at[0], others.at[3], {"context": context - 1, "tensor": 1 - tensor}, below)
    stage[:, :, own_bc:] = grad_w[:, :, bc_width:]
    copies.arrived(half, others.at[0])
    mixed = grad_w[:, :, cols].astype(F32) + half[...].astype(F32)
    stage[:, :, :own_bc] = mixed.astype(BF16)
    row = lax.broadcasted_iota(jnp.int32, small.shape[1:], 0)
    lane = lax.broadcasted_iota(jnp.int32, small.shape[1:], 1)
    shared = ((row < 5) & (lane < bc_width)) | ((row == 5) & (lane < model))
    copies.arrived(seen.at[0], others.at[4])
    small[1] = small[0] + jnp.where(shared, seen[0], 0.0)
    copies.start(small.at[1], seen.at[1], others.at[5], {"shard": shard ^ 1})
    for _ in scatter_blocks(copies, place, stage, out, *buffers):
        pass
    for step, device in ((1, {"shard": shard ^ 1}), (2, {"shard": shard ^ 2}), (3, {"context": context ^ 1}),
                         (4, {"context": context ^ 2})):
        if step > 1:
            copies.start(small.at[step], seen.at[step], others.at[4 + step], device)
        copies.arrived(seen.at[step], others.at[4 + step])
        small[step + 1] = small[step] + seen[step]
    total = small.at[5]
    conv_out[:, :own_bc] = total[:, cols]
    conv_out[:, own_bc:] = total[:, bc_width:]
    norm_out[...] = jnp.broadcast_to(total[5:6, :model], norm_out.shape)
    head_out[...] = jnp.zeros_like(head_out)
    head_out[0:1] = total[5:6, model : model + LANES]
    head_out[1:2] = total[5:6, model + LANES : model + 2 * LANES]
    inner_out[...] = jnp.zeros_like(inner_out)
    inner_out[0:2] = total[6:8, :inner]
    copies.arrived(other_grad.at[0], others.at[1])
    copies.arrived(own_tail, others.at[2], above)
    copies.arrived(other_tail.at[0], others.at[3], above)

    @pl.when(jnp.logical_not(above))
    def _():
        tails[...] = jnp.zeros_like(tails)
        for target, k in ((own_tail, 2), (other_tail.at[0], 3)):
            clear = pltpu.make_async_copy(tails, target, others.at[k])
            clear.start()
            clear.wait()

    copies.finish()


ANY = pl.BlockSpec(memory_space=pl.ANY)
IN_VMEM = pl.BlockSpec(memory_space=pltpu.VMEM)
DMA = pltpu.SemaphoreType.DMA


def call_between(kernel, collective_id, inputs, outputs, scratch):
    return pl.pallas_call(
        kernel,
        in_specs=[spec for _, spec in inputs],
        out_specs=[spec for _, spec in outputs],
        out_shape=[shape for shape, _ in outputs],
        scratch_shapes=scratch,
        compiler_params=pltpu.CompilerParams(
            collective_id=collective_id, has_side_effects=True, vmem_limit_bytes=VMEM_BYTES
        ),
        name=kernel.__name__,
    )(*[array for array, _ in inputs])


def gather_rows(rows):
    return lax.all_gather(rows, ("shard", "context"), axis=0, tiled=True)


def scatter_rows(rows):
    return lax.psum_scatter(rows.astype(F32), ("shard", "context"), scatter_dimension=0, tiled=True)


def passed_along(value, by):
    length = lax.axis_size("context")
    return lax.ppermute(value, "context", [(i, i + by) for i in range(length) if 0 <= i + by < length])


def chain(local, decay, by):
    arrived = jnp.zeros_like(local)
    for _ in range(lax.axis_size("context") - 1):
        leaving = decay[:, :1] * arrived.astype(F32) + local.astype(F32)
        arrived = passed_along(leaving.astype(BF16), by)
    return arrived


def exchange(value):
    everything = lax.all_gather(value, "tensor")
    return everything[0], everything[1:]


def part_of(width, at):
    return lambda array: pl.BlockSpec((array.shape[0], width), lambda i: (0, at))


class AnyMesh:
    def inputs(self, hid, w_bc, w_dt, w_x, conv_bc, conv_x):
        conv_bc_all = lax.all_gather(conv_bc, "tensor", axis=1, tiled=True)
        taps = jnp.pad(jnp.concatenate([conv_bc_all, conv_x], 1), ((0, 3), (0, 0)))
        w_bc_all = lax.all_gather(w_bc, "tensor", axis=1, tiled=True)
        w_dt_wide = jnp.pad(w_dt, ((0, 0), (0, LANES - w_dt.shape[1])))
        w_in = gather_rows(jnp.concatenate([w_bc_all, w_dt_wide, w_x], 1))
        return w_in, passed_along(hid[:, hid.shape[1] - HALO :], 1), taps

    def states_up(self, local, decay, w_z, w_out):
        return chain(local, decay, 1), (gather_rows(w_z), fixed), (gather_rows(w_out.T), fixed)

    def over_cores(self, stats):
        return lax.psum(stats, "tensor")

    def states_down(self, local, decay, grad_wz, grad_wo, part):
        sums = jnp.concatenate([scatter_rows(grad_wz), scatter_rows(grad_wo)], 1)
        return chain(local, decay, -1), sums, exchange(part)

    def last_sums(self, grad_w, grad_normed, grad_halo, conv_sums, norm_sums, head_sums, inner_sums, own_bc):
        mine, bc_width = lax.axis_index("tensor"), 2 * LANES
        grad_w = scatter_rows(grad_w)
        grad_w_bc = lax.psum_scatter(grad_w[:, :bc_width], "tensor", scatter_dimension=1, tiled=True)
        norm_sums, conv_bc = lax.psum((norm_sums, conv_sums[:, :bc_width]), ("shard", "context", "tensor"))
        conv_x, head_sums, inner_sums = lax.psum(
            (conv_sums[:, bc_width:], head_sums, inner_sums), ("shard", "context")
        )
        conv_bc = lax.dynamic_slice_in_dim(conv_bc, mine * own_bc, own_bc, 1)
        return (
            jnp.concatenate([grad_w_bc, grad_w[:, bc_width:]], 1),
            exchange(grad_normed),
            exchange(passed_along(grad_halo, -1)),
            (jnp.concatenate([conv_bc, conv_x], 1), norm_sums, head_sums, inner_sums),
        )


class FourByFourByTwo:
    def inputs(self, hid, w_bc, w_dt, w_x, conv_bc, conv_x):
        rows, inner = w_x.shape
        pieces, _, model = hid.shape
        blocks = model // rows
        in_width = 3 * LANES + inner
        w_in, halo, taps = call_between(
            gather_inputs, 1,
            [(w_bc, IN_VMEM), (w_dt, IN_VMEM), (w_x, IN_VMEM), (conv_bc, IN_VMEM), (conv_x, IN_VMEM), (hid, ANY)],
            [(shaped(BF16, blocks, rows, in_width), ANY), (shaped(BF16, pieces, HALO, model), ANY),
             (shaped(F32, 8, 2 * LANES + inner), IN_VMEM)],
            [pltpu.VMEM((rows, in_width), BF16), DMA((GATHER_COPIES,)), DMA((blocks,)), DMA((3,)), DMA],
        )
        return w_in.reshape(model, in_width), halo, taps

    def states_up(self, local, decay, w_z, w_out):
        rows, inner = w_z.shape
        model = w_out.shape[1] * 16
        pieces = local.shape[0]
        arrived, both = call_between(
            states_up, 2,
            [(local, IN_VMEM), (decay, IN_VMEM), (w_z, IN_VMEM), (w_out, IN_VMEM)],
            [(shaped(BF16, *local.shape), IN_VMEM), (shaped(BF16, 16, rows, 2 * inner), ANY)],
            [pltpu.VMEM((rows, 2 * inner), BF16), pltpu.VMEM(local.shape, BF16), DMA((GATHER_COPIES,)), DMA((16,)), DMA,
             DMA((2, pieces))],
        )
        both = both.reshape(model, 2 * inner)
        return arrived, (both, part_of(inner, 0)), (both, part_of(inner, 1))

    def over_cores(self, stats):
        return call_between(
            add_over_cores, 3, [(stats, IN_VMEM)], [(shaped(F32, *stats.shape), IN_VMEM)],
            [pltpu.VMEM(stats.shape, F32), DMA((1,)), DMA((1,))],
        )[0]

    def states_down(self, local, decay, grad_wz, grad_wo, part):
        model, inner = grad_wz.shape
        rows = model // 16
        pieces = local.shape[0]
        arrived, sums, other = call_between(
            states_down, 4,
            [(local, IN_VMEM), (decay, IN_VMEM), (grad_wz.reshape(16, rows, inner), IN_VMEM),
             (grad_wo.reshape(16, rows, inner), IN_VMEM), (part, ANY)],
            [(shaped(BF16, *local.shape), IN_VMEM), (shaped(F32, rows, 2 * inner), IN_VMEM),
             (shaped(BF16, 1, *part.shape), ANY)],
            [pltpu.VMEM((16, rows, 2 * inner), BF16), pltpu.VMEM(local.shape, BF16), DMA((SCATTER_COPIES,)), DMA((1,)),
             DMA((2, pieces))] + scatter_scratch(rows, 2 * inner),
        )
        return arrived, sums, (part, other)

    def last_sums(self, grad_w, grad_normed, grad_halo, conv_sums, norm_sums, head_sums, inner_sums, own_bc):
        model, in_width = grad_w.shape
        rows = model // 16
        width = in_width - own_bc
        channels = conv_sums.shape[1]
        out, other_grad, own_tail, other_tail, *small = call_between(
            last_sums, 5,
            [(grad_w.reshape(16, rows, in_width), IN_VMEM), (grad_normed, ANY), (grad_halo, ANY),
             (conv_sums, IN_VMEM), (norm_sums, IN_VMEM), (head_sums, IN_VMEM), (inner_sums, IN_VMEM)],
            [(shaped(F32, rows, width), IN_VMEM), (shaped(BF16, 1, *grad_normed.shape), ANY),
             (shaped(BF16, *grad_halo.shape), ANY), (shaped(BF16, 1, *grad_halo.shape), ANY),
             (shaped(F32, 8, channels - own_bc), IN_VMEM), (shaped(F32, 8, model), IN_VMEM),
             (shaped(F32, 8, LANES), IN_VMEM), (shaped(F32, *inner_sums.shape), IN_VMEM)],
            [pltpu.VMEM((16, rows, width), BF16), pltpu.VMEM((16, rows, own_bc), BF16),
             pltpu.VMEM((6, 8, channels), F32), pltpu.VMEM((5, 8, channels), F32), pltpu.VMEM(grad_halo.shape, BF16),
             DMA((SCATTER_COPIES + 9,)), DMA((9,))] + scatter_scratch(rows, width),
        )
        return out, (grad_normed, other_grad), (own_tail, other_tail), small


def links():
    sizes = tuple(lax.axis_size(axis) for axis in ("shard", "context", "tensor"))
    return FourByFourByTwo() if sizes == (4, 4, 2) else AnyMesh()


def shards(inner_all, hidden_in, out_grad, doc_start, norm_in, w_z, w_x, w_bc, w_dt, conv_x, conv_bc, dt_bias, a_log,
           skip_d, norm_gate, w_out):
    micro, per_device, length, model = hidden_in.shape
    pieces = micro * per_device
    inner = w_z.shape[1]
    head_count = w_dt.shape[1]
    bc_width = w_bc.shape[1] * lax.axis_size("tensor")
    channels = bc_width + inner
    in_width = channels + LANES
    lead = HALO + length
    offset = lax.axis_index("context") * length

    head_of = np.arange(inner) // HEAD
    gather = jnp.asarray(head_of[:, None] == np.arange(LANES)[None], BF16)
    spread = jnp.asarray(head_of[None] == np.arange(LANES)[:, None], BF16)
    tri = jnp.asarray(np.tril(np.ones((length, length))), BF16)
    tri_up = jnp.asarray(np.triu(np.ones((length, length))), BF16)

    def head_row(row):
        return jnp.pad(row, (0, LANES - head_count))

    heads = jnp.stack([head_row(dt_bias), head_row(a_log)] + [jnp.zeros((LANES,), F32)] * 6)
    skip = jnp.repeat(skip_d, HEAD)[None]
    norm_in, norm_gate = norm_in[None], norm_gate[None]
    hid = hidden_in.reshape(pieces, length, model)
    seed = out_grad.reshape(pieces, length, model)
    between = links()
    w_in, halo, taps = between.inputs(hid, w_bc, w_dt, w_x, conv_bc, conv_x)
    ages = (offset + jnp.arange(length, dtype=jnp.int32) - doc_start.reshape(pieces, length)).astype(F32)
    age = jnp.broadcast_to(ages[:, :, None], (pieces, length, LANES))
    age_row = jnp.broadcast_to(ages[:, None, :], (pieces, 8, length))

    token = functools.partial(shaped, F32, pieces, length)
    token_low = functools.partial(shaped, BF16, pieces, length)
    state = shaped(BF16, pieces, LANES, inner)
    normed, raw, pre, dt_raw, cum, local, decay = call(
        forward_local, pieces,
        [(hid, by_piece), (halo, by_piece), (age, by_piece), (norm_in, fixed), (w_in, fixed), (taps, fixed),
         (heads, fixed), (spread, fixed), (tri, fixed)],
        [(shaped(BF16, pieces, lead, model), by_piece), (shaped(F32, pieces, lead, channels), by_piece),
         (token(channels), by_piece), (token(LANES), by_piece), (token(LANES), by_piece), (state, by_piece),
         (shaped(F32, pieces, 8, inner), by_piece)],
        [((length, channels), F32)], "forward_local",
    )

    state_in, w_z_all, w_out_t = between.states_up(local, decay, w_z, w_out)

    square = ((length, length), F32)
    token_wide = ((length, inner), F32)
    token_narrow = ((length, inner), BF16)
    mixer, gate, grad_gn, part, stats = call(
        forward_mix, pieces,
        [(pre, by_piece), (dt_raw, by_piece), (cum, by_piece), (age, by_piece), (state_in, by_piece), (normed, by_piece),
         (seed, by_piece), w_z_all, w_out_t, (norm_gate, fixed), (skip, fixed), (heads, fixed),
         (spread, fixed)],
        [(token(inner), by_piece), (token(inner), by_piece), (token(inner), by_piece), (token_low(model), by_piece),
         (shaped(F32, pieces, 8, length), by_piece)],
        [((length, LANES), F32), square, square, token_wide, token_wide, token_narrow], "forward_mix",
    )

    stats = between.over_cores(stats)

    grad_fed, grad_mix, grad_gate, grad_cum, grad_bc, grad_state, grad_wz, grad_wo, sums = call(
        functools.partial(backward_local, inner_all), pieces,
        [(mixer, by_piece), (gate, by_piece), (grad_gn, by_piece), (stats, by_piece), (pre, by_piece),
         (dt_raw, by_piece), (cum, by_piece), (age, by_piece), (age_row, by_piece), (state_in, by_piece),
         (normed, by_piece), (seed, by_piece), (norm_gate, fixed), (skip, fixed), (heads, fixed), (spread, fixed),
         (gather, fixed)],
        [(token(inner), by_piece), (token_low(inner), by_piece), (token_low(inner), by_piece), (token(LANES), by_piece),
         (token(bc_width), by_piece), (state, by_piece), (shaped(BF16, model, inner), fixed),
         (shaped(BF16, model, inner), fixed), (shaped(F32, 8, inner), fixed)],
        [((model, inner), F32), ((model, inner), F32), ((length, LANES), F32), square, square, square, token_wide,
         token_wide, token_narrow, token_narrow], "backward_local",
    )

    grad_later, sums_zo, (own_part, other_part) = between.states_down(grad_state, decay, grad_wz, grad_wo, part)

    grad_normed, grad_halo, grad_w, conv_sums, head_sums, norm_sums = call(
        backward_finish, pieces,
        [(grad_later, by_piece), (state_in, by_piece), (pre, by_piece), (raw, by_piece), (dt_raw, by_piece),
         (cum, by_piece), (age, by_piece), (grad_fed, by_piece), (grad_mix, by_piece), (grad_cum, by_piece),
         (grad_bc, by_piece), (grad_gate, by_piece), (normed, by_piece), (hid, by_piece), (halo, by_piece),
         (w_in, fixed), w_z_all, (taps, fixed), (skip, fixed), (norm_in, fixed), (heads, fixed),
         (spread, fixed), (gather, fixed), (tri_up, fixed)],
        [(token_low(model), by_piece), (shaped(BF16, pieces, HALO, model), by_piece),
         (shaped(BF16, model, in_width), fixed), (shaped(F32, 8, channels), fixed), (shaped(F32, 8, LANES), fixed),
         (shaped(F32, 8, model), fixed)],
        [((model, in_width), F32), token_wide, token_wide, token_wide, token_narrow,
         ((lead + 8, channels), F32), ((lead + 8, LANES), F32), ((lead, in_width), BF16), ((lead, model), F32)],
        "backward_finish",
    )

    own_bc = w_bc.shape[1]
    sums_w, (own_grad, other_grad), (own_tail, other_tail), small = between.last_sums(
        grad_w, grad_normed, grad_halo, conv_sums, norm_sums, head_sums, sums, own_bc
    )
    rows = w_z.shape[0]
    outputs = [shaped(F32, rows, inner), shaped(F32, rows, inner), shaped(F32, rows, own_bc),
               shaped(F32, rows, head_count), shaped(F32, inner, rows), shaped(F32, 5, inner), shaped(F32, 5, own_bc),
               shaped(F32, 1, head_count), shaped(F32, 1, head_count), shaped(F32, 1, head_count),
               shaped(F32, 1, inner), shaped(F32, 1, model)]
    (out, in_grad, grad_wz, grad_wx, grad_wbc, grad_wdt, grad_wo, grad_conv_x, grad_conv_bc, grad_dt_bias, grad_a_log,
     grad_skip, grad_norm_gate, grad_norm_in) = call(
        functools.partial(finish, inner_all), pieces,
        [(hid, by_piece), (seed, by_piece), (stats, by_piece), (norm_in, fixed), (own_part, by_piece),
         (other_part, by_piece_second), (own_grad, by_piece), (other_grad, by_piece_second), (own_tail, by_piece),
         (other_tail, by_piece_second), (sums_zo, fixed), (sums_w, fixed)] + [(array, fixed) for array in small]
        + [(gather, fixed)],
        [(token_low(model), by_piece), (token_low(model), by_piece)] + [(shape, fixed) for shape in outputs],
        [((length, model), F32)], "finish",
    )
    return (
        out.reshape(hidden_in.shape),
        in_grad.reshape(hidden_in.shape),
        grad_norm_in[0],
        grad_wz,
        grad_wx,
        grad_wbc,
        grad_wdt,
        grad_conv_x,
        grad_conv_bc,
        grad_dt_bias[0],
        grad_a_log[0],
        grad_skip[0],
        grad_norm_gate[0],
        grad_wo,
    )


def solution(mesh):
    whole = P(None, "shard", "context", None)
    rows = P(("shard", "context"), "tensor")
    lanes = P(None, "tensor")
    heads = P("tensor")
    w_out = P("tensor", ("shard", "context"))
    inputs = (whole, whole, P(None, "shard", "context"), P(), rows, rows, rows, rows, lanes, lanes, heads, heads, heads, heads, w_out)
    outputs = (whole, whole, P(), rows, rows, rows, rows, lanes, lanes, heads, heads, heads, heads, w_out)

    def placed(*arrays):
        inner_all = arrays[4].shape[1]
        return jax.shard_map(
            functools.partial(shards, inner_all), mesh=mesh, in_specs=inputs, out_specs=outputs, check_vma=False
        )(*arrays)

    return placed
```

```python
import functools

import jax
import jax.numpy as jnp
import numpy as np
from jax import lax
from jax.experimental import pallas as pl
from jax.experimental.pallas import tpu as pltpu
from jax.sharding import PartitionSpec as P

EPSILON = 1e-05
F32, BF16 = jnp.float32, jnp.bfloat16
HEAD = 64
LANES = 128
HALO = 16
GONE = -1e30
VMEM_BYTES = 60 * 1024 * 1024


def mm(left, right):
    return jnp.dot(left, right, preferred_element_type=F32)


def mm_nt(left, right):
    return lax.dot_general(left, right, (((1,), (1,)), ((), ())), preferred_element_type=F32)


def mm_tn(left, right):
    return lax.dot_general(left, right, (((0,), (0,)), ((), ())), preferred_element_type=F32)


def parts_of(value, count):
    parts = []
    for _ in range(count - 1):
        parts.append(value.astype(BF16))
        value = value - parts[-1].astype(F32)
    return parts + [value.astype(BF16)]


def pick(value, ones, count=2):
    return sum(mm(part, ones) for part in parts_of(value, count))


def pick_left(ones, value, count=3):
    return sum(mm(ones, part) for part in parts_of(value, count))


def softplus(value):
    return jnp.maximum(value, 0.0) + jnp.log1p(jnp.exp(-jnp.abs(value)))


def sigmoid(value):
    return 1.0 / (1.0 + jnp.exp(-value))


def column_blocks(width):
    return [(at, min(LANES, width - at)) for at in range(0, width, LANES)]


def row_index(length):
    return lax.broadcasted_iota(jnp.int32, (length, LANES), 0).astype(F32)


def is_first_step():
    return pl.program_id(0) == 0


def is_last_step():
    return pl.program_id(0) == pl.num_programs(0) - 1


def half_masks(width):
    lane = lax.broadcasted_iota(jnp.int32, (1, width), 1)
    return [(lane // HEAD) == k for k in range(width // HEAD)]


def normalised(hidden, gain):
    scale = lax.rsqrt(jnp.mean(hidden * hidden, -1, keepdims=True) + EPSILON)
    return hidden * scale * gain, scale


def project(hid, halo, age, norm_in, w_in, taps, heads, spread, tri,
            normed, raw, pre, dt_raw, cum, local, decay, act):
    length, channels = hid.shape[0], taps.shape[1]
    bc_width = 2 * LANES
    normed[:HALO] = normalised(halo[...].astype(F32), norm_in[...])[0].astype(BF16)
    for at in range(0, length, 64):
        rows = normalised(hid[at : at + 64].astype(F32), norm_in[...])[0]
        normed[HALO + at : HALO + at + 64] = rows.astype(BF16)
    raw[:, :bc_width] = mm(normed[...], w_in[:, :bc_width])
    raw[:, bc_width:] = mm(normed[...], w_in[:, bc_width + LANES :])
    dt_raw[...] = mm(normed[HALO:], w_in[:, bc_width : bc_width + LANES])
    for at, width in column_blocks(channels):
        cols = slice(at, at + width)
        running = jnp.broadcast_to(taps[4:5, cols], (length, width))
        for lag in range(4):
            tapped = raw[HALO - lag : HALO - lag + length, cols]
            if lag:
                tapped = jnp.where(age[:, :width] >= lag, tapped, 0.0)
            running = running + taps[lag : lag + 1, cols] * tapped
        pre[:, cols] = running
        act[:, cols] = running * sigmoid(running)
    step = softplus(dt_raw[...] + heads[0:1])
    total = pick_left(tri[...], -jnp.exp(heads[1:2]) * step)
    cum[...] = total
    last, age_last = total[length - 1 :], age[length - 1 :]
    open_end = row_index(length) - (length - 1) + age_last >= 0
    weight = jnp.where(open_end, jnp.exp(last - total), 0.0) * step
    weighted = (act[:, bc_width:] * pick(weight, spread[...])).astype(BF16)
    local[...] = mm_tn(act[:, :LANES].astype(BF16), weighted).astype(BF16)
    kept = jnp.where(age_last > length - 1, jnp.exp(last), 0.0)
    decay[...] = pick(jnp.broadcast_to(kept, (8, LANES)), spread[...], 3)


def activated(pre):
    value = pre[...]
    return (value * sigmoid(value)).astype(BF16)


def mix_within(pre, dt_raw, cum, age, normed, out_grad, w_z, w_out_t, skip, heads, spread,
               near, gate, grad_gn, seg, pair, step_x):
    length, inner = near.shape
    bc_width = 2 * LANES
    gate[...] = mm(normed[HALO:], w_z())
    grad_gn[...] = mm(out_grad[...], w_out_t())
    pair[...] = mm_nt(activated(pre.at[:, LANES:bc_width]), activated(pre.at[:, :LANES]))
    row = lax.broadcasted_iota(jnp.int32, (length, length), 0)
    col = lax.broadcasted_iota(jnp.int32, (length, length), 1)
    back = (row - col).astype(F32)
    seg[...] = jnp.where((back >= 0) & (back <= age[:, :1]), 0.0, GONE)
    total = cum[...]
    total_t = total.T
    step_x[...] = pick(softplus(dt_raw[...] + heads[0:1]), spread[...])
    for at, width in column_blocks(inner):
        cols = slice(at, at + width)
        x_pre = pre[:, bc_width + at : bc_width + at + width]
        values = x_pre * sigmoid(x_pre)
        fed = (values * step_x[:, cols]).astype(BF16)
        masks = half_masks(width)
        near[:, cols] = skip[:, cols] * values
        for start in range(0, length, LANES):
            stop = start + LANES
            found = near[start:stop, cols]
            for k, mask in enumerate(masks):
                head = at // HEAD + k
                spread_log = total[start:stop, head : head + 1] - total_t[head : head + 1, :stop]
                mixing = pair[start:stop, :stop] * jnp.exp(spread_log + seg[start:stop, :stop])
                found = found + mm(mixing.astype(BF16), jnp.where(mask, fed[:stop], 0))
            near[start:stop, cols] = found


def mix_states(pre, cum, age, state_in, near, gate, grad_gn, w_out_t, norm_gate, spread,
               mixer, part, stats, carried, gated_low):
    length, inner = near.shape
    open_start = age[...] > row_index(length)
    carried[...] = pick(jnp.where(open_start, jnp.exp(cum[...]), 0.0), spread[...])
    carried[...] = carried[...] * mm(activated(pre.at[:, LANES : 2 * LANES]), state_in[...])
    squares = jnp.zeros((length, 1), F32)
    products = jnp.zeros((length, 1), F32)
    for at, width in column_blocks(inner):
        cols = slice(at, at + width)
        mixed = near[:, cols] + carried[:, cols]
        mixer[:, cols] = mixed
        raw_gate = gate[:, cols]
        gated = mixed * (raw_gate * sigmoid(raw_gate))
        weighted = gated * norm_gate[:, cols]
        gated_low[:, cols] = weighted.astype(BF16)
        squares = squares + jnp.sum(gated * gated, 1, keepdims=True)
        products = products + jnp.sum(grad_gn[:, cols] * weighted, 1, keepdims=True)
    part[...] = mm_nt(gated_low[...], w_out_t()).astype(BF16)
    lane = lax.broadcasted_iota(jnp.int32, (length, LANES), 1)
    columns = jnp.where(lane == 0, squares, jnp.where(lane == 1, products, 0.0))
    stats[...] = columns.T[:8]


def forward_local(hid, halo, age, norm_in, w_in, taps, heads, spread, tri,
                  normed, raw, pre, dt_raw, cum, local, decay, act):
    project(hid.at[0], halo.at[0], age.at[0], norm_in, w_in, taps, heads, spread, tri, normed.at[0], raw.at[0],
            pre.at[0], dt_raw.at[0], cum.at[0], local.at[0], decay.at[0], act)


def forward_mix(pre, dt_raw, cum, age, state_in, normed, out_grad, w_z, w_out_t, norm_gate, skip, heads, spread,
                mixer, gate, grad_gn, part, stats, near, seg, pair, carried, step_x, gated_low):
    w_z_all, w_out_all = (lambda: w_z[...]), (lambda: w_out_t[...])
    mix_within(pre.at[0], dt_raw.at[0], cum.at[0], age.at[0], normed.at[0], out_grad.at[0], w_z_all, w_out_all, skip,
               heads, spread, near, gate.at[0], grad_gn.at[0], seg, pair, step_x)
    mix_states(pre.at[0], cum.at[0], age.at[0], state_in.at[0], near, gate.at[0], grad_gn.at[0], w_out_all, norm_gate,
               spread, mixer.at[0], part.at[0], stats.at[0], carried, gated_low)


def backward_local(inner_all, mixer, gate, grad_gn, stats, pre, dt_raw, cum, age, age_row, state_in, normed, out_grad,
                   norm_gate, skip, heads, spread, gather,
                   grad_fed, grad_mix, grad_gate, grad_cum, grad_bc, grad_state, grad_wz, grad_wo, sums,
                   sum_z, sum_o, near, seg, pair, grad_pair, carried, step_x, gated_low, from_state):
    length, inner = mixer.shape[1:]
    bc_width = 2 * LANES

    @pl.when(is_first_step())
    def _():
        sum_z[...] = jnp.zeros_like(sum_z)
        sum_o[...] = jnp.zeros_like(sum_o)
        sums[...] = jnp.zeros_like(sums)

    readout = pre[0, :, LANES:bc_width]
    readout = (readout * sigmoid(readout)).astype(BF16)
    inputs_b = pre[0, :, :LANES]
    inputs_b = (inputs_b * sigmoid(inputs_b)).astype(BF16)
    pair[...] = mm_nt(inputs_b, readout)
    grad_pair[...] = jnp.zeros_like(grad_pair)
    row = lax.broadcasted_iota(jnp.int32, (length, length), 0)
    col = lax.broadcasted_iota(jnp.int32, (length, length), 1)
    back = (col - row).astype(F32)
    seg[...] = jnp.where((back >= 0) & (back <= age_row[0][:1]), 0.0, GONE)
    total = cum[0]
    total_t = total.T
    step = softplus(dt_raw[0] + heads[0:1])
    step_x[...] = pick(step, spread[...])
    open_start = age[0] > row_index(length)
    carried[...] = pick(jnp.where(open_start, jnp.exp(total), 0.0), spread[...])
    means = stats[0].T / inner_all
    scale = lax.rsqrt(means[:, :1] + EPSILON)
    pull = scale * scale * scale * means[:, 1:2]
    rows_sum = jnp.zeros((length, LANES), F32)
    for at, width in column_blocks(inner):
        cols = slice(at, at + width)
        x_pre = pre[0, :, bc_width + at : bc_width + at + width]
        values = x_pre * sigmoid(x_pre)
        fed = (values * step_x[:, cols]).astype(BF16)
        mixed = mixer[0, :, cols]
        raw_gate = gate[0, :, cols]
        logistic = sigmoid(raw_gate)
        acted = raw_gate * logistic
        gated = mixed * acted
        grad_out = grad_gn[0, :, cols]
        gated_scaled = gated * scale
        gated_low[:, cols] = (gated_scaled * norm_gate[:, cols]).astype(BF16)
        grad_gated = scale * (grad_out * norm_gate[:, cols]) - gated * pull
        grad_gate[0, :, cols] = (grad_gated * mixed * (logistic * (1.0 + raw_gate * (1.0 - logistic)))).astype(BF16)
        mix_low = (grad_gated * acted).astype(BF16)
        grad_mix[0, :, cols] = mix_low
        mix_wide = mix_low.astype(F32)
        sums[0:1, cols] += jnp.sum(grad_out * gated_scaled, 0, keepdims=True)
        sums[1:2, cols] += jnp.sum(mix_wide * values, 0, keepdims=True)
        rows_sum = rows_sum + pick(mix_wide * (mixed - skip[:, cols] * values), gather[cols])
        from_state[:, cols] = (carried[:, cols] * mix_wide).astype(BF16)
        masks = half_masks(width)
        for start in range(0, length, LANES):
            stop = start + LANES
            found = jnp.zeros((LANES, width), F32)
            for k, mask in enumerate(masks):
                head = at // HEAD + k
                spread_log = total_t[head : head + 1, start:] - total[start:stop, head : head + 1]
                decayed = jnp.exp(spread_log + seg[start:stop, start:])
                mixing = (pair[start:stop, start:] * decayed).astype(BF16)
                grad_mixing = mm_nt(jnp.where(mask, fed[start:stop], 0), mix_low[start:])
                grad_pair[start:stop, start:] += grad_mixing * decayed
                found = found + mm(mixing, jnp.where(mask, mix_low[start:], 0))
            near[start:stop, :width] = found
        grad_fed[0, :, cols] = near[:, :width]
        rows_sum = rows_sum - pick(near[:, :width] * fed.astype(F32), gather[cols])
    grad_cum[0] = rows_sum
    pair_low = grad_pair[...].astype(BF16)
    grad_bc[0, :, :LANES] = mm(pair_low, readout)
    grad_bc[0, :, LANES:] = mm_tn(pair_low, inputs_b) + mm_nt(from_state[...], state_in[0])
    grad_state[0] = mm_tn(readout, from_state[...]).astype(BF16)
    sum_z[...] += mm_tn(normed[0, HALO:], grad_gate[0])
    sum_o[...] += mm_tn(out_grad[0], gated_low[...])

    @pl.when(is_last_step())
    def _():
        grad_wz[...] = sum_z[...].astype(BF16)
        grad_wo[...] = sum_o[...].astype(BF16)


def backward_finish(grad_later, state_in, pre, raw, dt_raw, cum, age, grad_fed, grad_mix, grad_cum, grad_bc, grad_gate,
                    normed, hid, halo, w_in, w_z, taps, skip, norm_in, heads, spread, gather, tri_up,
                    grad_normed, grad_halo, grad_w, conv_sums, head_sums, norm_sums,
                    sum_w, step_x, open_x, from_state, fed_state, slope, age_long, grad_in, wide):
    length, inner = grad_fed.shape[1:]
    channels = taps.shape[1]
    bc_width = 2 * LANES
    lead = HALO + length

    @pl.when(is_first_step())
    def _():
        sum_w[...] = jnp.zeros_like(sum_w)
        conv_sums[...] = jnp.zeros_like(conv_sums)
        head_sums[...] = jnp.zeros_like(head_sums)
        norm_sums[...] = jnp.zeros_like(norm_sums)
        slope[:HALO] = jnp.zeros((HALO, channels), F32)
        slope[lead:] = jnp.zeros((8, channels), F32)
        age_long[:HALO] = jnp.zeros((HALO, LANES), F32)
        age_long[lead:] = jnp.zeros((8, LANES), F32)
        grad_in[:HALO, bc_width : bc_width + LANES] = jnp.zeros((HALO, LANES), BF16)

    age_long[HALO:lead] = age[0]
    total = cum[0]
    step_raw = dt_raw[0] + heads[0:1]
    step = softplus(step_raw)
    rate = -jnp.exp(heads[1:2])
    step_x[...] = pick(step, spread[...])
    last, age_last = total[length - 1 :], age[0, length - 1 :]
    open_end = row_index(length) - (length - 1) + age_last >= 0
    open_x[...] = pick(jnp.where(open_end, jnp.exp(last - total), 0.0), spread[...])
    b_pre = pre[0, :, :LANES]
    inputs_b = (b_pre * sigmoid(b_pre)).astype(BF16)
    from_state[...] = open_x[...] * mm(inputs_b, grad_later[0])
    state_sum = jnp.zeros((length, LANES), F32)
    step_sum = jnp.zeros((length, LANES), F32)
    for at, width in column_blocks(inner):
        cols = slice(at, at + width)
        x_pre = pre[0, :, bc_width + at : bc_width + at + width]
        logistic = sigmoid(x_pre)
        values = x_pre * logistic
        fed = values * step_x[:, cols]
        fed_state[:, cols] = (fed * open_x[:, cols]).astype(BF16)
        arrived = from_state[:, cols]
        grad = grad_fed[0, :, cols] + arrived
        state_sum = state_sum + pick(fed * arrived, gather[cols])
        step_sum = step_sum + pick(values * grad, gather[cols])
        grad_values = grad * step_x[:, cols] + skip[:, cols] * grad_mix[0, :, cols].astype(F32)
        slope[HALO:lead, bc_width + at : bc_width + at + width] = grad_values * (
            logistic * (1.0 + x_pre * (1.0 - logistic))
        )
    for at, extra in ((0, mm_nt(fed_state[...], grad_later[0])), (LANES, 0.0)):
        cols = slice(at, at + LANES)
        bc_pre = pre[0, :, cols]
        logistic = sigmoid(bc_pre)
        slope[HALO:lead, cols] = (grad_bc[0, :, cols] + extra) * (logistic * (1.0 + bc_pre * (1.0 - logistic)))
    kept = jnp.where(age_last > length - 1, jnp.exp(last), 0.0)
    met = jnp.sum(grad_later[0].astype(F32) * state_in[0].astype(F32), 0, keepdims=True)
    met = pick(jnp.broadcast_to(met, (8, inner)), gather[...], 3)[:1]
    end = met * kept + jnp.sum(state_sum, 0, keepdims=True)
    grad_a = pick_left(tri_up[...], grad_cum[0] - state_sum) + end
    head_sums[1:2] += jnp.sum(grad_a * rate * step, 0, keepdims=True)
    grad_step = (step_sum + grad_a * rate) * sigmoid(step_raw)
    head_sums[0:1] += jnp.sum(grad_step, 0, keepdims=True)
    grad_in[HALO:, bc_width : bc_width + LANES] = grad_step.astype(BF16)
    for at, width in column_blocks(channels):
        cols = slice(at, at + width)
        shifted = at if at < bc_width else at + LANES
        own = slope[HALO:lead, cols]
        total_in = taps[0:1, cols] * slope[:lead, cols]
        conv_sums[0:1, cols] += jnp.sum(own * raw[0, HALO:, cols], 0, keepdims=True)
        for lag in range(1, 4):
            kept_lag = jnp.where(age[0, :, :width] >= lag, own, 0.0)
            conv_sums[lag : lag + 1, cols] += jnp.sum(
                kept_lag * raw[0, HALO - lag : lead - lag, cols], 0, keepdims=True
            )
            later = jnp.where(age_long[lag : lead + lag, :width] >= lag, slope[lag : lead + lag, cols], 0.0)
            total_in = total_in + taps[lag : lag + 1, cols] * later
        conv_sums[4:5, cols] += jnp.sum(own, 0, keepdims=True)
        grad_in[:, shifted : shifted + width] = total_in.astype(BF16)
    wide[...] = mm_nt(grad_in[...], w_in[...])
    wide[HALO:] += mm_nt(grad_gate[0], w_z[...])
    hidden = halo[0].astype(F32)
    scale = normalised(hidden, 1.0)[1]
    norm_sums[0:1] += jnp.sum(wide[:HALO] * hidden * scale, 0, keepdims=True)
    for at in range(0, length, 64):
        hidden = hid[0, at : at + 64].astype(F32)
        scale = normalised(hidden, 1.0)[1]
        norm_sums[0:1] += jnp.sum(wide[HALO + at : HALO + at + 64] * hidden * scale, 0, keepdims=True)
    grad_halo[0] = wide[:HALO].astype(BF16)
    grad_normed[0] = wide[HALO:].astype(BF16)
    sum_w[...] += mm_tn(normed[0], grad_in[...])

    @pl.when(is_last_step())
    def _():
        grad_w[...] = sum_w[...].astype(BF16)


def finish(inner_all, hid, out_grad, stats, norm_in, own_part, other_part, own_grad, other_grad, own_tail, other_tail,
           sums_zo, sums_w, conv_sums, norm_sums, head_sums, inner_sums, gather,
           out, in_grad, grad_wz, grad_wx, grad_wbc, grad_wdt, grad_wo, grad_conv_x, grad_conv_bc, grad_dt_bias,
           grad_a_log, grad_skip, grad_norm_gate, grad_norm_in, total):
    length = hid.shape[1]

    def added(own, others, rows):
        found = own[0, rows].astype(F32)
        for k in range(others.shape[0]):
            found = found + others[k, 0, rows].astype(F32)
        return found

    everything = slice(None)
    total[...] = added(own_grad, other_grad, everything)
    total[length - HALO :] += added(own_tail, other_tail, everything)
    scales = lax.rsqrt(stats[0].T[:, :1] / inner_all + EPSILON)
    for at in range(0, length, 64):
        rows = slice(at, at + 64)
        hidden = hid[0, rows].astype(F32)
        out[0, rows] = (hidden + scales[rows] * added(own_part, other_part, rows)).astype(BF16)
        scale = normalised(hidden, 1.0)[1]
        weighted = total[rows] * norm_in[...]
        inner_mean = jnp.mean(weighted * hidden, -1, keepdims=True)
        in_grad[0, rows] = (
            out_grad[0, rows].astype(F32) + scale * weighted - hidden * (scale * scale * scale * inner_mean)
        ).astype(BF16)

    @pl.when(is_last_step())
    def _():
        inner, own_bc, head_count = grad_wz.shape[1], grad_wbc.shape[1], grad_wdt.shape[1]
        grad_wz[...] = sums_zo[:, :inner]
        grad_wo[...] = sums_zo[:, inner:].T
        grad_wbc[...] = sums_w[:, :own_bc]
        grad_wdt[...] = sums_w[:, own_bc : own_bc + head_count]
        grad_wx[...] = sums_w[:, own_bc + LANES :]
        grad_conv_bc[...] = conv_sums[:5, :own_bc]
        grad_conv_x[...] = conv_sums[:5, own_bc:]
        grad_dt_bias[...] = head_sums[0:1, :head_count]
        grad_a_log[...] = head_sums[1:2, :head_count]
        grad_norm_in[...] = norm_sums[0:1]
        grad_norm_gate[...] = inner_sums[0:1]
        grad_skip[...] = pick(inner_sums[...], gather[...], 3)[1:2, :head_count]


def by_piece(array):
    rest = array.shape[1:]
    return pl.BlockSpec((1,) + rest, lambda i: (i,) + (0,) * len(rest))


def by_piece_second(array):
    rest = array.shape[2:]
    return pl.BlockSpec((array.shape[0], 1) + rest, lambda i: (0, i) + (0,) * len(rest))


def fixed(array):
    return pl.BlockSpec(array.shape, lambda i: (0,) * len(array.shape))


def call(kernel, pieces, inputs, outputs, scratch, name):
    return pl.pallas_call(
        kernel,
        grid=(pieces,),
        in_specs=[cut(array) for array, cut in inputs],
        out_specs=[cut(shape) for shape, cut in outputs],
        out_shape=[shape for shape, _ in outputs],
        scratch_shapes=[pltpu.VMEM(shape, kind) for shape, kind in scratch],
        compiler_params=pltpu.CompilerParams(vmem_limit_bytes=VMEM_BYTES),
        name=name,
    )(*[array for array, _ in inputs])


def shaped(kind, *dims):
    return jax.ShapeDtypeStruct(dims, kind)


MESH = pl.DeviceIdType.MESH
UP, DOWN, NEXT_X, NEXT_Y = range(4)


def coordinates():
    return lax.axis_index("shard"), lax.axis_index("context"), lax.axis_index("tensor")


def greet(partners):
    barrier = pltpu.get_barrier_semaphore()
    count = 0
    for there, device in partners:
        if there is True:
            pl.semaphore_signal(barrier, inc=1, device_id=device, device_id_type=MESH)
            count = count + 1
        else:
            pl.when(there)(
                functools.partial(pl.semaphore_signal, barrier, inc=1, device_id=device, device_id_type=MESH)
            )
            count = count + there.astype(jnp.int32)
    pl.semaphore_wait(barrier, count)


class Copies:
    def __init__(self, send):
        self.send, self.used, self.started = send, 0, []

    def make(self, source, target, received, device, send=0):
        return pltpu.make_async_remote_copy(
            src_ref=source, dst_ref=target, send_sem=self.send.at[send], recv_sem=received,
            device_id=device, device_id_type=MESH,
        )

    def start(self, source, target, received, device, there=True):
        copy = self.make(source, target, received, device, self.used)
        self.used += 1
        self.started.append((there, copy))
        if there is True:
            copy.start()
        else:
            pl.when(there)(copy.start)

    def arrived(self, target, received, there=True):
        copy = self.make(target, target, received, {"tensor": 1 - lax.axis_index("tensor")})
        if there is True:
            copy.wait_recv()
        else:
            pl.when(there)(copy.wait_recv)

    def finish(self):
        for there, copy in self.started:
            if there is True:
                copy.wait_send()
            else:
                pl.when(there)(copy.wait_send)


def neighbours(place):
    shard, context, _ = place
    count = lax.axis_size("context")
    return [
        (context + 1 < count, {"context": context + 1}),
        (context > 0, {"context": context - 1}),
        (True, {"shard": shard ^ 1}),
        (True, {"shard": shard ^ 2}),
    ]


def gather_step(step, start, arrived, stage, out, received):
    place = shard, context, _ = coordinates()
    count = lax.axis_size("context")
    up, down, next_x, next_y = neighbours(place)
    mine, beside_x, beside_y, across = [(shard ^ k) * count for k in (0, 1, 2, 3)]

    def pass_on(number, source, slot, to, there=True):
        if to[0] is not True:
            there = to[0] if there is True else there & to[0]
        start(number, source, out.at[slot], received.at[slot], to[1], there)

    def both_ways(distance):
        found = [(context - distance, context >= distance, up),
                 (context + distance, context + distance < count, down)]
        return [(jnp.clip(at, 0, count - 1), there, to) for at, there, to in found[: 2 if distance else 1]]

    if step == 0:
        for k, to in enumerate((up, down, next_x, next_y)):
            pass_on(k, stage, mine + context, to)
    elif step < count:
        for k, (at, there, to) in enumerate(both_ways(step)):
            slot = mine + at
            arrived(out.at[slot], received.at[slot], there)
            for m, target in enumerate((to, next_x, next_y)):
                pass_on(4 + (step - 1) * 6 + k * 3 + m, out.at[slot], slot, target, there)
    elif step < 2 * count:
        for k, (at, there, _) in enumerate(both_ways(step - count)):
            number = 4 + (count - 1) * 6 + (step - count) * 4 + k * 2
            slot_x, slot_y = beside_x + at, beside_y + at
            arrived(out.at[slot_x], received.at[slot_x], there)
            pass_on(number, out.at[slot_x], slot_x, next_y, there & (at < count // 2))
            arrived(out.at[slot_y], received.at[slot_y], there)
            pass_on(number + 1, out.at[slot_y], slot_y, next_x, there & (at >= count // 2))
    else:
        for at in range(count):
            arrived(out.at[across + at], received.at[across + at], True)


def gather_steps():
    return 2 * lax.axis_size("context") + 1


GATHER_COPIES = 40


class Numbered:
    def __init__(self, send):
        self.send = send

    def copy(self, number, source, target, received, device):
        return pltpu.make_async_remote_copy(
            src_ref=source, dst_ref=target, send_sem=self.send.at[number], recv_sem=received,
            device_id=device, device_id_type=MESH,
        )

    def when(self, there, action):
        if there is True:
            action()
        else:
            pl.when(there)(action)

    def start(self, number, source, target, received, device, there=True):
        self.when(there, self.copy(number, source, target, received, device).start)

    def sent(self, number, source, target, received, device, there=True):
        self.when(there, self.copy(number, source, target, received, device).wait_send)

    def arrived(self, target, received, there=True):
        other = {"tensor": 1 - lax.axis_index("tensor")}
        self.when(there, self.copy(0, target, target, received, other).wait_recv)

    def nothing(self, *_):
        pass


def scatter_scratch(rows, width):
    block = pltpu.VMEM((4, rows, width), BF16)
    return [block, block, block, block, block, block, block, block, pltpu.VMEM((4, rows, width), F32),
            pltpu.SemaphoreType.DMA((5, 4))]


SCATTER_COPIES = 20


def scatter_blocks(copies, place, blocks, out, first, from_x, from_y, from_up, from_down, to_first, to_up, to_down,
                   column, received):
    shard, context, _ = place
    count = lax.axis_size("context")
    up, down, next_x, next_y = neighbours(place)
    mine, beside_x, beside_y, across = [(shard ^ k) * count for k in (0, 1, 2, 3)]
    low, high = range(count // 2), range(count // 2, count)
    for at in range(count // 2):
        for k, to in ((at, next_y), (at + count // 2, next_x)):
            copies.start(blocks.at[across + k], first.at[k], received.at[0, k], to[1])
    for k in reversed(high):
        copies.start(blocks.at[beside_x + k], from_x.at[k], received.at[1, k], next_x[1])
    for k in low:
        copies.start(blocks.at[beside_y + k], from_y.at[k], received.at[2, k], next_y[1])
    yield
    for at in range(count // 2):
        for k, beside, buffers, row, to in ((at, beside_x, from_x, 1, next_x), (count - 1 - at, beside_y, from_y, 2, next_y)):
            copies.arrived(first.at[k], received.at[0, k])
            to_first[k] = (blocks[beside + k].astype(F32) + first[k].astype(F32)).astype(BF16)
            copies.start(to_first.at[k], buffers.at[k], received.at[row, k], to[1])
        yield
    for at in range(count):
        k = count - 1 - at // 2 if at % 2 == 0 else at // 2
        copies.arrived(from_x.at[k], received.at[1, k])
        copies.arrived(from_y.at[k], received.at[2, k])
        column[k] = blocks[mine + k].astype(F32) + from_x[k].astype(F32) + from_y[k].astype(F32)
        yield
    for at in range(count - 1):
        k = count - 1 - at

        @pl.when(context < k)
        def _(k=k):
            @pl.when(context > 0)
            def _():
                copies.arrived(from_down.at[k], received.at[3, k])
                to_up[k] = (column[k] + from_down[k].astype(F32)).astype(BF16)

            @pl.when(context == 0)
            def _():
                to_up[k] = column[k].astype(BF16)

        copies.start(to_up.at[k], from_down.at[k], received.at[3, k], up[1], context < k)
        k = at

        @pl.when(context > k)
        def _(k=k):
            @pl.when(context < count - 1)
            def _():
                copies.arrived(from_up.at[k], received.at[4, k])
                to_down[k] = (column[k] + from_up[k].astype(F32)).astype(BF16)

            @pl.when(context == count - 1)
            def _():
                to_down[k] = column[k].astype(BF16)

        copies.start(to_down.at[k], from_up.at[k], received.at[4, k], down[1], context > k)
        yield
    out[...] = column[context]

    @pl.when(context > 0)
    def _():
        copies.arrived(from_down.at[context], received.at[3, context])
        out[...] += from_down[context].astype(F32)

    @pl.when(context < count - 1)
    def _():
        copies.arrived(from_up.at[context], received.at[4, context])
        out[...] += from_up[context].astype(F32)


def gather_inputs(w_bc, w_dt, w_x, conv_bc, conv_x, hid, out, halo, taps, stage, passing, send, received, others, own):
    place = shard, context, tensor = coordinates()
    length = hid.shape[1]
    own_bc, head_count = w_bc.shape[1], w_dt.shape[1]
    bc_width = 2 * LANES
    partner = {"tensor": 1 - tensor}
    around = neighbours(place)
    stage[:, bc_width : bc_width + LANES] = jnp.zeros((stage.shape[0], LANES), BF16)
    stage[:, bc_width : bc_width + head_count] = w_dt[...]
    stage[:, bc_width + LANES :] = w_x[...]
    cols = pl.ds(pl.multiple_of(tensor * own_bc, LANES), own_bc)
    other_cols = pl.ds(pl.multiple_of((1 - tensor) * own_bc, LANES), own_bc)
    stage[:, cols] = w_bc[...]
    taps[...] = jnp.zeros_like(taps)
    taps[:5, cols] = conv_bc[...]
    taps[:5, bc_width:] = conv_x[...]
    greet(around + [(True, partner)])
    copies = Copies(send)
    copies.start(stage.at[:, cols], stage.at[:, cols], others.at[0], partner)
    copies.start(taps.at[:, cols], taps.at[:, cols], others.at[1], partner)
    tail = pl.ds(length - HALO, HALO)
    copies.start(hid.at[:, tail], halo, others.at[2], around[UP][1], around[UP][0])
    copies.arrived(stage.at[:, other_cols], others.at[0])
    numbered = Numbered(passing)
    local = pltpu.make_async_copy(stage, out.at[shard * lax.axis_size("context") + context], own)
    local.start()
    for step in range(gather_steps()):
        gather_step(step, numbered.start, numbered.arrived, stage, out, received)
    for step in range(gather_steps()):
        gather_step(step, numbered.sent, numbered.nothing, stage, out, received)
    local.wait()
    copies.arrived(taps.at[:, other_cols], others.at[1])
    copies.arrived(halo, others.at[2], context > 0)

    @pl.when(context == 0)
    def _():
        clear = pltpu.make_async_copy(hid.at[:, tail], halo, others.at[2])
        clear.start()
        clear.wait()

    copies.finish()


def chain_states(copies, place, local, decay, arrived, leaving, received, by):
    _, context, _ = place
    count = lax.axis_size("context")
    first = context == (0 if by > 0 else count - 1)
    last = context == (count - 1 if by > 0 else 0)
    to = {"context": context + by}
    pieces = local.shape[0]

    def sent(i):
        return pltpu.make_async_remote_copy(
            src_ref=leaving.at[i], dst_ref=arrived.at[i], send_sem=received.at[1, i], recv_sem=received.at[0, i],
            device_id=to, device_id_type=MESH,
        )

    for i in range(pieces):

        @pl.when(first)
        def _(i=i):
            arrived[i] = jnp.zeros_like(arrived[i])
            leaving[i] = local[i]

        @pl.when(jnp.logical_not(first))
        def _(i=i):
            copies.arrived(arrived.at[i], received.at[0, i])

        @pl.when(jnp.logical_not(first | last))
        def _(i=i):
            leaving[i] = (decay[i, :1] * arrived[i].astype(F32) + local[i].astype(F32)).astype(BF16)

        pl.when(jnp.logical_not(last))(sent(i).start)
        yield
    for i in range(pieces):
        pl.when(jnp.logical_not(last))(sent(i).wait_send)


def in_turn(*steps):
    steps = list(steps)
    while steps:
        for one in list(steps):
            try:
                next(one)
            except StopIteration:
                steps.remove(one)


GATHER_TURNS = (0, 1, 2, 3, 3, 4, 5, 6, 7)


def forward(hid, halo, age, out_grad, norm_in, w_in, w_z, w_out, taps, heads, spread, tri, norm_gate, skip,
            raw, mixer, part, stats, normed_out, pre_out, dt_out, cum_out, gate_out, grad_gn_out, state_out, decay_out,
            both_out,
            normed, pre, dt_raw, cum, gate, grad_gn, near, leaving, arrived, decay, both, stage, act, seg, pair, step_x,
            gated_low, send, received, own, states, stores):
    place = shard, context, _ = coordinates()
    phase, i = pl.program_id(0), pl.program_id(1)
    pieces = pl.num_programs(1)
    inner = w_z.shape[1]
    count = lax.axis_size("context")
    numbered = Numbered(send)

    def store(k, source, target):
        return pltpu.make_async_copy(source.at[i], target.at[i], stores.at[k, i])

    first, last = context == 0, context == count - 1

    def passed(c):
        return pltpu.make_async_remote_copy(
            src_ref=leaving.at[c], dst_ref=arrived.at[c], send_sem=states.at[1, c], recv_sem=states.at[0, c],
            device_id={"context": context + 1}, device_id_type=MESH,
        )

    @pl.when((phase == 0) & (i == 0))
    def _():
        stage[:, :inner] = w_z[...]
        stage[:, inner:] = w_out[...].astype(F32).T.astype(BF16)
        greet(neighbours(place))
        gather_step(0, numbered.start, numbered.arrived, stage, both, received)
        pltpu.make_async_copy(stage, both.at[shard * count + context], own).start()

    turn = phase * pieces + i
    c = jnp.clip(turn // 2 - context, 0, pieces - 1)

    @pl.when((turn % 2 == 0) & (turn // 2 >= context) & (turn // 2 - context < pieces) & jnp.logical_not(first | last))
    def _():
        passed(c).wait_recv()
        leaving[c] = (decay[c, :1] * arrived[c].astype(F32) + leaving[c].astype(F32)).astype(BF16)
        passed(c).start()

    @pl.when(phase == 0)
    def _():
        project(hid.at[0], halo.at[0], age.at[0], norm_in, w_in, taps, heads, spread, tri, normed.at[i], raw.at[0],
                pre.at[i], dt_raw.at[i], cum.at[i], leaving.at[i], decay.at[i], act)
        for k, (source, target) in enumerate(((normed, normed_out), (pre, pre_out), (dt_raw, dt_out), (cum, cum_out),
                                              (decay, decay_out))):
            store(k, source, target).start()

        @pl.when(first)
        def _():
            arrived[i] = jnp.zeros(arrived.shape[1:], BF16)
            passed(i).start()

    for step in range(1, gather_steps()):

        @pl.when((phase == 0) & (i == GATHER_TURNS[step]))
        def _(step=step):
            gather_step(step, numbered.start, numbered.arrived, stage, both, received)

    @pl.when((phase == 0) & (i == pieces - 1))
    def _():
        for step in range(gather_steps()):
            gather_step(step, numbered.sent, numbered.nothing, stage, both, received)
        pltpu.make_async_copy(stage, both.at[shard * count + context], own).wait()
        pltpu.make_async_copy(both, both_out, own).start()

    @pl.when((phase == 1) & (i == pieces - 1))
    def _():
        pltpu.make_async_copy(both, both_out, own).wait()

    def w_z_all():
        return both[:, :, :inner].reshape(-1, inner)

    def w_out_all():
        return both[:, :, inner:].reshape(-1, inner)

    @pl.when(phase == 1)
    def _():
        mix_within(pre.at[i], dt_raw.at[i], cum.at[i], age.at[0], normed.at[i], out_grad.at[0], w_z_all, w_out_all, skip,
                   heads, spread, near.at[i], gate.at[i], grad_gn.at[i], seg, pair, step_x)
        store(5, gate, gate_out).start()
        store(6, grad_gn, grad_gn_out).start()

    @pl.when(phase == 2)
    def _():
        @pl.when(last)
        def _():
            passed(i).wait_recv()

        store(7, arrived, state_out).start()
        mix_states(pre.at[i], cum.at[i], age.at[0], arrived.at[i], near.at[i], gate.at[i], grad_gn.at[i], w_out_all,
                   norm_gate, spread, mixer.at[0], part.at[0], stats.at[0], step_x, gated_low)
        for k, (source, target) in enumerate(((normed, normed_out), (pre, pre_out), (dt_raw, dt_out), (cum, cum_out),
                                              (decay, decay_out), (gate, gate_out), (grad_gn, grad_gn_out),
                                              (arrived, state_out))):
            store(k, source, target).wait()

        @pl.when(jnp.logical_not(last))
        def _():
            passed(i).wait_send()


def add_over_cores(own, out, other, send, received):
    _, _, tensor = coordinates()
    partner = {"tensor": 1 - tensor}
    greet([(True, partner)])
    copies = Copies(send)
    copies.start(own, other, received.at[0], partner)
    copies.arrived(other, received.at[0])
    out[...] = own[...] + other[...]
    copies.finish()


def states_down(local, decay, grad_wz, grad_wo, part, arrived, out, other_part, stage, leaving, send, others, states,
                *buffers):
    place = _, _, tensor = coordinates()
    inner = grad_wz.shape[2]
    stage[:, :, :inner] = grad_wz[...]
    stage[:, :, inner:] = grad_wo[...]
    partner = {"tensor": 1 - tensor}
    greet(neighbours(place) + [(True, partner)])
    copies = Copies(send)
    copies.start(part, other_part.at[0], others.at[0], partner)
    in_turn(
        scatter_blocks(copies, place, stage, out, *buffers),
        chain_states(copies, place, local, decay, arrived, leaving, states, -1),
    )
    copies.arrived(other_part.at[0], others.at[0])
    copies.finish()


def last_sums(grad_w, grad_normed, grad_halo, conv_sums, norm_sums, head_sums, inner_sums,
              out, other_grad, own_tail, other_tail, conv_out, norm_out, head_out, inner_out,
              stage, half, small, seen, tails, send, others, *buffers):
    place = shard, context, tensor = coordinates()
    count = lax.axis_size("context")
    bc_width = 2 * LANES
    own_bc = bc_width // 2
    inner, model = inner_sums.shape[1], norm_sums.shape[1]
    partner = {"tensor": 1 - tensor}
    around = neighbours(place)
    cols = pl.ds(pl.multiple_of(tensor * own_bc, LANES), own_bc)
    other_cols = pl.ds(pl.multiple_of((1 - tensor) * own_bc, LANES), own_bc)
    small[0, :5] = conv_sums[:5]
    small[0, 5:6, :model] = norm_sums[:1]
    small[0, 5:6, model : model + LANES] = head_sums[:1]
    small[0, 5:6, model + LANES :] = head_sums[1:2]
    small[0, 6:8, :inner] = inner_sums[:2]
    small[0, 6:8, inner:] = jnp.zeros((2, small.shape[2] - inner), F32)
    below, above = (around[DOWN][0], around[UP][0])
    greet(around + [(True, partner), (True, {"context": context ^ 2}),
                    (above, {"context": context + 1, "tensor": 1 - tensor}),
                    (below, {"context": context - 1, "tensor": 1 - tensor})])
    copies = Copies(send)
    copies.start(small.at[0], seen.at[0], others.at[4], partner)
    copies.start(grad_w.at[:, :, other_cols], half, others.at[0], partner)
    copies.start(grad_normed, other_grad.at[0], others.at[1], partner)
    copies.start(grad_halo, own_tail, others.at[2], around[DOWN][1], below)
    copies.start(grad_halo, other_tail.at[0], others.at[3], {"context": context - 1, "tensor": 1 - tensor}, below)
    stage[:, :, own_bc:] = grad_w[:, :, bc_width:]
    copies.arrived(half, others.at[0])
    mixed = grad_w[:, :, cols].astype(F32) + half[...].astype(F32)
    stage[:, :, :own_bc] = mixed.astype(BF16)
    row = lax.broadcasted_iota(jnp.int32, small.shape[1:], 0)
    lane = lax.broadcasted_iota(jnp.int32, small.shape[1:], 1)
    shared = ((row < 5) & (lane < bc_width)) | ((row == 5) & (lane < model))
    copies.arrived(seen.at[0], others.at[4])
    small[1] = small[0] + jnp.where(shared, seen[0], 0.0)
    copies.start(small.at[1], seen.at[1], others.at[5], {"shard": shard ^ 1})
    for _ in scatter_blocks(copies, place, stage, out, *buffers):
        pass
    for step, device in ((1, {"shard": shard ^ 1}), (2, {"shard": shard ^ 2}), (3, {"context": context ^ 1}),
                         (4, {"context": context ^ 2})):
        if step > 1:
            copies.start(small.at[step], seen.at[step], others.at[4 + step], device)
        copies.arrived(seen.at[step], others.at[4 + step])
        small[step + 1] = small[step] + seen[step]
    total = small.at[5]
    conv_out[:, :own_bc] = total[:, cols]
    conv_out[:, own_bc:] = total[:, bc_width:]
    norm_out[...] = jnp.broadcast_to(total[5:6, :model], norm_out.shape)
    head_out[...] = jnp.zeros_like(head_out)
    head_out[0:1] = total[5:6, model : model + LANES]
    head_out[1:2] = total[5:6, model + LANES : model + 2 * LANES]
    inner_out[...] = jnp.zeros_like(inner_out)
    inner_out[0:2] = total[6:8, :inner]
    copies.arrived(other_grad.at[0], others.at[1])
    copies.arrived(own_tail, others.at[2], above)
    copies.arrived(other_tail.at[0], others.at[3], above)

    @pl.when(jnp.logical_not(above))
    def _():
        tails[...] = jnp.zeros_like(tails)
        for target, k in ((own_tail, 2), (other_tail.at[0], 3)):
            clear = pltpu.make_async_copy(tails, target, others.at[k])
            clear.start()
            clear.wait()

    copies.finish()


ANY = pl.BlockSpec(memory_space=pl.ANY)
IN_VMEM = pl.BlockSpec(memory_space=pltpu.VMEM)
DMA = pltpu.SemaphoreType.DMA


def call_between(kernel, collective_id, inputs, outputs, scratch):
    return pl.pallas_call(
        kernel,
        in_specs=[spec for _, spec in inputs],
        out_specs=[spec for _, spec in outputs],
        out_shape=[shape for shape, _ in outputs],
        scratch_shapes=scratch,
        compiler_params=pltpu.CompilerParams(
            collective_id=collective_id, has_side_effects=True, vmem_limit_bytes=VMEM_BYTES
        ),
        name=kernel.__name__,
    )(*[array for array, _ in inputs])


def gather_rows(rows):
    return lax.all_gather(rows, ("shard", "context"), axis=0, tiled=True)


def scatter_rows(rows):
    return lax.psum_scatter(rows.astype(F32), ("shard", "context"), scatter_dimension=0, tiled=True)


def passed_along(value, by):
    length = lax.axis_size("context")
    return lax.ppermute(value, "context", [(i, i + by) for i in range(length) if 0 <= i + by < length])


def chain(local, decay, by):
    arrived = jnp.zeros_like(local)
    for _ in range(lax.axis_size("context") - 1):
        leaving = decay[:, :1] * arrived.astype(F32) + local.astype(F32)
        arrived = passed_along(leaving.astype(BF16), by)
    return arrived


def exchange(value):
    everything = lax.all_gather(value, "tensor")
    return everything[0], everything[1:]


def part_of(width, at):
    return lambda array: pl.BlockSpec((array.shape[0], width), lambda i: (0, at))


class AnyMesh:
    def inputs(self, hid, w_bc, w_dt, w_x, conv_bc, conv_x):
        conv_bc_all = lax.all_gather(conv_bc, "tensor", axis=1, tiled=True)
        taps = jnp.pad(jnp.concatenate([conv_bc_all, conv_x], 1), ((0, 3), (0, 0)))
        w_bc_all = lax.all_gather(w_bc, "tensor", axis=1, tiled=True)
        w_dt_wide = jnp.pad(w_dt, ((0, 0), (0, LANES - w_dt.shape[1])))
        w_in = gather_rows(jnp.concatenate([w_bc_all, w_dt_wide, w_x], 1))
        return w_in, passed_along(hid[:, hid.shape[1] - HALO :], 1), taps

    def forward(self, hid, halo, age, seed, norm_in, w_in, w_z, w_out, taps, heads, spread, tri, norm_gate, skip):
        pieces, length, model = hid.shape
        inner, channels = w_z.shape[1], taps.shape[1]
        token = functools.partial(shaped, F32, pieces, length)
        token_low = functools.partial(shaped, BF16, pieces, length)
        normed, raw, pre, dt_raw, cum, local, decay = call(
            forward_local, pieces,
            [(hid, by_piece), (halo, by_piece), (age, by_piece), (norm_in, fixed), (w_in, fixed), (taps, fixed),
             (heads, fixed), (spread, fixed), (tri, fixed)],
            [(shaped(BF16, pieces, HALO + length, model), by_piece),
             (shaped(F32, pieces, HALO + length, channels), by_piece), (token(channels), by_piece),
             (token(LANES), by_piece), (token(LANES), by_piece), (shaped(BF16, pieces, LANES, inner), by_piece),
             (shaped(F32, pieces, 8, inner), by_piece)],
            [((length, channels), F32)], "forward_local",
        )
        state_in = chain(local, decay, 1)
        w_z_all, w_out_t = gather_rows(w_z), gather_rows(w_out.T)
        square = ((length, length), F32)
        token_wide = ((length, inner), F32)
        mixer, gate, grad_gn, part, stats = call(
            forward_mix, pieces,
            [(pre, by_piece), (dt_raw, by_piece), (cum, by_piece), (age, by_piece), (state_in, by_piece),
             (normed, by_piece), (seed, by_piece), (w_z_all, fixed), (w_out_t, fixed), (norm_gate, fixed),
             (skip, fixed), (heads, fixed), (spread, fixed)],
            [(token(inner), by_piece), (token(inner), by_piece), (token(inner), by_piece), (token_low(model), by_piece),
             (shaped(F32, pieces, 8, length), by_piece)],
            [token_wide, square, square, token_wide, token_wide, ((length, inner), BF16)], "forward_mix",
        )
        return normed, raw, pre, dt_raw, cum, decay, state_in, mixer, gate, grad_gn, part, stats, (w_z_all, fixed)

    def over_cores(self, stats):
        return lax.psum(stats, "tensor")

    def states_down(self, local, decay, grad_wz, grad_wo, part):
        sums = jnp.concatenate([scatter_rows(grad_wz), scatter_rows(grad_wo)], 1)
        return chain(local, decay, -1), sums, exchange(part)

    def last_sums(self, grad_w, grad_normed, grad_halo, conv_sums, norm_sums, head_sums, inner_sums, own_bc):
        mine, bc_width = lax.axis_index("tensor"), 2 * LANES
        grad_w = scatter_rows(grad_w)
        grad_w_bc = lax.psum_scatter(grad_w[:, :bc_width], "tensor", scatter_dimension=1, tiled=True)
        norm_sums, conv_bc = lax.psum((norm_sums, conv_sums[:, :bc_width]), ("shard", "context", "tensor"))
        conv_x, head_sums, inner_sums = lax.psum(
            (conv_sums[:, bc_width:], head_sums, inner_sums), ("shard", "context")
        )
        conv_bc = lax.dynamic_slice_in_dim(conv_bc, mine * own_bc, own_bc, 1)
        return (
            jnp.concatenate([grad_w_bc, grad_w[:, bc_width:]], 1),
            exchange(grad_normed),
            exchange(passed_along(grad_halo, -1)),
            (jnp.concatenate([conv_bc, conv_x], 1), norm_sums, head_sums, inner_sums),
        )


class FourByFourByTwo:
    def inputs(self, hid, w_bc, w_dt, w_x, conv_bc, conv_x):
        rows, inner = w_x.shape
        pieces, _, model = hid.shape
        blocks = model // rows
        in_width = 3 * LANES + inner
        w_in, halo, taps = call_between(
            gather_inputs, 1,
            [(w_bc, IN_VMEM), (w_dt, IN_VMEM), (w_x, IN_VMEM), (conv_bc, IN_VMEM), (conv_x, IN_VMEM), (hid, ANY)],
            [(shaped(BF16, blocks, rows, in_width), ANY), (shaped(BF16, pieces, HALO, model), ANY),
             (shaped(F32, 8, 2 * LANES + inner), IN_VMEM)],
            [pltpu.VMEM((rows, in_width), BF16), DMA((GATHER_COPIES,)), DMA((3,)), DMA((blocks,)), DMA((3,)), DMA],
        )
        return w_in.reshape(model, in_width), halo, taps

    def forward(self, hid, halo, age, seed, norm_in, w_in, w_z, w_out, taps, heads, spread, tri, norm_gate, skip):
        pieces, length, model = hid.shape
        rows, inner = w_z.shape
        channels = taps.shape[1]
        lead = HALO + length

        def at_phase(phase):
            def cut(array):
                rest = array.shape[1:]

                def where(p, i):
                    return (jnp.where(p == phase, i, jnp.where(p < phase, 0, pieces - 1)),) + (0,) * len(rest)

                return pl.BlockSpec((1,) + rest, where)

            return cut

        def always(array):
            return pl.BlockSpec((1,) + array.shape[1:], lambda p, i: (i,) + (0,) * (array.ndim - 1))

        def once(array):
            return pl.BlockSpec(array.shape, lambda p, i: (0,) * array.ndim, pipeline_mode=pl.Buffered(1))

        def anywhere(array):
            return ANY

        token = functools.partial(shaped, F32, pieces, length)
        state = shaped(BF16, pieces, LANES, inner)
        normed, pre, narrow = shaped(BF16, pieces, lead, model), token(channels), token(LANES)
        decay, both = shaped(F32, pieces, 8, inner), shaped(BF16, 16, rows, 2 * inner)
        inputs = [(hid, at_phase(0)), (halo, at_phase(0)), (age, always), (seed, at_phase(1)), (norm_in, once),
                  (w_in, once), (w_z, once), (w_out, once), (taps, once), (heads, once), (spread, once), (tri, once),
                  (norm_gate, once), (skip, once)]
        outputs = [(shaped(F32, pieces, lead, channels), at_phase(0)), (token(inner), at_phase(2)),
                   (shaped(BF16, pieces, length, model), at_phase(2)), (shaped(F32, pieces, 8, length), at_phase(2)),
                   (normed, anywhere), (pre, anywhere), (narrow, anywhere), (narrow, anywhere),
                   (token(inner), anywhere), (token(inner), anywhere), (state, anywhere), (decay, anywhere),
                   (both, anywhere)]
        kept = [normed, pre, narrow, narrow, token(inner), token(inner), token(inner), state, state, decay, both]
        raw, mixer, part, stats, normed, pre, dt_raw, cum, gate, grad_gn, state_in, decay, both = pl.pallas_call(
            forward,
            grid=(3, pieces),
            in_specs=[cut(array) for array, cut in inputs],
            out_specs=[cut(shape) for shape, cut in outputs],
            out_shape=[shape for shape, _ in outputs],
            scratch_shapes=[pltpu.VMEM(shape.shape, shape.dtype) for shape in kept]
            + [pltpu.VMEM((rows, 2 * inner), BF16), pltpu.VMEM((length, channels), F32),
               pltpu.VMEM((length, length), F32), pltpu.VMEM((length, length), F32), pltpu.VMEM((length, inner), F32),
               pltpu.VMEM((length, inner), BF16), DMA((GATHER_COPIES,)), DMA((16,)), DMA, DMA((2, pieces)),
               DMA((8, pieces))],
            compiler_params=pltpu.CompilerParams(
                collective_id=2, has_side_effects=True, vmem_limit_bytes=VMEM_BYTES
            ),
            name="forward",
        )(*[array for array, _ in inputs])
        w_z_all = (both.reshape(model, 2 * inner), part_of(inner, 0))
        return normed, raw, pre, dt_raw, cum, decay, state_in, mixer, gate, grad_gn, part, stats, w_z_all

    def over_cores(self, stats):
        return call_between(
            add_over_cores, 3, [(stats, IN_VMEM)], [(shaped(F32, *stats.shape), IN_VMEM)],
            [pltpu.VMEM(stats.shape, F32), DMA((1,)), DMA((1,))],
        )[0]

    def states_down(self, local, decay, grad_wz, grad_wo, part):
        model, inner = grad_wz.shape
        rows = model // 16
        pieces = local.shape[0]
        arrived, sums, other = call_between(
            states_down, 4,
            [(local, IN_VMEM), (decay, IN_VMEM), (grad_wz.reshape(16, rows, inner), IN_VMEM),
             (grad_wo.reshape(16, rows, inner), IN_VMEM), (part, ANY)],
            [(shaped(BF16, *local.shape), IN_VMEM), (shaped(F32, rows, 2 * inner), IN_VMEM),
             (shaped(BF16, 1, *part.shape), ANY)],
            [pltpu.VMEM((16, rows, 2 * inner), BF16), pltpu.VMEM(local.shape, BF16), DMA((SCATTER_COPIES,)), DMA((1,)),
             DMA((2, pieces))] + scatter_scratch(rows, 2 * inner),
        )
        return arrived, sums, (part, other)

    def last_sums(self, grad_w, grad_normed, grad_halo, conv_sums, norm_sums, head_sums, inner_sums, own_bc):
        model, in_width = grad_w.shape
        rows = model // 16
        width = in_width - own_bc
        channels = conv_sums.shape[1]
        out, other_grad, own_tail, other_tail, *small = call_between(
            last_sums, 5,
            [(grad_w.reshape(16, rows, in_width), IN_VMEM), (grad_normed, ANY), (grad_halo, ANY),
             (conv_sums, IN_VMEM), (norm_sums, IN_VMEM), (head_sums, IN_VMEM), (inner_sums, IN_VMEM)],
            [(shaped(F32, rows, width), IN_VMEM), (shaped(BF16, 1, *grad_normed.shape), ANY),
             (shaped(BF16, *grad_halo.shape), ANY), (shaped(BF16, 1, *grad_halo.shape), ANY),
             (shaped(F32, 8, channels - own_bc), IN_VMEM), (shaped(F32, 8, model), IN_VMEM),
             (shaped(F32, 8, LANES), IN_VMEM), (shaped(F32, *inner_sums.shape), IN_VMEM)],
            [pltpu.VMEM((16, rows, width), BF16), pltpu.VMEM((16, rows, own_bc), BF16),
             pltpu.VMEM((6, 8, channels), F32), pltpu.VMEM((5, 8, channels), F32), pltpu.VMEM(grad_halo.shape, BF16),
             DMA((SCATTER_COPIES + 9,)), DMA((9,))] + scatter_scratch(rows, width),
        )
        return out, (grad_normed, other_grad), (own_tail, other_tail), small


def links():
    sizes = tuple(lax.axis_size(axis) for axis in ("shard", "context", "tensor"))
    return FourByFourByTwo() if sizes == (4, 4, 2) else AnyMesh()


def shards(inner_all, hidden_in, out_grad, doc_start, norm_in, w_z, w_x, w_bc, w_dt, conv_x, conv_bc, dt_bias, a_log,
           skip_d, norm_gate, w_out):
    micro, per_device, length, model = hidden_in.shape
    pieces = micro * per_device
    inner = w_z.shape[1]
    head_count = w_dt.shape[1]
    bc_width = w_bc.shape[1] * lax.axis_size("tensor")
    channels = bc_width + inner
    in_width = channels + LANES
    lead = HALO + length
    offset = lax.axis_index("context") * length

    head_of = np.arange(inner) // HEAD
    gather = jnp.asarray(head_of[:, None] == np.arange(LANES)[None], BF16)
    spread = jnp.asarray(head_of[None] == np.arange(LANES)[:, None], BF16)
    tri = jnp.asarray(np.tril(np.ones((length, length))), BF16)
    tri_up = jnp.asarray(np.triu(np.ones((length, length))), BF16)

    def head_row(row):
        return jnp.pad(row, (0, LANES - head_count))

    heads = jnp.stack([head_row(dt_bias), head_row(a_log)] + [jnp.zeros((LANES,), F32)] * 6)
    skip = jnp.repeat(skip_d, HEAD)[None]
    norm_in, norm_gate = norm_in[None], norm_gate[None]
    hid = hidden_in.reshape(pieces, length, model)
    seed = out_grad.reshape(pieces, length, model)
    between = links()
    w_in, halo, taps = between.inputs(hid, w_bc, w_dt, w_x, conv_bc, conv_x)
    ages = (offset + jnp.arange(length, dtype=jnp.int32) - doc_start.reshape(pieces, length)).astype(F32)
    age = jnp.broadcast_to(ages[:, :, None], (pieces, length, LANES))
    age_row = jnp.broadcast_to(ages[:, None, :], (pieces, 8, length))

    token = functools.partial(shaped, F32, pieces, length)
    token_low = functools.partial(shaped, BF16, pieces, length)
    state = shaped(BF16, pieces, LANES, inner)
    normed, raw, pre, dt_raw, cum, decay, state_in, mixer, gate, grad_gn, part, stats, w_z_all = between.forward(
        hid, halo, age, seed, norm_in, w_in, w_z, w_out, taps, heads, spread, tri, norm_gate, skip
    )
    square = ((length, length), F32)
    token_wide = ((length, inner), F32)
    token_narrow = ((length, inner), BF16)

    stats = between.over_cores(stats)

    grad_fed, grad_mix, grad_gate, grad_cum, grad_bc, grad_state, grad_wz, grad_wo, sums = call(
        functools.partial(backward_local, inner_all), pieces,
        [(mixer, by_piece), (gate, by_piece), (grad_gn, by_piece), (stats, by_piece), (pre, by_piece),
         (dt_raw, by_piece), (cum, by_piece), (age, by_piece), (age_row, by_piece), (state_in, by_piece),
         (normed, by_piece), (seed, by_piece), (norm_gate, fixed), (skip, fixed), (heads, fixed), (spread, fixed),
         (gather, fixed)],
        [(token(inner), by_piece), (token_low(inner), by_piece), (token_low(inner), by_piece), (token(LANES), by_piece),
         (token(bc_width), by_piece), (state, by_piece), (shaped(BF16, model, inner), fixed),
         (shaped(BF16, model, inner), fixed), (shaped(F32, 8, inner), fixed)],
        [((model, inner), F32), ((model, inner), F32), ((length, LANES), F32), square, square, square, token_wide,
         token_wide, token_narrow, token_narrow], "backward_local",
    )

    grad_later, sums_zo, (own_part, other_part) = between.states_down(grad_state, decay, grad_wz, grad_wo, part)

    grad_normed, grad_halo, grad_w, conv_sums, head_sums, norm_sums = call(
        backward_finish, pieces,
        [(grad_later, by_piece), (state_in, by_piece), (pre, by_piece), (raw, by_piece), (dt_raw, by_piece),
         (cum, by_piece), (age, by_piece), (grad_fed, by_piece), (grad_mix, by_piece), (grad_cum, by_piece),
         (grad_bc, by_piece), (grad_gate, by_piece), (normed, by_piece), (hid, by_piece), (halo, by_piece),
         (w_in, fixed), w_z_all, (taps, fixed), (skip, fixed), (norm_in, fixed), (heads, fixed),
         (spread, fixed), (gather, fixed), (tri_up, fixed)],
        [(token_low(model), by_piece), (shaped(BF16, pieces, HALO, model), by_piece),
         (shaped(BF16, model, in_width), fixed), (shaped(F32, 8, channels), fixed), (shaped(F32, 8, LANES), fixed),
         (shaped(F32, 8, model), fixed)],
        [((model, in_width), F32), token_wide, token_wide, token_wide, token_narrow,
         ((lead + 8, channels), F32), ((lead + 8, LANES), F32), ((lead, in_width), BF16), ((lead, model), F32)],
        "backward_finish",
    )

    own_bc = w_bc.shape[1]
    sums_w, (own_grad, other_grad), (own_tail, other_tail), small = between.last_sums(
        grad_w, grad_normed, grad_halo, conv_sums, norm_sums, head_sums, sums, own_bc
    )
    rows = w_z.shape[0]
    outputs = [shaped(F32, rows, inner), shaped(F32, rows, inner), shaped(F32, rows, own_bc),
               shaped(F32, rows, head_count), shaped(F32, inner, rows), shaped(F32, 5, inner), shaped(F32, 5, own_bc),
               shaped(F32, 1, head_count), shaped(F32, 1, head_count), shaped(F32, 1, head_count),
               shaped(F32, 1, inner), shaped(F32, 1, model)]
    (out, in_grad, grad_wz, grad_wx, grad_wbc, grad_wdt, grad_wo, grad_conv_x, grad_conv_bc, grad_dt_bias, grad_a_log,
     grad_skip, grad_norm_gate, grad_norm_in) = call(
        functools.partial(finish, inner_all), pieces,
        [(hid, by_piece), (seed, by_piece), (stats, by_piece), (norm_in, fixed), (own_part, by_piece),
         (other_part, by_piece_second), (own_grad, by_piece), (other_grad, by_piece_second), (own_tail, by_piece),
         (other_tail, by_piece_second), (sums_zo, fixed), (sums_w, fixed)] + [(array, fixed) for array in small]
        + [(gather, fixed)],
        [(token_low(model), by_piece), (token_low(model), by_piece)] + [(shape, fixed) for shape in outputs],
        [((length, model), F32)], "finish",
    )
    return (
        out.reshape(hidden_in.shape),
        in_grad.reshape(hidden_in.shape),
        grad_norm_in[0],
        grad_wz,
        grad_wx,
        grad_wbc,
        grad_wdt,
        grad_conv_x,
        grad_conv_bc,
        grad_dt_bias[0],
        grad_a_log[0],
        grad_skip[0],
        grad_norm_gate[0],
        grad_wo,
    )


def solution(mesh):
    whole = P(None, "shard", "context", None)
    rows = P(("shard", "context"), "tensor")
    lanes = P(None, "tensor")
    heads = P("tensor")
    w_out = P("tensor", ("shard", "context"))
    inputs = (whole, whole, P(None, "shard", "context"), P(), rows, rows, rows, rows, lanes, lanes, heads, heads, heads, heads, w_out)
    outputs = (whole, whole, P(), rows, rows, rows, rows, lanes, lanes, heads, heads, heads, heads, w_out)

    def placed(*arrays):
        inner_all = arrays[4].shape[1]
        return jax.shard_map(
            functools.partial(shards, inner_all), mesh=mesh, in_specs=inputs, out_specs=outputs, check_vma=False
        )(*arrays)

    return placed
```

```python
import functools

import jax
import jax.numpy as jnp
import numpy as np
from jax import lax
from jax.experimental import pallas as pl
from jax.experimental.pallas import tpu as pltpu
from jax.sharding import PartitionSpec as P

EPSILON = 1e-05
F32, BF16 = jnp.float32, jnp.bfloat16
HEAD = 64
LANES = 128
HALO = 16
GONE = -1e30
VMEM_BYTES = 60 * 1024 * 1024


def mm(left, right):
    return jnp.dot(left, right, preferred_element_type=F32)


def mm_nt(left, right):
    return lax.dot_general(left, right, (((1,), (1,)), ((), ())), preferred_element_type=F32)


def mm_tn(left, right):
    return lax.dot_general(left, right, (((0,), (0,)), ((), ())), preferred_element_type=F32)


def parts_of(value, count):
    parts = []
    for _ in range(count - 1):
        parts.append(value.astype(BF16))
        value = value - parts[-1].astype(F32)
    return parts + [value.astype(BF16)]


def pick(value, ones, count=2):
    return sum(mm(part, ones) for part in parts_of(value, count))


def pick_left(ones, value, count=3):
    return sum(mm(ones, part) for part in parts_of(value, count))


def softplus(value):
    return jnp.maximum(value, 0.0) + jnp.log1p(jnp.exp(-jnp.abs(value)))


def sigmoid(value):
    return 1.0 / (1.0 + jnp.exp(-value))


def column_blocks(width):
    return [(at, min(LANES, width - at)) for at in range(0, width, LANES)]


def row_index(length):
    return lax.broadcasted_iota(jnp.int32, (length, LANES), 0).astype(F32)


def is_first_step():
    return pl.program_id(0) == 0


def is_last_step():
    return pl.program_id(0) == pl.num_programs(0) - 1


def half_masks(width):
    lane = lax.broadcasted_iota(jnp.int32, (1, width), 1)
    return [(lane // HEAD) == k for k in range(width // HEAD)]


def normalised(hidden, gain):
    scale = lax.rsqrt(jnp.mean(hidden * hidden, -1, keepdims=True) + EPSILON)
    return hidden * scale * gain, scale


def project(hid, halo, age, norm_in, w_in, taps, heads, spread, tri,
            normed, raw, pre, dt_raw, cum, local, decay, act):
    length, channels = hid.shape[0], taps.shape[1]
    bc_width = 2 * LANES
    normed[:HALO] = normalised(halo[...].astype(F32), norm_in[...])[0].astype(BF16)
    for at in range(0, length, 64):
        rows = normalised(hid[at : at + 64].astype(F32), norm_in[...])[0]
        normed[HALO + at : HALO + at + 64] = rows.astype(BF16)
    raw[:, :bc_width] = mm(normed[...], w_in[:, :bc_width])
    raw[:, bc_width:] = mm(normed[...], w_in[:, bc_width + LANES :])
    dt_raw[...] = mm(normed[HALO:], w_in[:, bc_width : bc_width + LANES])
    for at, width in column_blocks(channels):
        cols = slice(at, at + width)
        running = jnp.broadcast_to(taps[4:5, cols], (length, width))
        for lag in range(4):
            tapped = raw[HALO - lag : HALO - lag + length, cols]
            if lag:
                tapped = jnp.where(age[:, :width] >= lag, tapped, 0.0)
            running = running + taps[lag : lag + 1, cols] * tapped
        pre[:, cols] = running
        act[:, cols] = running * sigmoid(running)
    step = softplus(dt_raw[...] + heads[0:1])
    total = pick_left(tri[...], -jnp.exp(heads[1:2]) * step)
    cum[...] = total
    last, age_last = total[length - 1 :], age[length - 1 :]
    open_end = row_index(length) - (length - 1) + age_last >= 0
    weight = jnp.where(open_end, jnp.exp(last - total), 0.0) * step
    weighted = (act[:, bc_width:] * pick(weight, spread[...])).astype(BF16)
    local[...] = mm_tn(act[:, :LANES].astype(BF16), weighted).astype(BF16)
    kept = jnp.where(age_last > length - 1, jnp.exp(last), 0.0)
    decay[...] = pick(jnp.broadcast_to(kept, (8, LANES)), spread[...], 3)


def activated(pre):
    value = pre[...]
    return (value * sigmoid(value)).astype(BF16)


def mix_within(pre, dt_raw, cum, age, normed, out_grad, w_z, w_out_t, skip, heads, spread,
               near, gate, grad_gn, seg, pair, step_x):
    length, inner = near.shape
    bc_width = 2 * LANES
    gate[...] = mm(normed[HALO:], w_z())
    grad_gn[...] = mm(out_grad[...], w_out_t())
    pair[...] = mm_nt(activated(pre.at[:, LANES:bc_width]), activated(pre.at[:, :LANES]))
    row = lax.broadcasted_iota(jnp.int32, (length, length), 0)
    col = lax.broadcasted_iota(jnp.int32, (length, length), 1)
    back = (row - col).astype(F32)
    seg[...] = jnp.where((back >= 0) & (back <= age[:, :1]), 0.0, GONE)
    total = cum[...]
    total_t = total.T
    step_x[...] = pick(softplus(dt_raw[...] + heads[0:1]), spread[...])
    for at, width in column_blocks(inner):
        cols = slice(at, at + width)
        x_pre = pre[:, bc_width + at : bc_width + at + width]
        values = x_pre * sigmoid(x_pre)
        fed = (values * step_x[:, cols]).astype(BF16)
        masks = half_masks(width)
        near[:, cols] = skip[:, cols] * values
        for start in range(0, length, LANES):
            stop = start + LANES
            found = near[start:stop, cols]
            for k, mask in enumerate(masks):
                head = at // HEAD + k
                spread_log = total[start:stop, head : head + 1] - total_t[head : head + 1, :stop]
                mixing = pair[start:stop, :stop] * jnp.exp(spread_log + seg[start:stop, :stop])
                found = found + mm(mixing.astype(BF16), jnp.where(mask, fed[:stop], 0))
            near[start:stop, cols] = found


def mix_states(pre, cum, age, state_in, near, gate, grad_gn, w_out_t, norm_gate, spread,
               mixer, part, stats, carried, gated_low):
    length, inner = near.shape
    open_start = age[...] > row_index(length)
    carried[...] = pick(jnp.where(open_start, jnp.exp(cum[...]), 0.0), spread[...])
    carried[...] = carried[...] * mm(activated(pre.at[:, LANES : 2 * LANES]), state_in[...])
    squares = jnp.zeros((length, 1), F32)
    products = jnp.zeros((length, 1), F32)
    for at, width in column_blocks(inner):
        cols = slice(at, at + width)
        mixed = near[:, cols] + carried[:, cols]
        mixer[:, cols] = mixed
        raw_gate = gate[:, cols]
        gated = mixed * (raw_gate * sigmoid(raw_gate))
        weighted = gated * norm_gate[:, cols]
        gated_low[:, cols] = weighted.astype(BF16)
        squares = squares + jnp.sum(gated * gated, 1, keepdims=True)
        products = products + jnp.sum(grad_gn[:, cols] * weighted, 1, keepdims=True)
    part[...] = mm_nt(gated_low[...], w_out_t()).astype(BF16)
    lane = lax.broadcasted_iota(jnp.int32, (length, LANES), 1)
    columns = jnp.where(lane == 0, squares, jnp.where(lane == 1, products, 0.0))
    stats[...] = columns.T[:8]


def forward_local(hid, halo, age, norm_in, w_in, taps, heads, spread, tri,
                  normed, raw, pre, dt_raw, cum, local, decay, act):
    project(hid.at[0], halo.at[0], age.at[0], norm_in, w_in, taps, heads, spread, tri, normed.at[0], raw.at[0],
            pre.at[0], dt_raw.at[0], cum.at[0], local.at[0], decay.at[0], act)


def forward_mix(pre, dt_raw, cum, age, state_in, normed, out_grad, w_z, w_out_t, norm_gate, skip, heads, spread,
                mixer, gate, grad_gn, part, stats, near, seg, pair, carried, step_x, gated_low):
    w_z_all, w_out_all = (lambda: w_z[...]), (lambda: w_out_t[...])
    mix_within(pre.at[0], dt_raw.at[0], cum.at[0], age.at[0], normed.at[0], out_grad.at[0], w_z_all, w_out_all, skip,
               heads, spread, near, gate.at[0], grad_gn.at[0], seg, pair, step_x)
    mix_states(pre.at[0], cum.at[0], age.at[0], state_in.at[0], near, gate.at[0], grad_gn.at[0], w_out_all, norm_gate,
               spread, mixer.at[0], part.at[0], stats.at[0], carried, gated_low)


def gate_back(inner_all, mixer, gate, grad_gn, stats, pre, cum, age, state_in, normed, out_grad, norm_gate, skip,
              spread, gather, grad_mix, grad_gate, grad_cum, grad_c, grad_state, sums, sum_z, sum_o,
              carried, gated_low, from_state):
    length, inner = mixer.shape
    bc_width = 2 * LANES
    open_start = age[...] > row_index(length)
    carried[...] = pick(jnp.where(open_start, jnp.exp(cum[...]), 0.0), spread[...])
    means = stats[...].T / inner_all
    scale = lax.rsqrt(means[:, :1] + EPSILON)
    pull = scale * scale * scale * means[:, 1:2]
    rows_sum = jnp.zeros((length, LANES), F32)
    for at, width in column_blocks(inner):
        cols = slice(at, at + width)
        x_pre = pre[:, bc_width + at : bc_width + at + width]
        values = x_pre * sigmoid(x_pre)
        mixed = mixer[:, cols]
        raw_gate = gate[:, cols]
        logistic = sigmoid(raw_gate)
        acted = raw_gate * logistic
        gated = mixed * acted
        grad_out = grad_gn[:, cols]
        gated_scaled = gated * scale
        gated_low[:, cols] = (gated_scaled * norm_gate[:, cols]).astype(BF16)
        grad_gated = scale * (grad_out * norm_gate[:, cols]) - gated * pull
        grad_gate[:, cols] = (grad_gated * mixed * (logistic * (1.0 + raw_gate * (1.0 - logistic)))).astype(BF16)
        mix_low = (grad_gated * acted).astype(BF16)
        grad_mix[:, cols] = mix_low
        mix_wide = mix_low.astype(F32)
        sums[0:1, cols] += jnp.sum(grad_out * gated_scaled, 0, keepdims=True)
        sums[1:2, cols] += jnp.sum(mix_wide * values, 0, keepdims=True)
        rows_sum = rows_sum + pick(mix_wide * (mixed - skip[:, cols] * values), gather[cols])
        from_state[:, cols] = (carried[:, cols] * mix_wide).astype(BF16)
    grad_cum[...] = rows_sum
    grad_state[...] = mm_tn(activated(pre.at[:, LANES:bc_width]), from_state[...]).astype(BF16)
    grad_c[...] = mm_nt(from_state[...], state_in[...])
    sum_z[...] += mm_tn(normed[HALO:], grad_gate[...])
    sum_o[...] += mm_tn(out_grad[...], gated_low[...])


def within_back(pre, dt_raw, cum, age_row, grad_mix, heads, spread, gather, grad_fed, grad_cum, grad_bc,
                seg, pair, grad_pair, step_x):
    length, inner = grad_mix.shape
    bc_width = 2 * LANES
    readout, inputs_b = activated(pre.at[:, LANES:bc_width]), activated(pre.at[:, :LANES])
    pair[...] = mm_nt(inputs_b, readout)
    grad_pair[...] = jnp.zeros_like(grad_pair)
    row = lax.broadcasted_iota(jnp.int32, (length, length), 0)
    col = lax.broadcasted_iota(jnp.int32, (length, length), 1)
    back = (col - row).astype(F32)
    seg[...] = jnp.where((back >= 0) & (back <= age_row[:1]), 0.0, GONE)
    total = cum[...]
    total_t = total.T
    step_x[...] = pick(softplus(dt_raw[...] + heads[0:1]), spread[...])
    cols_sum = jnp.zeros((length, LANES), F32)
    for at, width in column_blocks(inner):
        cols = slice(at, at + width)
        x_pre = pre[:, bc_width + at : bc_width + at + width]
        fed = (x_pre * sigmoid(x_pre) * step_x[:, cols]).astype(BF16)
        mix_low = grad_mix[:, cols]
        masks = half_masks(width)
        for start in range(0, length, LANES):
            stop = start + LANES
            found = jnp.zeros((LANES, width), F32)
            for k, mask in enumerate(masks):
                head = at // HEAD + k
                spread_log = total_t[head : head + 1, start:] - total[start:stop, head : head + 1]
                decayed = jnp.exp(spread_log + seg[start:stop, start:])
                mixing = (pair[start:stop, start:] * decayed).astype(BF16)
                grad_mixing = mm_nt(jnp.where(mask, fed[start:stop], 0), mix_low[start:])
                grad_pair[start:stop, start:] += grad_mixing * decayed
                found = found + mm(mixing, jnp.where(mask, mix_low[start:], 0))
            grad_fed[start:stop, cols] = found
        cols_sum = cols_sum + pick(grad_fed[:, cols] * fed.astype(F32), gather[cols])
    grad_cum[...] -= cols_sum
    pair_low = grad_pair[...].astype(BF16)
    grad_bc[:, :LANES] = mm(pair_low, readout)
    grad_bc[:, LANES:] += mm_tn(pair_low, inputs_b)


def state_back(grad_later, state_in, pre, raw, dt_raw, cum, age, grad_fed, grad_mix, grad_cum, grad_bc, taps, skip,
               heads, spread, gather, tri_up, grad_in, conv_sums, head_sums,
               step_x, open_x, from_state, fed_state, slope, age_long):
    length, inner = grad_fed.shape
    channels = taps.shape[1]
    bc_width = 2 * LANES
    lead = HALO + length
    grad_in[:HALO, bc_width : bc_width + LANES] = jnp.zeros((HALO, LANES), BF16)
    age_long[HALO:lead] = age[...]
    total = cum[...]
    step_raw = dt_raw[...] + heads[0:1]
    step = softplus(step_raw)
    rate = -jnp.exp(heads[1:2])
    step_x[...] = pick(step, spread[...])
    last, age_last = total[length - 1 :], age[length - 1 :]
    open_end = row_index(length) - (length - 1) + age_last >= 0
    open_x[...] = pick(jnp.where(open_end, jnp.exp(last - total), 0.0), spread[...])
    from_state[...] = open_x[...] * mm(activated(pre.at[:, :LANES]), grad_later[...])
    state_sum = jnp.zeros((length, LANES), F32)
    step_sum = jnp.zeros((length, LANES), F32)
    for at, width in column_blocks(inner):
        cols = slice(at, at + width)
        x_pre = pre[:, bc_width + at : bc_width + at + width]
        logistic = sigmoid(x_pre)
        values = x_pre * logistic
        fed = values * step_x[:, cols]
        fed_state[:, cols] = (fed * open_x[:, cols]).astype(BF16)
        arrived = from_state[:, cols]
        grad = grad_fed[:, cols] + arrived
        state_sum = state_sum + pick(fed * arrived, gather[cols])
        step_sum = step_sum + pick(values * grad, gather[cols])
        grad_values = grad * step_x[:, cols] + skip[:, cols] * grad_mix[:, cols].astype(F32)
        slope[HALO:lead, bc_width + at : bc_width + at + width] = grad_values * (
            logistic * (1.0 + x_pre * (1.0 - logistic))
        )
    for at, extra in ((0, mm_nt(fed_state[...], grad_later[...])), (LANES, 0.0)):
        cols = slice(at, at + LANES)
        bc_pre = pre[:, cols]
        logistic = sigmoid(bc_pre)
        slope[HALO:lead, cols] = (grad_bc[:, cols] + extra) * (logistic * (1.0 + bc_pre * (1.0 - logistic)))
    kept = jnp.where(age_last > length - 1, jnp.exp(last), 0.0)
    met = jnp.sum(grad_later[...].astype(F32) * state_in[...].astype(F32), 0, keepdims=True)
    met = pick(jnp.broadcast_to(met, (8, inner)), gather[...], 3)[:1]
    end = met * kept + jnp.sum(state_sum, 0, keepdims=True)
    grad_a = pick_left(tri_up[...], grad_cum[...] - state_sum) + end
    head_sums[1:2] += jnp.sum(grad_a * rate * step, 0, keepdims=True)
    grad_step = (step_sum + grad_a * rate) * sigmoid(step_raw)
    head_sums[0:1] += jnp.sum(grad_step, 0, keepdims=True)
    grad_in[HALO:, bc_width : bc_width + LANES] = grad_step.astype(BF16)
    for at, width in column_blocks(channels):
        cols = slice(at, at + width)
        shifted = at if at < bc_width else at + LANES
        own = slope[HALO:lead, cols]
        total_in = taps[0:1, cols] * slope[:lead, cols]
        conv_sums[0:1, cols] += jnp.sum(own * raw[HALO:, cols], 0, keepdims=True)
        for lag in range(1, 4):
            kept_lag = jnp.where(age[:, :width] >= lag, own, 0.0)
            conv_sums[lag : lag + 1, cols] += jnp.sum(kept_lag * raw[HALO - lag : lead - lag, cols], 0, keepdims=True)
            later = jnp.where(age_long[lag : lead + lag, :width] >= lag, slope[lag : lead + lag, cols], 0.0)
            total_in = total_in + taps[lag : lag + 1, cols] * later
        conv_sums[4:5, cols] += jnp.sum(own, 0, keepdims=True)
        grad_in[:, shifted : shifted + width] = total_in.astype(BF16)


def clear_margins(slope, age_long, length):
    slope[:HALO] = jnp.zeros((HALO, slope.shape[1]), F32)
    slope[HALO + length :] = jnp.zeros((8, slope.shape[1]), F32)
    age_long[:HALO] = jnp.zeros((HALO, LANES), F32)
    age_long[HALO + length :] = jnp.zeros((8, LANES), F32)


def features_back(grad_in, grad_gate, hid, halo, w_in, w_z, grad_normed, grad_halo, norm_sums, wide):
    length = hid.shape[0]
    wide[...] = mm_nt(grad_in[...], w_in[...])
    wide[HALO:] += mm_nt(grad_gate[...], w_z[...])
    hidden = halo[...].astype(F32)
    scale = normalised(hidden, 1.0)[1]
    norm_sums[0:1] += jnp.sum(wide[:HALO] * hidden * scale, 0, keepdims=True)
    for at in range(0, length, 64):
        hidden = hid[at : at + 64].astype(F32)
        scale = normalised(hidden, 1.0)[1]
        norm_sums[0:1] += jnp.sum(wide[HALO + at : HALO + at + 64] * hidden * scale, 0, keepdims=True)
    grad_halo[...] = wide[:HALO].astype(BF16)
    grad_normed[...] = wide[HALO:].astype(BF16)


def backward_local(inner_all, mixer, gate, grad_gn, stats, pre, dt_raw, cum, age, age_row, state_in, normed, out_grad,
                   norm_gate, skip, heads, spread, gather,
                   grad_fed, grad_mix, grad_gate, grad_cum, grad_bc, grad_state, grad_wz, grad_wo, sums,
                   sum_z, sum_o, seg, pair, grad_pair, carried, step_x, gated_low, from_state):
    @pl.when(is_first_step())
    def _():
        sum_z[...] = jnp.zeros_like(sum_z)
        sum_o[...] = jnp.zeros_like(sum_o)
        sums[...] = jnp.zeros_like(sums)

    gate_back(inner_all, mixer.at[0], gate.at[0], grad_gn.at[0], stats.at[0], pre.at[0], cum.at[0], age.at[0],
              state_in.at[0], normed.at[0], out_grad.at[0], norm_gate, skip, spread, gather, grad_mix.at[0],
              grad_gate.at[0], grad_cum.at[0], grad_bc.at[0, :, LANES:], grad_state.at[0], sums, sum_z, sum_o,
              carried, gated_low, from_state)
    within_back(pre.at[0], dt_raw.at[0], cum.at[0], age_row.at[0], grad_mix.at[0], heads, spread, gather,
                grad_fed.at[0], grad_cum.at[0], grad_bc.at[0], seg, pair, grad_pair, step_x)

    @pl.when(is_last_step())
    def _():
        grad_wz[...] = sum_z[...].astype(BF16)
        grad_wo[...] = sum_o[...].astype(BF16)


def backward_finish(grad_later, state_in, pre, raw, dt_raw, cum, age, grad_fed, grad_mix, grad_cum, grad_bc, grad_gate,
                    normed, hid, halo, w_in, w_z, taps, skip, heads, spread, gather, tri_up,
                    grad_normed, grad_halo, grad_w, conv_sums, head_sums, norm_sums,
                    sum_w, step_x, open_x, from_state, fed_state, slope, age_long, grad_in, wide):
    @pl.when(is_first_step())
    def _():
        for sums in (sum_w, conv_sums, head_sums, norm_sums):
            sums[...] = jnp.zeros_like(sums)
        clear_margins(slope, age_long, hid.shape[1])

    state_back(grad_later.at[0], state_in.at[0], pre.at[0], raw.at[0], dt_raw.at[0], cum.at[0], age.at[0],
               grad_fed.at[0], grad_mix.at[0], grad_cum.at[0], grad_bc.at[0], taps, skip, heads, spread, gather, tri_up,
               grad_in, conv_sums, head_sums, step_x, open_x, from_state, fed_state, slope, age_long)
    features_back(grad_in, grad_gate.at[0], hid.at[0], halo.at[0], w_in, w_z, grad_normed.at[0], grad_halo.at[0],
                  norm_sums, wide)
    sum_w[...] += mm_tn(normed[0], grad_in[...])

    @pl.when(is_last_step())
    def _():
        grad_w[...] = sum_w[...].astype(BF16)


def finish(inner_all, hid, out_grad, stats, norm_in, own_part, other_part, own_grad, other_grad, own_tail, other_tail,
           sums_zo, sums_w, conv_sums, norm_sums, head_sums, inner_sums, gather,
           out, in_grad, grad_wz, grad_wx, grad_wbc, grad_wdt, grad_wo, grad_conv_x, grad_conv_bc, grad_dt_bias,
           grad_a_log, grad_skip, grad_norm_gate, grad_norm_in, total):
    length = hid.shape[1]

    def added(own, others, rows):
        found = own[0, rows].astype(F32)
        for k in range(others.shape[0]):
            found = found + others[k, 0, rows].astype(F32)
        return found

    everything = slice(None)
    total[...] = added(own_grad, other_grad, everything)
    total[length - HALO :] += added(own_tail, other_tail, everything)
    scales = lax.rsqrt(stats[0].T[:, :1] / inner_all + EPSILON)
    for at in range(0, length, 64):
        rows = slice(at, at + 64)
        hidden = hid[0, rows].astype(F32)
        out[0, rows] = (hidden + scales[rows] * added(own_part, other_part, rows)).astype(BF16)
        scale = normalised(hidden, 1.0)[1]
        weighted = total[rows] * norm_in[...]
        inner_mean = jnp.mean(weighted * hidden, -1, keepdims=True)
        in_grad[0, rows] = (
            out_grad[0, rows].astype(F32) + scale * weighted - hidden * (scale * scale * scale * inner_mean)
        ).astype(BF16)

    @pl.when(is_last_step())
    def _():
        inner, own_bc, head_count = grad_wz.shape[1], grad_wbc.shape[1], grad_wdt.shape[1]
        grad_wz[...] = sums_zo[:, :inner]
        grad_wo[...] = sums_zo[:, inner:].T
        grad_wbc[...] = sums_w[:, :own_bc]
        grad_wdt[...] = sums_w[:, own_bc : own_bc + head_count]
        grad_wx[...] = sums_w[:, own_bc + LANES :]
        grad_conv_bc[...] = conv_sums[:5, :own_bc]
        grad_conv_x[...] = conv_sums[:5, own_bc:]
        grad_dt_bias[...] = head_sums[0:1, :head_count]
        grad_a_log[...] = head_sums[1:2, :head_count]
        grad_norm_in[...] = norm_sums[0:1]
        grad_norm_gate[...] = inner_sums[0:1]
        grad_skip[...] = pick(inner_sums[...], gather[...], 3)[1:2, :head_count]


def by_piece(array):
    rest = array.shape[1:]
    return pl.BlockSpec((1,) + rest, lambda i: (i,) + (0,) * len(rest))


def by_piece_second(array):
    rest = array.shape[2:]
    return pl.BlockSpec((array.shape[0], 1) + rest, lambda i: (0, i) + (0,) * len(rest))


def fixed(array):
    return pl.BlockSpec(array.shape, lambda i: (0,) * len(array.shape))


def call(kernel, pieces, inputs, outputs, scratch, name):
    return pl.pallas_call(
        kernel,
        grid=(pieces,),
        in_specs=[cut(array) for array, cut in inputs],
        out_specs=[cut(shape) for shape, cut in outputs],
        out_shape=[shape for shape, _ in outputs],
        scratch_shapes=[pltpu.VMEM(shape, kind) for shape, kind in scratch],
        compiler_params=pltpu.CompilerParams(vmem_limit_bytes=VMEM_BYTES),
        name=name,
    )(*[array for array, _ in inputs])


def shaped(kind, *dims):
    return jax.ShapeDtypeStruct(dims, kind)


MESH = pl.DeviceIdType.MESH
UP, DOWN, NEXT_X, NEXT_Y = range(4)


def coordinates():
    return lax.axis_index("shard"), lax.axis_index("context"), lax.axis_index("tensor")


def greet(partners):
    barrier = pltpu.get_barrier_semaphore()
    count = 0
    for there, device in partners:
        if there is True:
            pl.semaphore_signal(barrier, inc=1, device_id=device, device_id_type=MESH)
            count = count + 1
        else:
            pl.when(there)(
                functools.partial(pl.semaphore_signal, barrier, inc=1, device_id=device, device_id_type=MESH)
            )
            count = count + there.astype(jnp.int32)
    pl.semaphore_wait(barrier, count)


class Copies:
    def __init__(self, send):
        self.send, self.used, self.started = send, 0, []

    def make(self, source, target, received, device, send=0):
        return pltpu.make_async_remote_copy(
            src_ref=source, dst_ref=target, send_sem=self.send.at[send], recv_sem=received,
            device_id=device, device_id_type=MESH,
        )

    def start(self, source, target, received, device, there=True):
        copy = self.make(source, target, received, device, self.used)
        self.used += 1
        self.started.append((there, copy))
        if there is True:
            copy.start()
        else:
            pl.when(there)(copy.start)

    def arrived(self, target, received, there=True):
        copy = self.make(target, target, received, {"tensor": 1 - lax.axis_index("tensor")})
        if there is True:
            copy.wait_recv()
        else:
            pl.when(there)(copy.wait_recv)

    def finish(self):
        for there, copy in self.started:
            if there is True:
                copy.wait_send()
            else:
                pl.when(there)(copy.wait_send)


def neighbours(place):
    shard, context, _ = place
    count = lax.axis_size("context")
    return [
        (context + 1 < count, {"context": context + 1}),
        (context > 0, {"context": context - 1}),
        (True, {"shard": shard ^ 1}),
        (True, {"shard": shard ^ 2}),
    ]


def gather_step(step, start, arrived, stage, out, received):
    place = shard, context, _ = coordinates()
    count = lax.axis_size("context")
    up, down, next_x, next_y = neighbours(place)
    mine, beside_x, beside_y, across = [(shard ^ k) * count for k in (0, 1, 2, 3)]

    def pass_on(number, source, slot, to, there=True):
        if to[0] is not True:
            there = to[0] if there is True else there & to[0]
        start(number, source, out.at[slot], received.at[slot], to[1], there)

    def both_ways(distance):
        found = [(context - distance, context >= distance, up),
                 (context + distance, context + distance < count, down)]
        return [(jnp.clip(at, 0, count - 1), there, to) for at, there, to in found[: 2 if distance else 1]]

    if step == 0:
        for k, to in enumerate((up, down, next_x, next_y)):
            pass_on(k, stage, mine + context, to)
    elif step < count:
        for k, (at, there, to) in enumerate(both_ways(step)):
            slot = mine + at
            arrived(out.at[slot], received.at[slot], there)
            for m, target in enumerate((to, next_x, next_y)):
                pass_on(4 + (step - 1) * 6 + k * 3 + m, out.at[slot], slot, target, there)
    elif step < 2 * count:
        for k, (at, there, _) in enumerate(both_ways(step - count)):
            number = 4 + (count - 1) * 6 + (step - count) * 4 + k * 2
            slot_x, slot_y = beside_x + at, beside_y + at
            arrived(out.at[slot_x], received.at[slot_x], there)
            pass_on(number, out.at[slot_x], slot_x, next_y, there & (at < count // 2))
            arrived(out.at[slot_y], received.at[slot_y], there)
            pass_on(number + 1, out.at[slot_y], slot_y, next_x, there & (at >= count // 2))
    else:
        for at in range(count):
            arrived(out.at[across + at], received.at[across + at], True)


def gather_steps():
    return 2 * lax.axis_size("context") + 1


GATHER_COPIES = 40


class Numbered:
    def __init__(self, send):
        self.send = send

    def copy(self, number, source, target, received, device):
        return pltpu.make_async_remote_copy(
            src_ref=source, dst_ref=target, send_sem=self.send.at[number], recv_sem=received,
            device_id=device, device_id_type=MESH,
        )

    def when(self, there, action):
        if there is True:
            action()
        else:
            pl.when(there)(action)

    def start(self, number, source, target, received, device, there=True):
        self.when(there, self.copy(number, source, target, received, device).start)

    def sent(self, number, source, target, received, device, there=True):
        self.when(there, self.copy(number, source, target, received, device).wait_send)

    def arrived(self, target, received, there=True):
        other = {"tensor": 1 - lax.axis_index("tensor")}
        self.when(there, self.copy(0, target, target, received, other).wait_recv)

    def nothing(self, *_):
        pass


def scatter_scratch(rows, width):
    return [pltpu.VMEM((4, rows, width), BF16) for _ in range(5)] + [DMA((5, 4)), DMA((SCATTER_COPIES,))]


SCATTER_COPIES = 18


def scatter_steps():
    return 1 + lax.axis_size("context") // 2 + lax.axis_size("context")


def scatter_step(step, start, arrived, blocks, out, first, from_x, from_y, from_up, from_down, received, add=True):
    shard, context, _ = coordinates()
    count = lax.axis_size("context")
    half = count // 2
    up, down, next_x, next_y = neighbours(coordinates())
    mine, beside_x, beside_y, across = [(shard ^ k) * count for k in (0, 1, 2, 3)]
    if step == 0:
        for k in range(count):
            start(k, blocks.at[across + k], first.at[k], received.at[0, k], (next_y if k < half else next_x)[1], True)
        for k in range(count):
            beside, target, row, to = (beside_y, from_y, 2, next_y) if k < half else (beside_x, from_x, 1, next_x)
            start(count + k, blocks.at[beside + k], target.at[k], received.at[row, k], to[1], True)
    elif step <= half:
        for k in (step - 1, count - step):
            beside, target, row, to = (beside_x, from_x, 1, next_x) if k < half else (beside_y, from_y, 2, next_y)
            arrived(first.at[k], received.at[0, k], True)
            if add:
                blocks[beside + k] = (blocks[beside + k].astype(F32) + first[k].astype(F32)).astype(BF16)
            start(2 * count + k, blocks.at[beside + k], target.at[k], received.at[row, k], to[1], True)
    else:
        at = step - half - 1

        def column(k, extra, row, there):
            arrived(from_x.at[k], received.at[1, k], True)
            arrived(from_y.at[k], received.at[2, k], True)
            found = blocks[mine + k].astype(F32) + from_x[k].astype(F32) + from_y[k].astype(F32)
            out[...] = found

            @pl.when(there)
            def _():
                arrived(extra.at[k], received.at[row, k], True)
                out[...] += extra[k].astype(F32)

        if at < count - 1:
            for k, sends, receives, to, row, extra, number in (
                (count - 1 - at, context < count - 1 - at, context > 0, up, 3, from_down, 0),
                (at, context > at, context < count - 1, down, 4, from_up, 1),
            ):
                if add:

                    @pl.when(sends)
                    def _(k=k, receives=receives, row=row, extra=extra):
                        column(k, extra, row, receives)
                        blocks[mine + k] = out[...].astype(BF16)

                start(3 * count + 2 * at + number, blocks.at[mine + k], extra.at[k], received.at[row, k], to[1], sends)
        else:
            column(context, from_down, 3, context > 0)

            @pl.when(context < count - 1)
            def _():
                arrived(from_up.at[context], received.at[4, context], True)
                out[...] += from_up[context].astype(F32)


def gather_inputs(w_bc, w_dt, w_x, conv_bc, conv_x, hid, out, halo, taps, stage, passing, send, received, others, own):
    place = shard, context, tensor = coordinates()
    length = hid.shape[1]
    own_bc, head_count = w_bc.shape[1], w_dt.shape[1]
    bc_width = 2 * LANES
    partner = {"tensor": 1 - tensor}
    around = neighbours(place)
    stage[:, bc_width : bc_width + LANES] = jnp.zeros((stage.shape[0], LANES), BF16)
    stage[:, bc_width : bc_width + head_count] = w_dt[...]
    stage[:, bc_width + LANES :] = w_x[...]
    cols = pl.ds(pl.multiple_of(tensor * own_bc, LANES), own_bc)
    other_cols = pl.ds(pl.multiple_of((1 - tensor) * own_bc, LANES), own_bc)
    stage[:, cols] = w_bc[...]
    taps[...] = jnp.zeros_like(taps)
    taps[:5, cols] = conv_bc[...]
    taps[:5, bc_width:] = conv_x[...]
    greet(around + [(True, partner)])
    copies = Copies(send)
    copies.start(stage.at[:, cols], stage.at[:, cols], others.at[0], partner)
    copies.start(taps.at[:, cols], taps.at[:, cols], others.at[1], partner)
    tail = pl.ds(length - HALO, HALO)
    copies.start(hid.at[:, tail], halo, others.at[2], around[UP][1], around[UP][0])
    copies.arrived(stage.at[:, other_cols], others.at[0])
    numbered = Numbered(passing)
    local = pltpu.make_async_copy(stage, out.at[shard * lax.axis_size("context") + context], own)
    local.start()
    for step in range(gather_steps()):
        gather_step(step, numbered.start, numbered.arrived, stage, out, received)
    for step in range(gather_steps()):
        gather_step(step, numbered.sent, numbered.nothing, stage, out, received)
    local.wait()
    copies.arrived(taps.at[:, other_cols], others.at[1])
    copies.arrived(halo, others.at[2], context > 0)

    @pl.when(context == 0)
    def _():
        clear = pltpu.make_async_copy(hid.at[:, tail], halo, others.at[2])
        clear.start()
        clear.wait()

    copies.finish()


GATHER_TURNS = (0, 1, 2, 3, 3, 4, 5, 6, 7)


def forward(hid, halo, age, out_grad, norm_in, w_in, w_z, w_out, taps, heads, spread, tri, norm_gate, skip,
            raw, mixer, part, stats, normed_out, pre_out, dt_out, cum_out, gate_out, grad_gn_out, state_out, decay_out,
            both_out,
            normed, pre, dt_raw, cum, gate, grad_gn, near, leaving, arrived, decay, both, stage, act, seg, pair, step_x,
            gated_low, send, received, own, states, stores):
    place = shard, context, _ = coordinates()
    phase, i = pl.program_id(0), pl.program_id(1)
    pieces = pl.num_programs(1)
    inner = w_z.shape[1]
    count = lax.axis_size("context")
    numbered = Numbered(send)

    def store(k, source, target):
        return pltpu.make_async_copy(source.at[i], target.at[i], stores.at[k, i])

    first, last = context == 0, context == count - 1

    def passed(c):
        return pltpu.make_async_remote_copy(
            src_ref=leaving.at[c], dst_ref=arrived.at[c], send_sem=states.at[1, c], recv_sem=states.at[0, c],
            device_id={"context": context + 1}, device_id_type=MESH,
        )

    @pl.when((phase == 0) & (i == 0))
    def _():
        stage[:, :inner] = w_z[...]
        stage[:, inner:] = w_out[...].astype(F32).T.astype(BF16)
        greet(neighbours(place))
        gather_step(0, numbered.start, numbered.arrived, stage, both, received)
        pltpu.make_async_copy(stage, both.at[shard * count + context], own).start()

    turn = phase * pieces + i
    c = jnp.clip(turn // 2 - context, 0, pieces - 1)

    @pl.when((turn % 2 == 0) & (turn // 2 >= context) & (turn // 2 - context < pieces) & jnp.logical_not(first | last))
    def _():
        passed(c).wait_recv()
        leaving[c] = (decay[c, :1] * arrived[c].astype(F32) + leaving[c].astype(F32)).astype(BF16)
        passed(c).start()

    @pl.when(phase == 0)
    def _():
        project(hid.at[0], halo.at[0], age.at[0], norm_in, w_in, taps, heads, spread, tri, normed.at[i], raw.at[0],
                pre.at[i], dt_raw.at[i], cum.at[i], leaving.at[i], decay.at[i], act)
        for k, (source, target) in enumerate(((normed, normed_out), (pre, pre_out), (dt_raw, dt_out), (cum, cum_out),
                                              (decay, decay_out))):
            store(k, source, target).start()

        @pl.when(first)
        def _():
            arrived[i] = jnp.zeros(arrived.shape[1:], BF16)
            passed(i).start()

    for step in range(1, gather_steps()):

        @pl.when((phase == 0) & (i == GATHER_TURNS[step]))
        def _(step=step):
            gather_step(step, numbered.start, numbered.arrived, stage, both, received)

    @pl.when((phase == 0) & (i == pieces - 1))
    def _():
        for step in range(gather_steps()):
            gather_step(step, numbered.sent, numbered.nothing, stage, both, received)
        pltpu.make_async_copy(stage, both.at[shard * count + context], own).wait()
        pltpu.make_async_copy(both, both_out, own).start()

    @pl.when((phase == 1) & (i == pieces - 1))
    def _():
        pltpu.make_async_copy(both, both_out, own).wait()

    def w_z_all():
        return both[:, :, :inner].reshape(-1, inner)

    def w_out_all():
        return both[:, :, inner:].reshape(-1, inner)

    @pl.when(phase == 1)
    def _():
        mix_within(pre.at[i], dt_raw.at[i], cum.at[i], age.at[0], normed.at[i], out_grad.at[0], w_z_all, w_out_all, skip,
                   heads, spread, near.at[i], gate.at[i], grad_gn.at[i], seg, pair, step_x)
        store(5, gate, gate_out).start()
        store(6, grad_gn, grad_gn_out).start()

    @pl.when(phase == 2)
    def _():
        @pl.when(last)
        def _():
            passed(i).wait_recv()

        store(7, arrived, state_out).start()
        mix_states(pre.at[i], cum.at[i], age.at[0], arrived.at[i], near.at[i], gate.at[i], grad_gn.at[i], w_out_all,
                   norm_gate, spread, mixer.at[0], part.at[0], stats.at[0], step_x, gated_low)
        for k, (source, target) in enumerate(((normed, normed_out), (pre, pre_out), (dt_raw, dt_out), (cum, cum_out),
                                              (decay, decay_out), (gate, gate_out), (grad_gn, grad_gn_out),
                                              (arrived, state_out))):
            store(k, source, target).wait()

        @pl.when(jnp.logical_not(last))
        def _():
            passed(i).wait_send()


OUTER_TURNS = (7, 9, 10, 12, 14, 16, 18)


def backward(inner_all, mixer, gate, grad_gn, pre, dt_raw, cum, age, age_row, state_in, normed, out_grad, raw, hid, halo,
             stats, decay, norm_gate, skip, heads, spread, gather, tri_up, taps, w_in, w_z, part,
             stats_out, sums_zo, sums_w, conv_out, norm_out, head_out, inner_out, other_part, own_grad, other_grad,
             own_tail, other_tail,
             grad_mix, grad_gate, grad_cum, grad_bc, grad_fed, sum_all, grad_in, stage, half_out, half_in,
             leaving, arrived, carried, step_x, low_a, low_b, slope, age_long, wide, seg, pair, grad_pair, tails, blank,
             stats_in, small, seen, conv_sums, head_sums, norm_sums, inner_sums,
             send, got, grad_send, grad_got, states, stores, *buffers):
    outer, last_ones = buffers[:7], buffers[7:]
    shard, context, tensor = coordinates()
    phase, i = pl.program_id(0), pl.program_id(1)
    pieces = pl.num_programs(1)
    count = lax.axis_size("context")
    model, inner = sum_all.shape[0], grad_mix.shape[2]
    in_width, channels = w_in.shape[1], taps.shape[1]
    length = grad_mix.shape[1]
    bc_width = 2 * LANES
    own_bc = bc_width // 2
    partner = {"tensor": 1 - tensor}
    below, above = context > 0, context < count - 1
    below_partner = {"context": context - 1, "tensor": 1 - tensor}
    turn = phase * pieces + i
    misc = Numbered(send)
    rows = stage.shape[1]
    cols = pl.ds(pl.multiple_of(tensor * own_bc, LANES), own_bc)
    other_cols = pl.ds(pl.multiple_of((1 - tensor) * own_bc, LANES), own_bc)

    def link(number, source, target, device):
        return misc.copy(number, source, target, got.at[number], device)

    def stats_link():
        return link(0, stats, stats_in, partner)

    def part_link():
        return link(1, part, other_part.at[0], partner)

    def half_link():
        return link(2, half_out, half_in, partner)

    def tail_links():
        return [link(3, tails, own_tail, {"context": context - 1}), link(4, tails, other_tail.at[0], below_partner)]

    def small_link(k):
        to = [partner, {"shard": shard ^ 1}, {"shard": shard ^ 2}, {"context": context ^ 1}, {"context": context ^ 2}]
        return link(5 + k, small.at[k], seen.at[k], to[k])

    def grad_link(k):
        return pltpu.make_async_remote_copy(
            src_ref=grad_gate.at[k], dst_ref=other_grad.at[0, k], send_sem=grad_send.at[k], recv_sem=grad_got.at[k],
            device_id=partner, device_id_type=MESH,
        )

    def grad_store(k):
        return pltpu.make_async_copy(grad_gate.at[k], own_grad.at[k], stores.at[k])

    def passed(c):
        return pltpu.make_async_remote_copy(
            src_ref=leaving.at[c], dst_ref=arrived.at[c], send_sem=states.at[1, c], recv_sem=states.at[0, c],
            device_id={"context": context - 1}, device_id_type=MESH,
        )

    first, last = context == count - 1, context == 0
    hops = count - 1 - context

    @pl.when(turn == 0)
    def _():
        for sums in (sum_all, conv_sums, head_sums, norm_sums, inner_sums):
            sums[...] = jnp.zeros_like(sums)
        clear_margins(slope, age_long, length)
        greet(neighbours(coordinates()) + [(True, partner), (True, {"context": context ^ 2}),
              (above, {"context": context + 1, "tensor": 1 - tensor}), (below, below_partner)])
        stats_link().start()
        part_link().start()
        stats_link().wait_recv()
        stats_out[...] = stats[...] + stats_in[...]

    c = jnp.clip(turn // 2 - hops, 0, pieces - 1)

    @pl.when((turn % 2 == 0) & (turn // 2 >= hops) & (turn // 2 - hops < pieces) & jnp.logical_not(first | last))
    def _():
        passed(c).wait_recv()
        leaving[c] = (decay[c, :1] * arrived[c].astype(F32) + leaving[c].astype(F32)).astype(BF16)
        passed(c).start()

    @pl.when(phase == 0)
    def _():
        gate_back(inner_all, mixer.at[0], gate.at[0], grad_gn.at[0], stats_out.at[i], pre.at[0], cum.at[0], age.at[0],
                  state_in.at[0], normed.at[0], out_grad.at[0], norm_gate, skip, spread, gather, grad_mix.at[i],
                  grad_gate.at[i], grad_cum.at[i], grad_bc.at[i, :, LANES:], leaving.at[i], inner_sums,
                  sum_all.at[:, :inner], sum_all.at[:, inner:], carried, low_a, low_b)

        @pl.when(first)
        def _():
            arrived[i] = jnp.zeros(arrived.shape[1:], BF16)
            passed(i).start()

    @pl.when(turn == pieces - 1)
    def _():
        stage[...] = sum_all[...].reshape(stage.shape).astype(BF16)

    outer_links = Numbered(outer[6])
    for step in range(scatter_steps()):

        @pl.when(turn == OUTER_TURNS[step])
        def _(step=step):
            scatter_step(step, outer_links.start, outer_links.arrived, stage, sums_zo, *outer[:6])

    @pl.when(turn == OUTER_TURNS[-1] + 1)
    def _():
        for step in range(scatter_steps() - 1):
            scatter_step(step, outer_links.sent, outer_links.nothing, stage, sums_zo, *outer[:6], add=False)

    @pl.when(phase == 1)
    def _():
        within_back(pre.at[0], dt_raw.at[0], cum.at[0], age_row.at[0], grad_mix.at[i], heads, spread, gather,
                    grad_fed.at[i], grad_cum.at[i], grad_bc.at[i], seg, pair, grad_pair, step_x)

    @pl.when(phase == 2)
    def _():
        @pl.when(i == 0)
        def _():
            sum_all[...] = jnp.zeros_like(sum_all)

        @pl.when(last)
        def _():
            passed(i).wait_recv()

        state_back(arrived.at[i], state_in.at[0], pre.at[0], raw.at[0], dt_raw.at[0], cum.at[0], age.at[0],
                   grad_fed.at[i], grad_mix.at[i], grad_cum.at[i], grad_bc.at[i], taps, skip, heads, spread, gather,
                   tri_up, grad_in.at[i], conv_sums, head_sums, step_x, carried, wide.at[HALO:], low_a, slope,
                   age_long)
        sum_all[:, :in_width] += mm_tn(normed[0], grad_in[i])

        @pl.when(jnp.logical_not(last))
        def _():
            passed(i).wait_send()

    last_stage = stage.at[:, :, : in_width - own_bc]

    @pl.when(turn == 3 * pieces - 1)
    def _():
        half_out[...] = sum_all[:, other_cols].reshape(half_out.shape).astype(BF16)
        half_link().start()
        stage[:, :, own_bc : in_width - own_bc] = (
            sum_all[:, bc_width:in_width].reshape(16, rows, in_width - bc_width).astype(BF16)
        )

    @pl.when(phase == 3)
    def _():
        features_back(grad_in.at[i], grad_gate.at[i], hid.at[0], halo.at[0], w_in, w_z, grad_gate.at[i], tails.at[i],
                      norm_sums, wide)
        grad_link(i).start()
        grad_store(i).start()

    last_links = Numbered(last_ones[6])

    def last_step(step):
        scatter_step(step, last_links.start, last_links.arrived, last_stage, sums_w, *last_ones[:6])

    @pl.when(turn == 3 * pieces)
    def _():
        half_link().wait_recv()
        own_half = sum_all[:, cols].reshape(half_in.shape) + half_in[...].astype(F32)
        stage[:, :, :own_bc] = own_half.astype(BF16)
        last_step(0)

    @pl.when(turn == 3 * pieces + 4)
    def _():
        last_step(1)

    @pl.when(turn == 3 * pieces + 5)
    def _():
        last_step(2)

    @pl.when(turn == 4 * pieces - 1)
    def _():
        for link_down in tail_links():
            pl.when(below)(link_down.start)
        small[0, :5] = conv_sums[:5]
        small[0, 5:6, :model] = norm_sums[:1]
        small[0, 5:6, model : model + LANES] = head_sums[:1]
        small[0, 5:6, model + LANES :] = head_sums[1:2]
        small[0, 6:8, :inner] = inner_sums[:2]
        small[0, 6:8, inner:] = jnp.zeros((2, channels - inner), F32)
        row = lax.broadcasted_iota(jnp.int32, small.shape[1:], 0)
        lane = lax.broadcasted_iota(jnp.int32, small.shape[1:], 1)
        shared = ((row < 5) & (lane < bc_width)) | ((row == 5) & (lane < model))
        small_link(0).start()
        for k in range(5):
            if k + 3 < scatter_steps():
                last_step(k + 3)
            small_link(k).wait_recv()
            small[k + 1] = small[k] + (jnp.where(shared, seen[k], 0.0) if k == 0 else seen[k])
            if k < 4:
                small_link(k + 1).start()
        total = small.at[5]
        conv_out[:, :own_bc] = total[:, cols]
        conv_out[:, own_bc:] = total[:, bc_width:]
        norm_out[...] = jnp.broadcast_to(total[5:6, :model], norm_out.shape)
        head_out[...] = jnp.zeros_like(head_out)
        head_out[0:1] = total[5:6, model : model + LANES]
        head_out[1:2] = total[5:6, model + LANES : model + 2 * LANES]
        inner_out[...] = jnp.zeros_like(inner_out)
        inner_out[0:2] = total[6:8, :inner]
        for link_down in tail_links():
            pl.when(above)(link_down.wait_recv)

        @pl.when(jnp.logical_not(above))
        def _():
            blank[...] = jnp.zeros_like(blank)
            for target, k in ((own_tail, 3), (other_tail.at[0], 4)):
                clear = pltpu.make_async_copy(blank, target, got.at[k])
                clear.start()
                clear.wait()

        part_link().wait_recv()
        for k in range(pieces_of(grad_gate)):
            grad_link(k).wait_recv()
            grad_link(k).wait_send()
            grad_store(k).wait()
        stats_link().wait_send()
        part_link().wait_send()
        half_link().wait_send()
        for link_down in tail_links():
            pl.when(below)(link_down.wait_send)
        for k in range(5):
            small_link(k).wait_send()
        for step in range(scatter_steps() - 1):
            scatter_step(step, last_links.sent, last_links.nothing, last_stage, sums_w, *last_ones[:6], add=False)


def pieces_of(array):
    return array.shape[0]


ANY = pl.BlockSpec(memory_space=pl.ANY)
IN_VMEM = pl.BlockSpec(memory_space=pltpu.VMEM)
DMA = pltpu.SemaphoreType.DMA


def call_between(kernel, collective_id, inputs, outputs, scratch):
    return pl.pallas_call(
        kernel,
        in_specs=[spec for _, spec in inputs],
        out_specs=[spec for _, spec in outputs],
        out_shape=[shape for shape, _ in outputs],
        scratch_shapes=scratch,
        compiler_params=pltpu.CompilerParams(
            collective_id=collective_id, has_side_effects=True, vmem_limit_bytes=VMEM_BYTES
        ),
        name=kernel.__name__,
    )(*[array for array, _ in inputs])


def gather_rows(rows):
    return lax.all_gather(rows, ("shard", "context"), axis=0, tiled=True)


def scatter_rows(rows):
    return lax.psum_scatter(rows.astype(F32), ("shard", "context"), scatter_dimension=0, tiled=True)


def passed_along(value, by):
    length = lax.axis_size("context")
    return lax.ppermute(value, "context", [(i, i + by) for i in range(length) if 0 <= i + by < length])


def chain(local, decay, by):
    arrived = jnp.zeros_like(local)
    for _ in range(lax.axis_size("context") - 1):
        leaving = decay[:, :1] * arrived.astype(F32) + local.astype(F32)
        arrived = passed_along(leaving.astype(BF16), by)
    return arrived


def exchange(value):
    everything = lax.all_gather(value, "tensor")
    return everything[0], everything[1:]


def part_of(width, at):
    return lambda array: pl.BlockSpec((array.shape[0], width), lambda i: (0, at))


class AnyMesh:
    def inputs(self, hid, w_bc, w_dt, w_x, conv_bc, conv_x):
        conv_bc_all = lax.all_gather(conv_bc, "tensor", axis=1, tiled=True)
        taps = jnp.pad(jnp.concatenate([conv_bc_all, conv_x], 1), ((0, 3), (0, 0)))
        w_bc_all = lax.all_gather(w_bc, "tensor", axis=1, tiled=True)
        w_dt_wide = jnp.pad(w_dt, ((0, 0), (0, LANES - w_dt.shape[1])))
        w_in = gather_rows(jnp.concatenate([w_bc_all, w_dt_wide, w_x], 1))
        return w_in, passed_along(hid[:, hid.shape[1] - HALO :], 1), taps

    def forward(self, hid, halo, age, seed, norm_in, w_in, w_z, w_out, taps, heads, spread, tri, norm_gate, skip):
        pieces, length, model = hid.shape
        inner, channels = w_z.shape[1], taps.shape[1]
        token = functools.partial(shaped, F32, pieces, length)
        token_low = functools.partial(shaped, BF16, pieces, length)
        normed, raw, pre, dt_raw, cum, local, decay = call(
            forward_local, pieces,
            [(hid, by_piece), (halo, by_piece), (age, by_piece), (norm_in, fixed), (w_in, fixed), (taps, fixed),
             (heads, fixed), (spread, fixed), (tri, fixed)],
            [(shaped(BF16, pieces, HALO + length, model), by_piece),
             (shaped(F32, pieces, HALO + length, channels), by_piece), (token(channels), by_piece),
             (token(LANES), by_piece), (token(LANES), by_piece), (shaped(BF16, pieces, LANES, inner), by_piece),
             (shaped(F32, pieces, 8, inner), by_piece)],
            [((length, channels), F32)], "forward_local",
        )
        state_in = chain(local, decay, 1)
        w_z_all, w_out_t = gather_rows(w_z), gather_rows(w_out.T)
        square = ((length, length), F32)
        token_wide = ((length, inner), F32)
        mixer, gate, grad_gn, part, stats = call(
            forward_mix, pieces,
            [(pre, by_piece), (dt_raw, by_piece), (cum, by_piece), (age, by_piece), (state_in, by_piece),
             (normed, by_piece), (seed, by_piece), (w_z_all, fixed), (w_out_t, fixed), (norm_gate, fixed),
             (skip, fixed), (heads, fixed), (spread, fixed)],
            [(token(inner), by_piece), (token(inner), by_piece), (token(inner), by_piece), (token_low(model), by_piece),
             (shaped(F32, pieces, 8, length), by_piece)],
            [token_wide, square, square, token_wide, token_wide, ((length, inner), BF16)], "forward_mix",
        )
        return normed, raw, pre, dt_raw, cum, decay, state_in, mixer, gate, grad_gn, part, stats, (w_z_all, fixed)

    def backward(self, inner_all, saved, stats, age_row, seed, hid, halo, age, own_bc, norm_gate, skip, heads, spread,
                 gather, tri_up, taps, w_in):
        normed, raw, pre, dt_raw, cum, decay, state_in, mixer, gate, grad_gn, part, _, w_z_all = saved
        pieces, length, model = hid.shape
        inner, channels, in_width, lead = mixer.shape[2], taps.shape[1], w_in.shape[1], HALO + length
        token = functools.partial(shaped, F32, pieces, length)
        token_low = functools.partial(shaped, BF16, pieces, length)
        square, token_wide, token_narrow = ((length, length), F32), ((length, inner), F32), ((length, inner), BF16)
        stats = lax.psum(stats, "tensor")
        grad_fed, grad_mix, grad_gate, grad_cum, grad_bc, grad_state, grad_wz, grad_wo, sums = call(
            functools.partial(backward_local, inner_all), pieces,
            [(mixer, by_piece), (gate, by_piece), (grad_gn, by_piece), (stats, by_piece), (pre, by_piece),
             (dt_raw, by_piece), (cum, by_piece), (age, by_piece), (age_row, by_piece), (state_in, by_piece),
             (normed, by_piece), (seed, by_piece), (norm_gate, fixed), (skip, fixed), (heads, fixed), (spread, fixed),
             (gather, fixed)],
            [(token(inner), by_piece), (token_low(inner), by_piece), (token_low(inner), by_piece),
             (token(LANES), by_piece), (token(2 * LANES), by_piece), (shaped(BF16, pieces, LANES, inner), by_piece),
             (shaped(BF16, model, inner), fixed), (shaped(BF16, model, inner), fixed), (shaped(F32, 8, inner), fixed)],
            [((model, inner), F32), ((model, inner), F32), square, square, square, token_wide, token_wide, token_narrow,
             token_narrow], "backward_local",
        )
        grad_later = chain(grad_state, decay, -1)
        grad_normed, grad_halo, grad_w, conv_sums, head_sums, norm_sums = call(
            backward_finish, pieces,
            [(grad_later, by_piece), (state_in, by_piece), (pre, by_piece), (raw, by_piece), (dt_raw, by_piece),
             (cum, by_piece), (age, by_piece), (grad_fed, by_piece), (grad_mix, by_piece), (grad_cum, by_piece),
             (grad_bc, by_piece), (grad_gate, by_piece), (normed, by_piece), (hid, by_piece), (halo, by_piece),
             (w_in, fixed), w_z_all, (taps, fixed), (skip, fixed), (heads, fixed), (spread, fixed), (gather, fixed),
             (tri_up, fixed)],
            [(token_low(model), by_piece), (shaped(BF16, pieces, HALO, model), by_piece),
             (shaped(BF16, model, in_width), fixed), (shaped(F32, 8, channels), fixed), (shaped(F32, 8, LANES), fixed),
             (shaped(F32, 8, model), fixed)],
            [((model, in_width), F32), token_wide, token_wide, token_wide, token_narrow,
             ((lead + 8, channels), F32), ((lead + 8, LANES), F32), ((lead, in_width), BF16), ((lead, model), F32)],
            "backward_finish",
        )
        sums_zo = jnp.concatenate([scatter_rows(grad_wz), scatter_rows(grad_wo)], 1)
        mine, bc_width = lax.axis_index("tensor"), 2 * LANES
        grad_w = scatter_rows(grad_w)
        grad_w_bc = lax.psum_scatter(grad_w[:, :bc_width], "tensor", scatter_dimension=1, tiled=True)
        norm_sums, conv_bc = lax.psum((norm_sums, conv_sums[:, :bc_width]), ("shard", "context", "tensor"))
        conv_x, head_sums, sums = lax.psum((conv_sums[:, bc_width:], head_sums, sums), ("shard", "context"))
        conv_bc = lax.dynamic_slice_in_dim(conv_bc, mine * own_bc, own_bc, 1)
        sums_w = jnp.concatenate([grad_w_bc, grad_w[:, bc_width:]], 1)
        small = (jnp.concatenate([conv_bc, conv_x], 1), norm_sums, head_sums, sums)
        return stats, sums_zo, sums_w, small, exchange(part), exchange(grad_normed), exchange(passed_along(grad_halo, -1))


class FourByFourByTwo:
    def inputs(self, hid, w_bc, w_dt, w_x, conv_bc, conv_x):
        rows, inner = w_x.shape
        pieces, _, model = hid.shape
        blocks = model // rows
        in_width = 3 * LANES + inner
        w_in, halo, taps = call_between(
            gather_inputs, 1,
            [(w_bc, IN_VMEM), (w_dt, IN_VMEM), (w_x, IN_VMEM), (conv_bc, IN_VMEM), (conv_x, IN_VMEM), (hid, ANY)],
            [(shaped(BF16, blocks, rows, in_width), ANY), (shaped(BF16, pieces, HALO, model), ANY),
             (shaped(F32, 8, 2 * LANES + inner), IN_VMEM)],
            [pltpu.VMEM((rows, in_width), BF16), DMA((GATHER_COPIES,)), DMA((3,)), DMA((blocks,)), DMA((3,)), DMA],
        )
        return w_in.reshape(model, in_width), halo, taps

    def forward(self, hid, halo, age, seed, norm_in, w_in, w_z, w_out, taps, heads, spread, tri, norm_gate, skip):
        pieces, length, model = hid.shape
        rows, inner = w_z.shape
        channels = taps.shape[1]
        lead = HALO + length

        def at_phase(phase):
            def cut(array):
                rest = array.shape[1:]

                def where(p, i):
                    return (jnp.where(p == phase, i, jnp.where(p < phase, 0, pieces - 1)),) + (0,) * len(rest)

                return pl.BlockSpec((1,) + rest, where)

            return cut

        def always(array):
            return pl.BlockSpec((1,) + array.shape[1:], lambda p, i: (i,) + (0,) * (array.ndim - 1))

        def once(array):
            return pl.BlockSpec(array.shape, lambda p, i: (0,) * array.ndim, pipeline_mode=pl.Buffered(1))

        def anywhere(array):
            return ANY

        token = functools.partial(shaped, F32, pieces, length)
        state = shaped(BF16, pieces, LANES, inner)
        normed, pre, narrow = shaped(BF16, pieces, lead, model), token(channels), token(LANES)
        decay, both = shaped(F32, pieces, 8, inner), shaped(BF16, 16, rows, 2 * inner)
        inputs = [(hid, at_phase(0)), (halo, at_phase(0)), (age, always), (seed, at_phase(1)), (norm_in, once),
                  (w_in, once), (w_z, once), (w_out, once), (taps, once), (heads, once), (spread, once), (tri, once),
                  (norm_gate, once), (skip, once)]
        outputs = [(shaped(F32, pieces, lead, channels), at_phase(0)), (token(inner), at_phase(2)),
                   (shaped(BF16, pieces, length, model), at_phase(2)), (shaped(F32, pieces, 8, length), at_phase(2)),
                   (normed, anywhere), (pre, anywhere), (narrow, anywhere), (narrow, anywhere),
                   (token(inner), anywhere), (token(inner), anywhere), (state, anywhere), (decay, anywhere),
                   (both, anywhere)]
        kept = [normed, pre, narrow, narrow, token(inner), token(inner), token(inner), state, state, decay, both]
        raw, mixer, part, stats, normed, pre, dt_raw, cum, gate, grad_gn, state_in, decay, both = pl.pallas_call(
            forward,
            grid=(3, pieces),
            in_specs=[cut(array) for array, cut in inputs],
            out_specs=[cut(shape) for shape, cut in outputs],
            out_shape=[shape for shape, _ in outputs],
            scratch_shapes=[pltpu.VMEM(shape.shape, shape.dtype) for shape in kept]
            + [pltpu.VMEM((rows, 2 * inner), BF16), pltpu.VMEM((length, channels), F32),
               pltpu.VMEM((length, length), F32), pltpu.VMEM((length, length), F32), pltpu.VMEM((length, inner), F32),
               pltpu.VMEM((length, inner), BF16), DMA((GATHER_COPIES,)), DMA((16,)), DMA, DMA((2, pieces)),
               DMA((8, pieces))],
            compiler_params=pltpu.CompilerParams(
                collective_id=2, has_side_effects=True, vmem_limit_bytes=VMEM_BYTES
            ),
            name="forward",
        )(*[array for array, _ in inputs])
        w_z_all = (both.reshape(model, 2 * inner), part_of(inner, 0))
        return normed, raw, pre, dt_raw, cum, decay, state_in, mixer, gate, grad_gn, part, stats, w_z_all

    def backward(self, inner_all, saved, stats, age_row, seed, hid, halo, age, own_bc, norm_gate, skip, heads, spread,
                 gather, tri_up, taps, w_in):
        normed, raw, pre, dt_raw, cum, decay, state_in, mixer, gate, grad_gn, part, _, (w_z, w_z_spec) = saved
        pieces, length, model = hid.shape
        inner, channels, in_width, lead = mixer.shape[2], taps.shape[1], w_in.shape[1], HALO + length
        rows = model // 16
        width = in_width - own_bc

        def during(*phases):
            def cut(array):
                rest = array.shape[1:]

                def where(p, i):
                    at = jnp.where(p < phases[0], 0, pieces - 1)
                    for phase in phases:
                        at = jnp.where(p == phase, i, at)
                    return (at,) + (0,) * len(rest)

                return pl.BlockSpec((1,) + rest, where)

            return cut

        def once(array):
            return pl.BlockSpec(array.shape, lambda p, i: (0,) * array.ndim, pipeline_mode=pl.Buffered(1))

        def first_columns(array):
            return pl.BlockSpec((array.shape[0], inner), lambda p, i: (0, 0), pipeline_mode=pl.Buffered(1))

        def kept(array):
            return pl.BlockSpec(array.shape, lambda p, i: (0,) * array.ndim)

        def anywhere(array):
            return ANY

        def vmem(kind, *dims):
            return pltpu.VMEM(dims, kind)

        token_low = shaped(BF16, pieces, length, model)
        tail = shaped(BF16, pieces, HALO, model)
        inputs = [(mixer, during(0)), (gate, during(0)), (grad_gn, during(0)), (pre, during(0, 1, 2)),
                  (dt_raw, during(1, 2)), (cum, during(0, 1, 2)), (age, during(0, 2)), (age_row, during(1)),
                  (state_in, during(0, 2)), (normed, during(0, 2)), (seed, during(0)), (raw, during(2)), (hid, during(3)),
                  (halo, during(3)), (stats, once), (decay, once), (norm_gate, once), (skip, once), (heads, once),
                  (spread, once), (gather, once), (tri_up, once), (taps, once), (w_in, once), (w_z, first_columns),
                  (part, anywhere)]
        outputs = [(shaped(F32, *stats.shape), kept), (shaped(F32, rows, 2 * inner), kept), (shaped(F32, rows, width), kept),
                   (shaped(F32, 8, channels - own_bc), kept), (shaped(F32, 8, model), kept), (shaped(F32, 8, LANES), kept),
                   (shaped(F32, 8, inner), kept), (shaped(BF16, 1, *part.shape), anywhere), (token_low, anywhere),
                   (shaped(BF16, 1, *token_low.shape), anywhere), (tail, anywhere),
                   (shaped(BF16, 1, *tail.shape), anywhere)]
        square = vmem(F32, length, length)
        scratch = [
            vmem(BF16, pieces, length, inner), vmem(BF16, pieces, length, inner), vmem(F32, pieces, length, LANES),
            vmem(F32, pieces, length, 2 * LANES), vmem(F32, pieces, length, inner), vmem(F32, model, 2 * inner),
            vmem(BF16, pieces, lead, in_width), vmem(BF16, 16, rows, 2 * inner), vmem(BF16, 16, rows, own_bc),
            vmem(BF16, 16, rows, own_bc), vmem(BF16, *state_in.shape), vmem(BF16, *state_in.shape),
            vmem(F32, length, inner), vmem(F32, length, inner), vmem(BF16, length, inner), vmem(BF16, length, inner),
            vmem(F32, lead + 8, channels), vmem(F32, lead + 8, LANES), vmem(F32, lead, model), square, square, square,
            vmem(BF16, *tail.shape), vmem(BF16, *tail.shape), vmem(F32, *stats.shape), vmem(F32, 6, 8, channels),
            vmem(F32, 5, 8, channels), vmem(F32, 8, channels), vmem(F32, 8, LANES), vmem(F32, 8, model),
            vmem(F32, 8, inner), DMA((10,)), DMA((10,)), DMA((pieces,)), DMA((pieces,)), DMA((2, pieces)), DMA((pieces,)),
        ]
        (stats, sums_zo, sums_w, conv_sums, norm_sums, head_sums, sums, other_part, own_grad, other_grad, own_tail,
         other_tail) = pl.pallas_call(
            functools.partial(backward, inner_all),
            grid=(4, pieces),
            in_specs=[cut(array) for array, cut in inputs],
            out_specs=[cut(shape) for shape, cut in outputs],
            out_shape=[shape for shape, _ in outputs],
            scratch_shapes=scratch + scatter_scratch(rows, 2 * inner) + scatter_scratch(rows, width),
            compiler_params=pltpu.CompilerParams(collective_id=3, has_side_effects=True, vmem_limit_bytes=VMEM_BYTES),
            name="backward",
        )(*[array for array, _ in inputs])
        small = (conv_sums, norm_sums, head_sums, sums)
        return stats, sums_zo, sums_w, small, (part, other_part), (own_grad, other_grad), (own_tail, other_tail)


def links():
    sizes = tuple(lax.axis_size(axis) for axis in ("shard", "context", "tensor"))
    return FourByFourByTwo() if sizes == (4, 4, 2) else AnyMesh()


def shards(inner_all, hidden_in, out_grad, doc_start, norm_in, w_z, w_x, w_bc, w_dt, conv_x, conv_bc, dt_bias, a_log,
           skip_d, norm_gate, w_out):
    micro, per_device, length, model = hidden_in.shape
    pieces = micro * per_device
    inner = w_z.shape[1]
    head_count = w_dt.shape[1]
    bc_width = w_bc.shape[1] * lax.axis_size("tensor")
    channels = bc_width + inner
    in_width = channels + LANES
    lead = HALO + length
    offset = lax.axis_index("context") * length

    head_of = np.arange(inner) // HEAD
    gather = jnp.asarray(head_of[:, None] == np.arange(LANES)[None], BF16)
    spread = jnp.asarray(head_of[None] == np.arange(LANES)[:, None], BF16)
    tri = jnp.asarray(np.tril(np.ones((length, length))), BF16)
    tri_up = jnp.asarray(np.triu(np.ones((length, length))), BF16)

    def head_row(row):
        return jnp.pad(row, (0, LANES - head_count))

    heads = jnp.stack([head_row(dt_bias), head_row(a_log)] + [jnp.zeros((LANES,), F32)] * 6)
    skip = jnp.repeat(skip_d, HEAD)[None]
    norm_in, norm_gate = norm_in[None], norm_gate[None]
    hid = hidden_in.reshape(pieces, length, model)
    seed = out_grad.reshape(pieces, length, model)
    between = links()
    w_in, halo, taps = between.inputs(hid, w_bc, w_dt, w_x, conv_bc, conv_x)
    ages = (offset + jnp.arange(length, dtype=jnp.int32) - doc_start.reshape(pieces, length)).astype(F32)
    age = jnp.broadcast_to(ages[:, :, None], (pieces, length, LANES))
    age_row = jnp.broadcast_to(ages[:, None, :], (pieces, 8, length))

    token = functools.partial(shaped, F32, pieces, length)
    token_low = functools.partial(shaped, BF16, pieces, length)
    state = shaped(BF16, pieces, LANES, inner)
    saved = between.forward(
        hid, halo, age, seed, norm_in, w_in, w_z, w_out, taps, heads, spread, tri, norm_gate, skip
    )
    own_bc = w_bc.shape[1]
    stats, sums_zo, sums_w, small, (own_part, other_part), (own_grad, other_grad), (own_tail, other_tail) = (
        between.backward(inner_all, saved, saved[-2], age_row, seed, hid, halo, age, own_bc, norm_gate, skip, heads,
                         spread, gather, tri_up, taps, w_in)
    )
    token_low = functools.partial(shaped, BF16, pieces, length)
    rows = w_z.shape[0]
    outputs = [shaped(F32, rows, inner), shaped(F32, rows, inner), shaped(F32, rows, own_bc),
               shaped(F32, rows, head_count), shaped(F32, inner, rows), shaped(F32, 5, inner), shaped(F32, 5, own_bc),
               shaped(F32, 1, head_count), shaped(F32, 1, head_count), shaped(F32, 1, head_count),
               shaped(F32, 1, inner), shaped(F32, 1, model)]
    (out, in_grad, grad_wz, grad_wx, grad_wbc, grad_wdt, grad_wo, grad_conv_x, grad_conv_bc, grad_dt_bias, grad_a_log,
     grad_skip, grad_norm_gate, grad_norm_in) = call(
        functools.partial(finish, inner_all), pieces,
        [(hid, by_piece), (seed, by_piece), (stats, by_piece), (norm_in, fixed), (own_part, by_piece),
         (other_part, by_piece_second), (own_grad, by_piece), (other_grad, by_piece_second), (own_tail, by_piece),
         (other_tail, by_piece_second), (sums_zo, fixed), (sums_w, fixed)] + [(array, fixed) for array in small]
        + [(gather, fixed)],
        [(token_low(model), by_piece), (token_low(model), by_piece)] + [(shape, fixed) for shape in outputs],
        [((length, model), F32)], "finish",
    )
    return (
        out.reshape(hidden_in.shape),
        in_grad.reshape(hidden_in.shape),
        grad_norm_in[0],
        grad_wz,
        grad_wx,
        grad_wbc,
        grad_wdt,
        grad_conv_x,
        grad_conv_bc,
        grad_dt_bias[0],
        grad_a_log[0],
        grad_skip[0],
        grad_norm_gate[0],
        grad_wo,
    )


def solution(mesh):
    whole = P(None, "shard", "context", None)
    rows = P(("shard", "context"), "tensor")
    lanes = P(None, "tensor")
    heads = P("tensor")
    w_out = P("tensor", ("shard", "context"))
    inputs = (whole, whole, P(None, "shard", "context"), P(), rows, rows, rows, rows, lanes, lanes, heads, heads, heads, heads, w_out)
    outputs = (whole, whole, P(), rows, rows, rows, rows, lanes, lanes, heads, heads, heads, heads, w_out)

    def placed(*arrays):
        inner_all = arrays[4].shape[1]
        return jax.shard_map(
            functools.partial(shards, inner_all), mesh=mesh, in_specs=inputs, out_specs=outputs, check_vma=False
        )(*arrays)

    return placed
```

```python
import functools

import jax
import jax.numpy as jnp
import numpy as np
from jax import lax
from jax.experimental import pallas as pl
from jax.experimental.pallas import tpu as pltpu
from jax.sharding import PartitionSpec as P

EPSILON = 1e-05
F32, BF16 = jnp.float32, jnp.bfloat16
HEAD = 64
LANES = 128
HALO = 16
ROWS = 64
GONE = -1e30
VMEM_BYTES = 60 * 1024 * 1024
BLOCK_VMEM_BYTES = 63 * 1024 * 1024


def mm(left, right):
    return jnp.dot(left, right, preferred_element_type=F32)


def mm_nt(left, right):
    return lax.dot_general(left, right, (((1,), (1,)), ((), ())), preferred_element_type=F32)


def mm_tn(left, right):
    return lax.dot_general(left, right, (((0,), (0,)), ((), ())), preferred_element_type=F32)


def parts_of(value, count):
    parts = []
    for _ in range(count - 1):
        parts.append(value.astype(BF16))
        value = value - parts[-1].astype(F32)
    return parts + [value.astype(BF16)]


def pick(value, ones, count=2):
    return sum(mm(part, ones) for part in parts_of(value, count))


def pick_left(ones, value, count=3):
    found = mm(ones, jnp.concatenate(parts_of(value, count), 1))
    width = value.shape[1]
    return sum(found[:, k * width : (k + 1) * width] for k in range(count))


SLOTS = 16


def three_parts(value):
    high = value.astype(BF16).astype(F32)
    middle = (value - high).astype(BF16).astype(F32)
    lane = lax.broadcasted_iota(jnp.int32, value.shape, 1)
    chosen = jnp.where(lane < SLOTS, high, jnp.where(lane < 2 * SLOTS, middle, value - high - middle))
    return jnp.where(lane < 3 * SLOTS, chosen, 0.0).astype(BF16)


def to_lanes(value, ones):
    return mm(three_parts(value), ones)


def folded(value):
    return jnp.sum(value.reshape(-1, 8, value.shape[1]), 0)


def to_rows(folds):
    rows = [jnp.sum(fold, 0, keepdims=True) for fold in folds]
    return jnp.concatenate(rows + [jnp.zeros_like(rows[0])] * (8 - len(rows)), 0)


def softplus(value):
    return jnp.maximum(value, 0.0) + jnp.log1p(jnp.exp(-jnp.abs(value)))


def sigmoid(value):
    return jax.nn.sigmoid(value)


def column_blocks(width):
    return [(at, min(LANES, width - at)) for at in range(0, width, LANES)]


def row_blocks(length):
    return [(at, min(ROWS, length - at)) for at in range(0, length, ROWS)]


def row_index(length):
    return lax.broadcasted_iota(jnp.int32, (length, LANES), 0).astype(F32)


def is_first_step():
    return pl.program_id(0) == 0


def is_last_step():
    return pl.program_id(0) == pl.num_programs(0) - 1


def half_masks(width):
    lane = lax.broadcasted_iota(jnp.int32, (1, width), 1)
    return [(lane // HEAD) == k for k in range(width // HEAD)]


def normalised(hidden, gain):
    scale = lax.rsqrt(jnp.mean(hidden * hidden, -1, keepdims=True) + EPSILON)
    return hidden * scale * gain, scale


def keep_masks(age, masks):
    for lag in range(1, 4):
        masks[lag - 1] = jnp.where(age[...] >= lag, 1.0, 0.0)


def normalise(hid, norm_in, normed):
    for at in range(0, hid.shape[0], 64):
        rows = slice(at, min(at + 64, hid.shape[0]))
        normed[rows] = normalised(hid[rows].astype(F32), norm_in[...])[0].astype(BF16)


def project(age, w_in, taps, heads, spread, tri,
            normed, raw_low, pre, dt_raw, cum, local, decay, act, masks, raw):
    length, channels = act.shape[0], taps.shape[1]
    bc_width = 2 * LANES
    raw[:, :bc_width] = mm(normed[...], w_in[:, :bc_width])
    raw[:, bc_width:] = mm(normed[...], w_in[:, bc_width + LANES :])
    raw_low[:, :bc_width] = raw[:, :bc_width].astype(BF16)
    raw_low[:, bc_width + LANES :] = raw[:, bc_width:].astype(BF16)
    dt_raw[...] = mm(normed[HALO:], w_in[:, bc_width : bc_width + LANES])
    keep_masks(age, masks)
    for at, width in column_blocks(channels):
        cols = slice(at, at + width)
        running = taps[4:5, cols] + taps[0:1, cols] * raw[HALO:, cols]
        for lag in range(1, 4):
            tapped = masks[lag - 1, :, :width] * raw[HALO - lag : HALO - lag + length, cols]
            running = running + taps[lag : lag + 1, cols] * tapped
        pre[:, cols] = running.astype(BF16)
        running = pre[:, cols].astype(F32)
        act[:, cols] = running * sigmoid(running)
    step = softplus(dt_raw[...] + heads[0:1])
    total = pick_left(tri[...], -jnp.exp(heads[1:2]) * step)
    cum[...] = total
    last, age_last = total[length - 1 :], age[length - 1 :]
    open_end = row_index(length) - (length - 1) + age_last >= 0
    weight = jnp.where(open_end, jnp.exp(last - total), 0.0) * step
    weighted = (act[:, bc_width:] * to_lanes(weight, spread[...])).astype(BF16)
    local[...] = mm_tn(act[:, :LANES].astype(BF16), weighted).astype(BF16)
    kept = jnp.where(age_last > length - 1, jnp.exp(last), 0.0)
    decay[...] = to_lanes(jnp.broadcast_to(kept, (8, LANES)), spread[...])


def activated(pre):
    value = pre[...].astype(F32)
    return (value * sigmoid(value)).astype(BF16)


def wide_mask(back, age):
    age = jnp.concatenate([age] * (back.shape[1] // LANES), 1) if age.shape[0] > 1 else age
    return jnp.where((back >= 0) & (back <= age), 0.0, GONE)


def gate_products(normed, out_grad, w_z, w_out_t, gate, grad_gn):
    gate[...] = mm(normed[HALO:], w_z()).astype(BF16)
    grad_gn[...] = mm(out_grad[...], w_out_t()).astype(BF16)


def mix_within(pre, dt_raw, cum, age, skip, heads, spread, near, seg, pair, step_x):
    length, inner = near.shape
    bc_width = 2 * LANES
    pair[...] = mm_nt(activated(pre.at[:, LANES:bc_width]), activated(pre.at[:, :LANES]))
    row = lax.broadcasted_iota(jnp.int32, (length, length), 0)
    col = lax.broadcasted_iota(jnp.int32, (length, length), 1)
    back = (row - col).astype(F32)
    seg[...] = wide_mask(back, age[...])
    total = cum[...]
    total_t = cum[...].T
    step_x[...] = to_lanes(softplus(dt_raw[...] + heads[0:1]), spread[...])
    for at, width in column_blocks(inner):
        cols = slice(at, at + width)
        x_pre = pre[:, bc_width + at : bc_width + at + width].astype(F32)
        values = x_pre * sigmoid(x_pre)
        fed = (values * step_x[:, cols]).astype(BF16)
        masks = half_masks(width)
        for start in range(0, length, LANES):
            stop = start + LANES
            mixing = []
            for head in range(at // HEAD, (at + width) // HEAD):
                spread_log = total[start:stop, head : head + 1] - total_t[head : head + 1, :stop]
                mixing.append((pair[start:stop, :stop] * jnp.exp(spread_log + seg[start:stop, :stop])).astype(BF16))
            fed_to = jnp.concatenate([jnp.where(mask, fed[:stop], 0) for mask in masks], 0)
            near[start:stop, cols] = skip[:, cols] * values[start:stop] + mm(jnp.concatenate(mixing, 1), fed_to)


def mix_states(pre, cum, age, state_in, near, gate, grad_gn, w_out_t, norm_gate, spread,
               mixer, part, stats, carried, gated_low):
    length, inner = near.shape
    open_start = age[...] > row_index(length)
    carried[...] = to_lanes(jnp.where(open_start, jnp.exp(cum[...]), 0.0), spread[...])
    carried[...] = carried[...] * mm(activated(pre.at[:, LANES : 2 * LANES]), state_in[...])
    squares, products = {}, {}
    for at, width in column_blocks(inner):
        cols = slice(at, at + width)
        mixed = near[:, cols] + carried[:, cols]
        mixer[:, cols] = mixed
        raw_gate = gate[:, cols].astype(F32)
        gated = mixed * (raw_gate * sigmoid(raw_gate))
        weighted = gated * norm_gate[:, cols]
        gated_low[:, cols] = weighted.astype(BF16)
        squares[width] = squares.get(width, 0.0) + gated * gated
        products[width] = products.get(width, 0.0) + grad_gn[:, cols].astype(F32) * weighted
    part[...] = mm_nt(gated_low[...], w_out_t()).astype(BF16)
    lane = lax.broadcasted_iota(jnp.int32, (length, LANES), 1)
    squares = sum(jnp.sum(found, 1, keepdims=True) for found in squares.values())
    products = sum(jnp.sum(found, 1, keepdims=True) for found in products.values())
    columns = jnp.where(lane == 0, squares, jnp.where(lane == 1, products, 0.0))
    stats[...] = columns.T[:8]


def forward_local(hid, halo, age, norm_in, w_in, taps, heads, spread, tri,
                  normed, raw, pre, dt_raw, cum, local, decay, act, masks, raw_wide):
    normalise(halo.at[0], norm_in, normed.at[0, :HALO])
    normalise(hid.at[0], norm_in, normed.at[0, HALO:])
    project(age.at[0], w_in, taps, heads, spread, tri, normed.at[0], raw.at[0],
            pre.at[0], dt_raw.at[0], cum.at[0], local.at[0], decay.at[0], act, masks, raw_wide)


def forward_mix(pre, dt_raw, cum, age, state_in, normed, out_grad, w_z, w_out_t, norm_gate, skip, heads, spread,
                mixer, gate, grad_gn, part, stats, near, seg, pair, carried, step_x, gated_low):
    w_z_all, w_out_all = (lambda: w_z[...]), (lambda: w_out_t[...])
    gate_products(normed.at[0], out_grad.at[0], w_z_all, w_out_all, gate.at[0], grad_gn.at[0])
    mix_within(pre.at[0], dt_raw.at[0], cum.at[0], age.at[0], skip, heads, spread, near, seg, pair, step_x)
    mix_states(pre.at[0], cum.at[0], age.at[0], state_in.at[0], near, gate.at[0], grad_gn.at[0], w_out_all, norm_gate,
               spread, mixer.at[0], part.at[0], stats.at[0], carried, gated_low)


def gate_back(inner_all, mixer, gate, grad_gn, stats, pre, cum, age, state_in, normed, out_grad, norm_gate,
              spread, grad_mix, grad_gate, grad_c, grad_state, sums, sum_z, sum_o,
              carried, gated_low, from_state):
    length, inner = mixer.shape
    bc_width = 2 * LANES
    open_start = age[...] > row_index(length)
    carried[...] = to_lanes(jnp.where(open_start, jnp.exp(cum[...]), 0.0), spread[...])
    means = stats[...].T / inner_all
    scale_all = jnp.broadcast_to(lax.rsqrt(means[:, :1] + EPSILON), (length, LANES))
    pull_all = scale_all * scale_all * scale_all * jnp.broadcast_to(means[:, 1:2], (length, LANES))
    for at, width in column_blocks(inner):
        cols = slice(at, at + width)
        scale, pull = scale_all[:, :width], pull_all[:, :width]
        mixed = mixer[:, cols]
        raw_gate = gate[:, cols].astype(F32)
        logistic = sigmoid(raw_gate)
        acted = raw_gate * logistic
        gated = mixed * acted
        grad_out = grad_gn[:, cols].astype(F32)
        gated_scaled = gated * scale
        gated_low[:, cols] = (gated_scaled * norm_gate[:, cols]).astype(BF16)
        grad_gated = scale * (grad_out * norm_gate[:, cols]) - gated * pull
        grad_gate[:, cols] = (grad_gated * mixed * (logistic * (1.0 + raw_gate * (1.0 - logistic)))).astype(BF16)
        mix_low = (grad_gated * acted).astype(BF16)
        grad_mix[:, cols] = mix_low
        sums[0, :, cols] += folded(grad_out * gated_scaled)
        from_state[:, cols] = (carried[:, cols] * mix_low.astype(F32)).astype(BF16)
    grad_state[...] = mm_tn(activated(pre.at[:, LANES:bc_width]), from_state[...]).astype(BF16)
    grad_c[...] = mm_nt(from_state[...], state_in[...])
    sum_z[...] += mm_tn(normed[HALO:], grad_gate[...])
    sum_o[...] += mm_tn(out_grad[...], gated_low[...])


def within_back(mixer, pre, dt_raw, cum, age_row, grad_mix, skip, heads, spread, gather, grad_fed, grad_cum, grad_bc,
                sums, seg, pair, grad_pair, step_x, high, low):
    length, inner = grad_mix.shape
    bc_width = 2 * LANES
    readout, inputs_b = activated(pre.at[:, LANES:bc_width]), activated(pre.at[:, :LANES])
    pair[...] = mm_nt(inputs_b, readout)
    grad_pair[...] = jnp.zeros_like(grad_pair)
    row = lax.broadcasted_iota(jnp.int32, (length, length), 0)
    col = lax.broadcasted_iota(jnp.int32, (length, length), 1)
    back = (col - row).astype(F32)
    seg[...] = wide_mask(back, age_row[:1])
    total = cum[...]
    total_t = cum[...].T
    step_x[...] = to_lanes(softplus(dt_raw[...] + heads[0:1]), spread[...])
    for at, width in column_blocks(inner):
        cols = slice(at, at + width)
        x_pre = pre[:, bc_width + at : bc_width + at + width].astype(F32)
        values = x_pre * sigmoid(x_pre)
        fed = (values * step_x[:, cols]).astype(BF16)
        mix_low = grad_mix[:, cols]
        mix_wide = mix_low.astype(F32)
        kept = mix_wide * (mixer[:, cols] - skip[:, cols] * values)
        masks = half_masks(width)
        for start in range(0, length, LANES):
            stop = start + LANES
            fed_from = jnp.concatenate([jnp.where(mask, fed[start:stop], 0) for mask in masks], 0)
            grad_mixing = mm_nt(fed_from, mix_low[start:])
            total_pair = grad_pair[start:stop, start:]
            mixing = []
            for k, head in enumerate(range(at // HEAD, (at + width) // HEAD)):
                spread_log = total_t[head : head + 1, start:] - total[start:stop, head : head + 1]
                decayed = jnp.exp(spread_log + seg[start:stop, start:])
                mixing.append((pair[start:stop, start:] * decayed).astype(BF16))
                total_pair = total_pair + grad_mixing[k * LANES : (k + 1) * LANES] * decayed
            grad_pair[start:stop, start:] = total_pair
            mix_to = jnp.concatenate([jnp.where(mask, mix_low[start:], 0) for mask in masks], 0)
            grad_fed[start:stop, cols] = mm(jnp.concatenate(mixing, 1), mix_to)
        sums[1, :, cols] += folded(mix_wide * values)
        kept = kept - grad_fed[:, cols] * fed.astype(F32)
        high[:, cols] = kept.astype(BF16)
        low[:, cols] = (kept - high[:, cols].astype(F32)).astype(BF16)
    grad_cum[...] = mm(high[...], gather[...]) + mm(low[...], gather[...])
    pair_low = grad_pair[...].astype(BF16)
    grad_bc[:, :LANES] = mm(pair_low, readout)
    grad_bc[:, LANES:] += mm_tn(pair_low, inputs_b)


def state_back(grad_later, state_in, pre, raw, dt_raw, cum, age, grad_fed, grad_mix, grad_cum, grad_bc, taps, skip,
               heads, spread, gather, tri_up, grad_in, conv_sums, head_sums,
               step_x, open_x, from_state, fed_state, met_state, met_all, slope, keep):
    length, inner = grad_fed.shape
    channels = taps.shape[1]
    bc_width = 2 * LANES
    lead = HALO + length
    grad_in[:HALO, bc_width : bc_width + LANES] = jnp.zeros((HALO, LANES), BF16)
    for lag in range(1, 4):
        keep[lag - 1, HALO - lag : lead - lag] = jnp.where(age[...] >= lag, 1.0, 0.0)
    total = cum[...]
    step_raw = dt_raw[...] + heads[0:1]
    step = softplus(step_raw)
    rate = -jnp.exp(heads[1:2])
    step_x[...] = to_lanes(step, spread[...])
    last, age_last = total[length - 1 :], age[length - 1 :]
    open_end = row_index(length) - (length - 1) + age_last >= 0
    open_x[...] = to_lanes(jnp.where(open_end, jnp.exp(last - total), 0.0), spread[...])
    from_state[...] = open_x[...] * mm(activated(pre.at[:, :LANES]), grad_later[...])
    for at, width in column_blocks(inner):
        cols = slice(at, at + width)
        x_pre = pre[:, bc_width + at : bc_width + at + width].astype(F32)
        logistic = sigmoid(x_pre)
        values = x_pre * logistic
        fed = values * step_x[:, cols]
        fed_state[:, cols] = (fed * open_x[:, cols]).astype(BF16)
        arrived = from_state[:, cols]
        grad = grad_fed[:, cols] + arrived
        met_state[:, cols] = (values * arrived).astype(BF16)
        met_all[:, cols] = (values * grad).astype(BF16)
        grad_values = grad * step_x[:, cols] + skip[:, cols] * grad_mix[:, cols].astype(F32)
        slope[HALO:lead, bc_width + at : bc_width + at + width] = grad_values * (
            logistic * (1.0 + x_pre * (1.0 - logistic))
        )
    for at, extra in ((0, mm_nt(fed_state[...], grad_later[...])), (LANES, 0.0)):
        cols = slice(at, at + LANES)
        bc_pre = pre[:, cols].astype(F32)
        logistic = sigmoid(bc_pre)
        slope[HALO:lead, cols] = (grad_bc[:, cols] + extra) * (logistic * (1.0 + bc_pre * (1.0 - logistic)))
    state_sum, step_sum = mm(met_state[...], gather[...]) * step, mm(met_all[...], gather[...])
    kept = jnp.where(age_last > length - 1, jnp.exp(last), 0.0)
    met = jnp.sum(grad_later[...].astype(F32) * state_in[...].astype(F32), 0, keepdims=True)
    met = pick(jnp.broadcast_to(met, (8, inner)), gather[...], 3)[:1]
    end = met * kept + jnp.sum(state_sum, 0, keepdims=True)
    grad_a = pick_left(tri_up[...], grad_cum[...] - state_sum) + end
    head_sums[1] += folded(grad_a * rate * step)
    grad_step = (step_sum + grad_a * rate) * sigmoid(step_raw)
    head_sums[0] += folded(grad_step)
    grad_in[HALO:, bc_width : bc_width + LANES] = grad_step.astype(BF16)
    for at, width in column_blocks(channels):
        cols = slice(at, at + width)
        shifted = at if at < bc_width else at + LANES
        for top, rows in row_blocks(lead):
            here = slice(top, top + rows)
            own, fed_in = slope[here, cols], raw[here, shifted : shifted + width].astype(F32)
            total_in = taps[0:1, cols] * own
            conv_sums[0, :, cols] += folded(own * fed_in)
            conv_sums[4, :, cols] += folded(own)
            for lag in range(1, 4):
                later = keep[lag - 1, here, :width] * slope[top + lag : top + rows + lag, cols]
                conv_sums[lag, :, cols] += folded(later * fed_in)
                total_in = total_in + taps[lag : lag + 1, cols] * later
            grad_in[here, shifted : shifted + width] = total_in.astype(BF16)


def clear_margins(slope, keep, length):
    slope[:HALO] = jnp.zeros((HALO, slope.shape[1]), F32)
    slope[HALO + length :] = jnp.zeros((8, slope.shape[1]), F32)
    keep[...] = jnp.zeros_like(keep)


def features_back(grad_in, grad_gate, w_in, w_z, grad_normed, grad_halo, wide):
    wide[...] = mm_nt(grad_in[...], w_in[...])
    wide[HALO:] += mm_nt(grad_gate[...], w_z())
    grad_halo[...] = wide[:HALO].astype(BF16)
    grad_normed[...] = wide[HALO:].astype(BF16)


def gain_back(weights, gradients, sums):
    for top in range(0, weights.shape[0], 2 * LANES):
        rows = slice(top, top + 2 * LANES)
        total = 0.0
        for at, width in column_blocks(weights.shape[1]):
            cols = slice(at, at + width)
            total = total + weights[rows, cols].astype(F32) * gradients[rows, cols]
        sums[:, rows] += folded(total.T)


def backward_local(inner_all, mixer, gate, grad_gn, stats, pre, dt_raw, cum, age, age_row, state_in, normed, out_grad,
                   norm_gate, skip, heads, spread, gather,
                   grad_fed, grad_mix, grad_gate, grad_cum, grad_bc, grad_state, grad_wz, grad_wo, sums_out,
                   sums, sum_z, sum_o, seg, pair, grad_pair, carried, step_x, gated_low, from_state):
    @pl.when(is_first_step())
    def _():
        sum_z[...] = jnp.zeros_like(sum_z)
        sum_o[...] = jnp.zeros_like(sum_o)
        sums[...] = jnp.zeros_like(sums)

    gate_back(inner_all, mixer.at[0], gate.at[0], grad_gn.at[0], stats.at[0], pre.at[0], cum.at[0], age.at[0],
              state_in.at[0], normed.at[0], out_grad.at[0], norm_gate, spread, grad_mix.at[0],
              grad_gate.at[0], grad_bc.at[0, :, LANES:], grad_state.at[0], sums, sum_z, sum_o,
              carried, gated_low, from_state)
    within_back(mixer.at[0], pre.at[0], dt_raw.at[0], cum.at[0], age_row.at[0], grad_mix.at[0], skip, heads, spread,
                gather, grad_fed.at[0], grad_cum.at[0], grad_bc.at[0], sums, seg, pair, grad_pair, step_x, gated_low,
                from_state)

    @pl.when(is_last_step())
    def _():
        grad_wz[...] = sum_z[...].astype(BF16)
        grad_wo[...] = sum_o[...].astype(BF16)
        sums_out[...] = to_rows([sums[0], sums[1]])


def backward_finish(grad_later, state_in, pre, raw, dt_raw, cum, age, grad_fed, grad_mix, grad_cum, grad_bc, grad_gate,
                    normed, hid, halo, w_in, w_z, taps, skip, heads, spread, gather, tri_up,
                    grad_normed, grad_halo, grad_w, conv_out, head_out, norm_out,
                    conv_sums, head_sums, norm_sums, sum_w, step_x, open_x, from_state, fed_state, met_state, met_all,
                    slope, keep, grad_in, wide):
    @pl.when(is_first_step())
    def _():
        for sums in (sum_w, conv_sums, head_sums, norm_sums):
            sums[...] = jnp.zeros_like(sums)
        clear_margins(slope, keep, hid.shape[1])

    state_back(grad_later.at[0], state_in.at[0], pre.at[0], raw.at[0], dt_raw.at[0], cum.at[0], age.at[0],
               grad_fed.at[0], grad_mix.at[0], grad_cum.at[0], grad_bc.at[0], taps, skip, heads, spread, gather, tri_up,
               grad_in, conv_sums, head_sums, step_x, open_x, from_state, fed_state, met_state, met_all, slope,
               keep)
    features_back(grad_in, grad_gate.at[0], w_in, lambda: w_z[...], grad_normed.at[0], grad_halo.at[0], wide)
    for rows, kept in ((slice(0, HALO), halo.at[0]), (slice(HALO, None), hid.at[0])):
        hidden = kept[...].astype(F32)
        norm_sums[...] += folded(wide[rows] * hidden * normalised(hidden, 1.0)[1])
    sum_w[...] += mm_tn(normed[0], grad_in[...])

    @pl.when(is_last_step())
    def _():
        grad_w[...] = sum_w[...].astype(BF16)
        conv_out[...] = to_rows([conv_sums[k] for k in range(5)])
        head_out[...] = to_rows([head_sums[0], head_sums[1]])
        norm_out[...] = to_rows([norm_sums[...]])


def finish(inner_all, hid, out_grad, stats, norm_in, own_part, other_part, own_grad, other_grad, own_tail, other_tail,
           sums_zo, sums_w, conv_sums, norm_sums, head_sums, inner_sums, gather,
           out, in_grad, grad_wz, grad_wx, grad_wbc, grad_wdt, grad_wo, grad_conv_x, grad_conv_bc, grad_dt_bias,
           grad_a_log, grad_skip, grad_norm_gate, grad_norm_in, total):
    length = hid.shape[1]
    gain = norm_in[...].reshape(1, -1)
    for i in range(hid.shape[0]):

        def added(own, others, rows, i=i):
            found = own[i, rows].astype(F32)
            for k in range(others.shape[0]):
                found = found + others[k, i, rows].astype(F32)
            return found

        total[...] = added(own_grad, other_grad, slice(None))
        total[length - HALO :] += added(own_tail, other_tail, slice(None))
        scales = lax.rsqrt(stats[i].T[:, :1] / inner_all + EPSILON)
        for at in range(0, length, 64):
            rows = slice(at, at + 64)
            hidden = hid[i, rows].astype(F32)
            out[i, rows] = (hidden + scales[rows] * added(own_part, other_part, rows)).astype(BF16)
            scale = normalised(hidden, 1.0)[1]
            weighted = total[rows] * gain
            inner_mean = jnp.mean(weighted * hidden, -1, keepdims=True)
            in_grad[i, rows] = (
                out_grad[i, rows].astype(F32) + scale * weighted - hidden * (scale * scale * scale * inner_mean)
            ).astype(BF16)

    @pl.when(is_last_step())
    def _():
        inner, own_bc, head_count = grad_wz.shape[1], grad_wbc.shape[1], grad_wdt.shape[0]
        grad_wz[...] = sums_zo[:, :inner]
        grad_wo[...] = sums_zo[:, inner:]
        grad_wbc[...] = sums_w[:, :own_bc]
        grad_wdt[...] = sums_w[:, own_bc : own_bc + LANES].T[:head_count]
        grad_wx[...] = sums_w[:, own_bc + LANES :]
        grad_conv_bc[...] = conv_sums[:5, :own_bc]
        grad_conv_x[...] = conv_sums[:5, own_bc:]
        grad_dt_bias[...] = head_sums[0:1, :head_count]
        grad_a_log[...] = head_sums[1:2, :head_count]
        grad_norm_in[...] = norm_sums[0:1].reshape(-1)
        grad_norm_gate[...] = inner_sums[0:1].reshape(-1)
        grad_skip[...] = pick(inner_sums[...], gather[...], 3)[1:2, :head_count]


def by_piece(array):
    rest = array.shape[1:]
    return pl.BlockSpec((1,) + rest, lambda i: (i,) + (0,) * len(rest))


SPAN = 2


def by_span(array):
    rest = array.shape[1:]
    return pl.BlockSpec((SPAN,) + rest, lambda i: (i,) + (0,) * len(rest))


def by_span_second(array):
    rest = array.shape[2:]
    return pl.BlockSpec((array.shape[0], SPAN) + rest, lambda i: (0, i) + (0,) * len(rest))


def fixed(array):
    return pl.BlockSpec(array.shape, lambda i: (0,) * len(array.shape))


def call(kernel, pieces, inputs, outputs, scratch, name):
    return pl.pallas_call(
        kernel,
        grid=(pieces,),
        in_specs=[cut(array) for array, cut in inputs],
        out_specs=[cut(shape) for shape, cut in outputs],
        out_shape=[shape for shape, _ in outputs],
        scratch_shapes=[pltpu.VMEM(shape, kind) for shape, kind in scratch],
        compiler_params=pltpu.CompilerParams(vmem_limit_bytes=VMEM_BYTES),
        name=name,
    )(*[array for array, _ in inputs])


def shaped(kind, *dims):
    return jax.ShapeDtypeStruct(dims, kind)


MESH = pl.DeviceIdType.MESH
UP, DOWN, NEXT_X, NEXT_Y = range(4)


def coordinates():
    return lax.axis_index("shard"), lax.axis_index("context"), lax.axis_index("tensor")


def greet(partners):
    barrier = pltpu.get_barrier_semaphore()
    count = 0
    for there, device in partners:
        if there is True:
            pl.semaphore_signal(barrier, inc=1, device_id=device, device_id_type=MESH)
            count = count + 1
        else:
            pl.when(there)(
                functools.partial(pl.semaphore_signal, barrier, inc=1, device_id=device, device_id_type=MESH)
            )
            count = count + there.astype(jnp.int32)
    pl.semaphore_wait(barrier, count)


def neighbours(place):
    shard, context, _ = place
    count = lax.axis_size("context")
    return [
        (context + 1 < count, {"context": context + 1}),
        (context > 0, {"context": context - 1}),
        (True, {"shard": shard ^ 1}),
        (True, {"shard": shard ^ 2}),
    ]


def gather_step(step, start, arrived, stage, out, received):
    place = shard, context, _ = coordinates()
    count = lax.axis_size("context")
    up, down, next_x, next_y = neighbours(place)
    mine, beside_x, beside_y, across = [(shard ^ k) * count for k in (0, 1, 2, 3)]

    def pass_on(number, source, slot, to, there=True):
        if to[0] is not True:
            there = to[0] if there is True else there & to[0]
        start(number, source, out(slot), received.at[slot], to[1], there)

    def both_ways(distance):
        found = [(context - distance, context >= distance, up),
                 (context + distance, context + distance < count, down)]
        return [(jnp.clip(at, 0, count - 1), there, to) for at, there, to in found[: 2 if distance else 1]]

    if step == 0:
        for k, to in enumerate((up, down, next_x, next_y)):
            pass_on(k, stage, mine + context, to)
    elif step < count:
        for k, (at, there, to) in enumerate(both_ways(step)):
            slot = mine + at
            arrived(out(slot), received.at[slot], there)
            for m, target in enumerate((to, next_x, next_y)):
                pass_on(4 + (step - 1) * 6 + k * 3 + m, out(slot), slot, target, there)
    elif step < 2 * count:
        for k, (at, there, _) in enumerate(both_ways(step - count)):
            number = 4 + (count - 1) * 6 + (step - count) * 4 + k * 2
            slot_x, slot_y = beside_x + at, beside_y + at
            arrived(out(slot_x), received.at[slot_x], there)
            pass_on(number, out(slot_x), slot_x, next_y, there & (at < count // 2))
            arrived(out(slot_y), received.at[slot_y], there)
            pass_on(number + 1, out(slot_y), slot_y, next_x, there & (at >= count // 2))
    else:
        for at in range(count):
            arrived(out(across + at), received.at[across + at], True)


def gather_steps():
    return 2 * lax.axis_size("context") + 1


GATHER_COPIES = 40


class Numbered:
    def __init__(self, send):
        self.send = send

    def copy(self, number, source, target, received, device):
        return pltpu.make_async_remote_copy(
            src_ref=source, dst_ref=target, send_sem=self.send.at[number], recv_sem=received,
            device_id=device, device_id_type=MESH,
        )

    def when(self, there, action):
        if there is True:
            action()
        else:
            pl.when(there)(action)

    def start(self, number, source, target, received, device, there=True):
        self.when(there, self.copy(number, source, target, received, device).start)

    def sent(self, number, source, target, received, device, there=True):
        self.when(there, self.copy(number, source, target, received, device).wait_send)

    def arrived(self, target, received, there=True):
        other = {"tensor": 1 - lax.axis_index("tensor")}
        self.when(there, self.copy(0, target, target, received, other).wait_recv)

    def nothing(self, *_):
        pass


def scatter_scratch(rows, width):
    return [pltpu.VMEM((4, rows, width), BF16) for _ in range(4)] + [DMA((4, 4)), DMA((SCATTER_COPIES,))]


SCATTER_COPIES = 16


def scatter_steps():
    return 2 + lax.axis_size("context") // 2 + lax.axis_size("context")


def scatter_step(step, start, arrived, blocks, out, first, from_x, from_y, along, received, add=True):
    shard, context, _ = coordinates()
    count = lax.axis_size("context")
    half = count // 2
    _, _, next_x, next_y = neighbours(coordinates())
    mine, beside_x, beside_y, across = [(shard ^ k) * count for k in (0, 1, 2, 3)]
    if step == 0:
        for k in range(count):
            start(k, blocks.at[across + k], first.at[k], received.at[0, k], (next_y if k < half else next_x)[1], True)
        for k in (0, count - 1, *range(1, count - 1)):
            beside, target, row, to = (beside_y, from_y, 2, next_y) if k < half else (beside_x, from_x, 1, next_x)
            start(count + k, blocks.at[beside + k], target.at[k], received.at[row, k], to[1], True)
    elif step <= half:
        for k in (step - 1, count - step):
            beside, target, row, to = (beside_x, from_x, 1, next_x) if k < half else (beside_y, from_y, 2, next_y)
            arrived(first.at[k], received.at[0, k], True)
            if add:
                blocks[beside + k] = (blocks[beside + k].astype(F32) + first[k].astype(F32)).astype(BF16)
            start(2 * count + k, blocks.at[beside + k], target.at[k], received.at[row, k], to[1], True)
    elif step <= half + count:
        at = step - half - 1
        k = at // 2 if at % 2 == 0 else count - 1 - at // 2
        arrived(from_x.at[k], received.at[1, k], True)
        arrived(from_y.at[k], received.at[2, k], True)
        if add:
            found = blocks[mine + k].astype(F32) + from_x[k].astype(F32) + from_y[k].astype(F32)
            blocks[mine + k] = found.astype(BF16)

            @pl.when(context == k)
            def _():
                out[...] = found

        there = context != k
        start(3 * count + k, blocks.at[mine + k], along.at[context], received.at[3, context], {"context": k}, there)
    else:
        for k in range(count):

            @pl.when(context != k)
            def _(k=k):
                arrived(along.at[k], received.at[3, k], True)
                out[...] += along[k].astype(F32)


GATHER_TURNS = (0, 0, 1, 3, 2, 4, 6, 8, 10)
OUTER_TURNS = (24, 28, 29, 33, 33, 34, 34, 38)
OUTER_END = 39
SMALL_TURNS = (5, 6, 7)
UP_TURNS = ((4, 6, 8, 11, 14, 16, 18, 19), (7, 10, 12, 15, 17, 18, 20, 21))
DOWN_TURNS = ((20, 21, 22, 23, 24, 26, 28, 30), (22, 23, 24, 25, 27, 29, 31, 33))


def block(inner_all, out_grad, hid_all, doc_start, w_bc, w_dt_t, w_x, conv_bc, conv_x, norm_in_all, norm_gate_all,
          dt_bias, a_log, skip_d, w_z, w_out_t, spread, gather, tri, tri_up,
          stats_out, sums_zo, sums_w, conv_out, norm_out, head_out, inner_out, own_part, other_part, own_grad,
          other_grad, own_tail, other_tail,
          halo, ages, age_lanes, vectors, w_in, taps, heads, stage_w, dt_rows, out_grad_last,
          normed, pre, cum, gates, near, inputs, state_in, leaving, arrived, decay, both, grad_bc, grad_cum, sum_all,
          stage_in, stage, half_out, half_in, carried, step_x, low_a, low_b, low_c, slope, keep, wide, seg, pair,
          grad_pair, step_raw, tails, stats, stats_in, small, seen, conv_sums, head_sums, norm_sums,
          inner_sums,
          send_w, received_w, others_sent, others, send_in, received, states_up, states_down, send, got, grad_send, grad_got, stats_send, stats_got,
          part_send, part_got, stores, tail_send, tail_got, *buffers):
    outer, last_ones = buffers[:6], buffers[6:]
    shard, context, tensor = coordinates()
    phase, i = pl.program_id(0), pl.program_id(1)
    pieces = pl.num_programs(1)
    turn = phase * pieces + i
    count = lax.axis_size("context")
    length = hid_all.shape[1]
    model, inner = sum_all.shape[0], w_z.shape[1]
    in_width, channels = w_in.shape[1], taps.shape[1]
    lead = HALO + length
    bc_width = 2 * LANES
    own_bc = bc_width // 2
    rows = stage.shape[1]
    partner = {"tensor": 1 - tensor}
    below, above = context > 0, context < count - 1
    cols = pl.ds(pl.multiple_of(tensor * own_bc, LANES), own_bc)
    other_cols = pl.ds(pl.multiple_of((1 - tensor) * own_bc, LANES), own_bc)
    norm_in, norm_gate, skip = [vectors.at[k : k + 1] for k in range(3)]
    numbered, misc = Numbered(send_in), Numbered(send)
    act, features = wide.at[:length], wide.at[:, :model]

    def piece(array, k=i):
        return array.at[k]

    def link(number, source, target, device):
        return misc.copy(number, source, target, got.at[number], device)

    def half_link():
        return link(0, half_out, half_in, partner)

    def tail_link(k):
        return pltpu.make_async_remote_copy(
            src_ref=tails.at[k], dst_ref=own_tail.at[k], send_sem=tail_send.at[0, k], recv_sem=tail_got.at[0, k],
            device_id={"context": context - 1}, device_id_type=MESH,
        )

    def tail_partner_link(k):
        return to_partner(own_tail.at[k], other_tail.at[0, k], tail_send.at[1, k], tail_got.at[1, k])

    def tail_blanks(k):
        targets = (own_tail.at[k], other_tail.at[0, k])
        return [pltpu.make_async_copy(arrived.at[k, :HALO], target, tail_got.at[n, k]) for n, target in enumerate(targets)]

    def small_link(k):
        to = [partner, {"shard": shard ^ 1}, {"shard": shard ^ 2}, {"context": context ^ 1}, {"context": context ^ 2}]
        return link(3 + k, small.at[k], seen.at[k], to[k])

    def to_partner(source, target, sent, arrives):
        return pltpu.make_async_remote_copy(
            src_ref=source, dst_ref=target, send_sem=sent, recv_sem=arrives, device_id=partner, device_id_type=MESH
        )

    def stats_link(k):
        return to_partner(stats.at[k], stats_in.at[k], stats_send.at[k], stats_got.at[k])

    def part_link(k):
        return to_partner(low_c, other_part.at[0, k], part_send.at[k], part_got.at[k])

    def part_store(k):
        return pltpu.make_async_copy(low_c, own_part.at[k], stores.at[0, k])

    def grad_link(k):
        return to_partner(gates.at[k, :, :inner], other_grad.at[0, k], grad_send.at[k], grad_got.at[k])

    def grad_store(k):
        return pltpu.make_async_copy(gates.at[k, :, :inner], own_grad.at[k], stores.at[1, k])

    def passed(c, target, semaphores, by):
        return pltpu.make_async_remote_copy(
            src_ref=leaving.at[c], dst_ref=target.at[c], send_sem=semaphores.at[1, c], recv_sem=semaphores.at[0, c],
            device_id={"context": context + by}, device_id_type=MESH,
        )

    def up(c):
        return passed(c, state_in, states_up, 1)

    def down(c):
        return passed(c, arrived, states_down, -1)

    def pass_on(c, target, copy):
        copy.wait_recv()
        leaving[c] = (decay[c, :1] * target[c].astype(F32) + leaving[c].astype(F32)).astype(BF16)
        copy.start()

    def step_sizes(k):
        return mm(normed[k, HALO:], w_in[:, bc_width : bc_width + LANES])

    def age_of(k):
        return age_lanes.at[k]

    middle = below & above
    hops = count - 1 - context

    def fetch_features(k):
        return pltpu.make_async_copy(hid_all.at[k], gates.at[k, :, :model], stores.at[0, k])

    def w_in_block(slot):
        return w_in.at[pl.ds(pl.multiple_of(slot * rows, HALO), rows)]

    def both_block(slot):
        return both.at[slot]

    @pl.when(turn == 0)
    def _():
        for k in range(pieces_of(gates)):
            fetch_features(k).start()
        head_count = w_dt_t.shape[0]
        dt_rows[...] = jnp.zeros_like(dt_rows)
        for copy in range(3):
            dt_rows[copy * SLOTS : copy * SLOTS + head_count] = w_dt_t[...].astype(F32)
        stage_w[:, bc_width : bc_width + LANES] = dt_rows[...].T.astype(BF16)
        stage_w[:, bc_width + LANES :] = w_x[...]
        stage_w[:, cols] = w_bc[...]
        taps[...] = jnp.zeros_like(taps)
        taps[:5, cols] = conv_bc[...]
        taps[:5, bc_width:] = conv_x[...]
        greet([(True, partner), (True, {"shard": shard ^ 1}), (True, {"shard": shard ^ 2})]
              + [(True, {"context": context ^ k}) for k in range(1, count)])
        first_links = Numbered(others_sent)
        tail = pl.ds(length - HALO, HALO)
        first_copies = [(0, stage_w.at[:, cols], stage_w.at[:, cols], others.at[0], partner, True),
                        (1, taps.at[:, cols], taps.at[:, cols], others.at[1], partner, True),
                        (2, hid_all.at[:, tail], halo, others.at[2], {"context": context + 1}, above)]
        for copy in first_copies:
            first_links.start(*copy)
        first_links.arrived(stage_w.at[:, other_cols], others.at[0])
        half = in_width // 2 // LANES * LANES
        halves = []
        for k, cut in enumerate((slice(0, half), slice(half, in_width))):
            to = functools.partial(lambda slot, cut: w_in_block(slot).at[:, cut], cut=cut)
            halves.append((Numbered(send_w.at[k]), stage_w.at[:, cut], to, received_w.at[k]))
        for numbered_w, *refs in halves:
            gather_step(0, numbered_w.start, numbered_w.arrived, *refs)
        stage_in[:, :inner] = w_z[...]
        stage_in[:, inner:] = w_out_t[...]
        gather_step(0, numbered.start, numbered.arrived, stage_in, both_block, received)
        w_in_block(shard * count + context)[...] = stage_w[...]
        both[shard * count + context] = stage_in[...]
        lane = lax.broadcasted_iota(jnp.int32, (1, LANES), 1)
        slot = jnp.where(lane < 3 * SLOTS, lane % SLOTS, -1)
        lane_x = lax.broadcasted_iota(jnp.int32, (1, inner), 1)
        head_rows = [jnp.zeros((1, LANES), F32) for _ in range(8)]
        skips = jnp.zeros((1, inner), F32)
        for head in range(head_count):
            head_rows[0] = jnp.where(slot == head, dt_bias[head], head_rows[0])
            head_rows[1] = jnp.where(slot == head, a_log[head], head_rows[1])
            skips = jnp.where(lane_x // HEAD == head, skip_d[head], skips)
        heads[...] = jnp.concatenate(head_rows, 0)
        vectors[0:1] = norm_in_all[...].reshape(1, -1)
        vectors[1:2] = norm_gate_all[...].reshape(1, -1)
        vectors[2:3] = skips
        position = context * length + lax.broadcasted_iota(jnp.int32, (1, length), 1)
        for k in range(pieces_of(gates)):
            at = divmod(k, doc_start.shape[1])
            age = (position - doc_start[at[0], at[1] : at[1] + 1]).astype(F32)
            ages[k] = jnp.broadcast_to(age, (8, length))
        for k in range(pieces_of(gates)):
            fetch_features(k).wait()

        def one(k, carry):
            normalise(gates.at[k, :, :model], norm_in, normed.at[k, HALO:])
            return carry

        lax.fori_loop(0, pieces_of(gates), one, 0)
        for step in range(1, gather_steps()):
            for numbered_w, *refs in halves:
                gather_step(step, numbered_w.start, numbered_w.arrived, *refs)
        for step in range(gather_steps()):
            for numbered_w, *refs in halves:
                gather_step(step, numbered_w.sent, numbered_w.nothing, *refs)
        first_links.arrived(taps.at[:, other_cols], others.at[1])
        first_links.arrived(halo, others.at[2], below)
        for copy in first_copies:
            first_links.sent(*copy)

        @pl.when(jnp.logical_not(below))
        def _():
            halo[...] = jnp.zeros_like(halo)

        for sums in (sum_all, conv_sums, head_sums, norm_sums, inner_sums):
            sums[...] = jnp.zeros_like(sums)

    for c in range(len(UP_TURNS[0])):

        @pl.when((turn == jnp.where(context == 1, UP_TURNS[0][c], UP_TURNS[1][c])) & middle)
        def _(c=c):
            pass_on(c, state_in, up(c))

        @pl.when((turn == jnp.where(hops == 1, DOWN_TURNS[0][c], DOWN_TURNS[1][c])) & middle)
        def _(c=c):
            pass_on(c, arrived, down(c))

    @pl.when(phase == 0)
    def _():
        age_lanes[i] = jnp.broadcast_to(ages[i].T[:, :1], (length, LANES))
        age = age_of(i)
        normalise(halo.at[i], norm_in, normed.at[i, :HALO])
        project(age, w_in, taps, heads, spread, tri, normed.at[i], inputs.at[i],
                pre.at[i], step_raw, cum.at[i], leaving.at[i], decay.at[i], act, keep.at[:, :length], slope.at[:lead])

        @pl.when(jnp.logical_not(below))
        def _():
            state_in[i] = jnp.zeros(state_in.shape[1:], BF16)
            up(i).start()

    @pl.when(turn < 2 * pieces)
    def _():
        for step in range(1, gather_steps()):

            @pl.when(turn == GATHER_TURNS[step])
            def _(step=step):
                gather_step(step, numbered.start, numbered.arrived, stage_in, both_block, received)

        @pl.when(turn == 2 * pieces - 1)
        def _():
            for step in range(gather_steps()):
                gather_step(step, numbered.sent, numbered.nothing, stage_in, both_block, received)

    def w_z_all():
        return both[:, :, :inner].reshape(-1, inner)

    def w_out_all():
        return both[:, :, inner:].reshape(-1, inner)

    def gate_parts(k):
        return gates.at[k, :, :inner], gates.at[k, :, inner:]

    @pl.when(phase == 1)
    def _():
        mix_within(pre.at[i], step_sizes(i), cum.at[i], age_of(i), skip, heads, spread, near.at[i], seg, pair, step_x)

    @pl.when(phase == 2)
    def _():
        gate_products(normed.at[i], out_grad.at[0], w_z_all, w_out_all, *gate_parts(i))

        @pl.when(jnp.logical_not(above))
        def _():
            up(i).wait_recv()

        @pl.when(i >= 1)
        def _():
            part_link(i - 1).wait_send()
            part_store(i - 1).wait()

        mix_states(pre.at[i], cum.at[i], age_of(i), state_in.at[i], near.at[i], *gate_parts(i), w_out_all, norm_gate, spread,
                   near.at[i], low_c, stats.at[i], carried, low_a)
        stats_link(i).start()
        part_link(i).start()
        part_store(i).start()

        @pl.when(above)
        def _():
            up(i).wait_send()

    @pl.when((turn > 2 * pieces) & (turn <= 3 * pieces))
    def _():
        k = turn - 2 * pieces - 1
        stats_link(k).wait_recv()
        stats_out[k] = stats[k] + stats_in[k]
        gate, grad_gn = gate_parts(k)
        gate_back(inner_all, near.at[k], gate, grad_gn, stats_out.at[k], pre.at[k], cum.at[k], age_of(k), state_in.at[k],
                  normed.at[k], out_grad_last, norm_gate, spread, grad_gn, gate, grad_bc.at[k, :, LANES:],
                  leaving.at[k], inner_sums, sum_all.at[:, :inner], sum_all.at[:, inner:], carried, low_a, low_b)

        @pl.when(jnp.logical_not(above))
        def _():
            arrived[k] = jnp.zeros(arrived.shape[1:], BF16)
            down(k).start()

    @pl.when(phase == 2)
    def _():
        out_grad_last[...] = out_grad[0]

    @pl.when(turn == 3 * pieces)
    def _():
        part_link(pieces - 1).wait_send()
        part_store(pieces - 1).wait()
        gain_back(w_z_all(), sum_all.at[:, :inner], norm_sums)
        stage[...] = sum_all[...].reshape(stage.shape).astype(BF16)

    outer_links = Numbered(outer[5])

    @pl.when((turn >= OUTER_TURNS[0]) & (turn <= OUTER_END))
    def _():
        for step, when in enumerate(OUTER_TURNS):

            @pl.when(turn == when)
            def _(step=step):
                scatter_step(step, outer_links.start, outer_links.arrived, stage, sums_zo, *outer[:5])

        @pl.when(turn == OUTER_END)
        def _():
            for step in range(scatter_steps() - 1):
                scatter_step(step, outer_links.sent, outer_links.nothing, stage, sums_zo, *outer[:5], add=False)

    @pl.when(phase == 3)
    def _():
        within_back(near.at[i], pre.at[i], step_sizes(i), cum.at[i], ages.at[i], gates.at[i, :, inner:], skip, heads, spread, gather,
                    near.at[i], grad_cum.at[i], grad_bc.at[i], inner_sums, seg, pair, grad_pair, step_x, low_a,
                    low_b)

    @pl.when(phase == 4)
    def _():
        @pl.when(i == 0)
        def _():
            sum_all[...] = jnp.zeros_like(sum_all)
            clear_margins(slope, keep, length)

        @pl.when(jnp.logical_not(below))
        def _():
            down(i).wait_recv()

        state_back(arrived.at[i], state_in.at[i], pre.at[i], inputs.at[i], step_sizes(i), cum.at[i], age_of(i), near.at[i],
                   gates.at[i, :, inner:], grad_cum.at[i], grad_bc.at[i], taps, skip, heads, spread, gather, tri_up,
                   inputs.at[i], conv_sums, head_sums, step_x, carried, wide.at[:length, :inner], low_a, low_b, low_c,
                   slope, keep)
        sum_all[:, :in_width] += mm_tn(normed[i, HALO:], inputs[i, HALO:])

        @pl.when(below)
        def _():
            down(i).wait_send()

    last_stage = stage.at[:, :, : in_width - own_bc]
    last_links = Numbered(last_ones[5])

    def last_step(step):
        scatter_step(step, last_links.start, last_links.arrived, last_stage, sums_w, *last_ones[:5])

    @pl.when(turn == 5 * pieces - 1)
    def _():
        small[0] = to_rows([conv_sums[k] for k in range(5)])
        small[0, 5:6, model : model + LANES] = jnp.sum(head_sums[0], 0, keepdims=True)
        small[0, 5:6, model + LANES :] = jnp.sum(head_sums[1], 0, keepdims=True)
        small[0, 6:8, :inner] = to_rows([inner_sums[0], inner_sums[1]])[:2]
        small[0, 6:8, inner:] = jnp.zeros((2, channels - inner), F32)
        sum_all[:, :in_width] += mm_tn(
            normed[:, :HALO].reshape(-1, model), inputs[:, :HALO].reshape(-1, in_width)
        )
        half_out[...] = sum_all[:, other_cols].reshape(half_out.shape).astype(BF16)
        half_link().start()
        stage[:, :, own_bc : in_width - own_bc] = (
            sum_all[:, bc_width:in_width].reshape(16, rows, in_width - bc_width).astype(BF16)
        )
        gain_back(w_in, sum_all, norm_sums)
        small[0, 5:6, :model] = jnp.sum(norm_sums[...], 0, keepdims=True) / norm_in[...]
        small_link(0).start()

    def small_step(k):
        row = lax.broadcasted_iota(jnp.int32, small.shape[1:], 0)
        lane = lax.broadcasted_iota(jnp.int32, small.shape[1:], 1)
        shared = ((row < 5) & (lane < bc_width)) | ((row == 5) & (lane < model))
        small_link(k).wait_recv()
        small[k + 1] = small[k] + (jnp.where(shared, seen[k], 0.0) if k == 0 else seen[k])
        if k < 4:
            small_link(k + 1).start()

    for k, at in enumerate(SMALL_TURNS):
        pl.when(turn == 5 * pieces + at)(functools.partial(small_step, k))

    @pl.when(phase == 5)
    def _():
        features_back(inputs.at[i], gates.at[i, :, :inner], w_in, w_z_all, gates.at[i, :, :inner], tails.at[i], features)
        grad_link(i).start()
        grad_store(i).start()
        pl.when(below)(tail_link(i).start)

        @pl.when(jnp.logical_not(above))
        def _():
            for copy in tail_blanks(i):
                copy.start()

        @pl.when(above & (i >= 2))
        def _():
            tail_link(i - 2).wait_recv()
            tail_partner_link(i - 2).start()

        @pl.when(i == 0)
        def _():
            half_link().wait_recv()
            own_half = sum_all[:, cols].reshape(half_in.shape) + half_in[...].astype(F32)
            stage[:, :, :own_bc] = own_half.astype(BF16)
            last_step(0)

        @pl.when(i == 4)
        def _():
            last_step(1)

        @pl.when(i == 5)
        def _():
            last_step(2)

    @pl.when(turn == 6 * pieces - 1)
    def _():
        for k in (pieces_of(gates) - 2, pieces_of(gates) - 1):

            @pl.when(above)
            def _(k=k):
                tail_link(k).wait_recv()
                tail_partner_link(k).start()

        for step in range(3, scatter_steps()):
            last_step(step)
            if step in (5, 6):
                small_step(step - 2)
        total = small.at[5]
        conv_out[:, :own_bc] = total[:, cols]
        conv_out[:, own_bc:] = total[:, bc_width:]
        norm_out[...] = jnp.broadcast_to(total[5:6, :model], norm_out.shape)
        head_out[...] = jnp.zeros_like(head_out)
        head_out[0:1] = total[5:6, model : model + LANES]
        head_out[1:2] = total[5:6, model + LANES : model + 2 * LANES]
        inner_out[...] = jnp.zeros_like(inner_out)
        inner_out[0:2] = total[6:8, :inner]
        for k in range(pieces_of(gates)):

            @pl.when(above)
            def _(k=k):
                tail_partner_link(k).wait_recv()
                tail_partner_link(k).wait_send()

            @pl.when(jnp.logical_not(above))
            def _(k=k):
                for copy in tail_blanks(k):
                    copy.wait()

            pl.when(below)(tail_link(k).wait_send)
            grad_link(k).wait_recv()
            grad_link(k).wait_send()
            grad_store(k).wait()
            part_link(k).wait_recv()
            stats_link(k).wait_send()
        half_link().wait_send()
        for k in range(5):
            small_link(k).wait_send()
        for step in range(scatter_steps() - 1):
            scatter_step(step, last_links.sent, last_links.nothing, last_stage, sums_w, *last_ones[:5], add=False)


def pieces_of(array):
    return array.shape[0]


ANY = pl.BlockSpec(memory_space=pl.ANY)
IN_VMEM = pl.BlockSpec(memory_space=pltpu.VMEM)
DMA = pltpu.SemaphoreType.DMA


def gather_rows(rows):
    return lax.all_gather(rows, ("shard", "context"), axis=0, tiled=True)


def scatter_rows(rows):
    return lax.psum_scatter(rows.astype(F32), ("shard", "context"), scatter_dimension=0, tiled=True)


def passed_along(value, by):
    length = lax.axis_size("context")
    return lax.ppermute(value, "context", [(i, i + by) for i in range(length) if 0 <= i + by < length])


def chain(local, decay, by):
    arrived = jnp.zeros_like(local)
    for _ in range(lax.axis_size("context") - 1):
        leaving = decay[:, :1] * arrived.astype(F32) + local.astype(F32)
        arrived = passed_along(leaving.astype(BF16), by)
    return arrived


def exchange(value):
    everything = lax.all_gather(value, "tensor")
    return everything[0], everything[1:]


def part_of(width, at):
    return lambda array: pl.BlockSpec((array.shape[0], width), lambda i: (0, at))


class AnyMesh:
    def prepare(self, hid, doc_start, norm_in, norm_gate, dt_bias, a_log, skip_d, w_bc, w_dt, w_x, conv_bc, conv_x):
        pieces, length, _ = hid.shape
        head_count = w_dt.shape[1]

        def head_row(row):
            return jnp.pad(jnp.tile(jnp.pad(row, (0, SLOTS - head_count)), 3), (0, LANES - 3 * SLOTS))

        heads = jnp.stack([head_row(dt_bias), head_row(a_log)] + [jnp.zeros((LANES,), F32)] * 6)
        vectors = (norm_in[None], norm_gate[None], jnp.repeat(skip_d, HEAD)[None])
        position = lax.axis_index("context") * length + jnp.arange(length, dtype=jnp.int32)
        ages = (position - doc_start.reshape(pieces, length)).astype(F32)
        age = jnp.broadcast_to(ages[:, :, None], (pieces, length, LANES))
        age_row = jnp.broadcast_to(ages[:, None, :], (pieces, 8, length))
        conv_bc_all = lax.all_gather(conv_bc, "tensor", axis=1, tiled=True)
        taps = jnp.pad(jnp.concatenate([conv_bc_all, conv_x], 1), ((0, 3), (0, 0)))
        w_bc_all = lax.all_gather(w_bc, "tensor", axis=1, tiled=True)
        w_dt_wide = jnp.pad(jnp.tile(jnp.pad(w_dt, ((0, 0), (0, SLOTS - w_dt.shape[1]))), (1, 3)), ((0, 0), (0, LANES - 3 * SLOTS)))
        w_in = gather_rows(jnp.concatenate([w_bc_all, w_dt_wide, w_x], 1))
        return w_in, passed_along(hid[:, length - HALO :], 1), taps, heads, vectors, (age, age_row)

    def forward(self, hid, seed, prepared, w_z, w_out, spread, tri):
        w_in, halo, taps, heads, (norm_in, norm_gate, skip), (age, _) = prepared
        pieces, length, model = hid.shape
        inner, channels = w_z.shape[1], taps.shape[1]
        token = functools.partial(shaped, F32, pieces, length)
        token_low = functools.partial(shaped, BF16, pieces, length)
        normed, raw, pre, dt_raw, cum, local, decay = call(
            forward_local, pieces,
            [(hid, by_piece), (halo, by_piece), (age, by_piece), (norm_in, fixed), (w_in, fixed), (taps, fixed),
             (heads, fixed), (spread, fixed), (tri, fixed)],
            [(shaped(BF16, pieces, HALO + length, model), by_piece),
             (shaped(BF16, pieces, HALO + length, w_in.shape[1]), by_piece), (token_low(channels), by_piece),
             (token(LANES), by_piece), (token(LANES), by_piece), (shaped(BF16, pieces, LANES, inner), by_piece),
             (shaped(F32, pieces, 8, inner), by_piece)],
            [((length, channels), F32), ((3, length, LANES), F32), ((HALO + length, channels), F32)], "forward_local",
        )
        state_in = chain(local, decay, 1)
        w_z_all, w_out_t = gather_rows(w_z), gather_rows(w_out.T)
        square = ((length, length), F32)
        token_wide = ((length, inner), F32)
        mixer, gate, grad_gn, part, stats = call(
            forward_mix, pieces,
            [(pre, by_piece), (dt_raw, by_piece), (cum, by_piece), (age, by_piece), (state_in, by_piece),
             (normed, by_piece), (seed, by_piece), (w_z_all, fixed), (w_out_t, fixed), (norm_gate, fixed),
             (skip, fixed), (heads, fixed), (spread, fixed)],
            [(token(inner), by_piece), (token_low(inner), by_piece), (token_low(inner), by_piece),
             (token_low(model), by_piece), (shaped(F32, pieces, 8, length), by_piece)],
            [token_wide, square, square, token_wide, token_wide, ((length, inner), BF16)], "forward_mix",
        )
        return normed, raw, pre, dt_raw, cum, decay, state_in, mixer, gate, grad_gn, part, stats, (w_z_all, fixed)

    def backward(self, inner_all, hid, seed, prepared, saved, own_bc, spread, gather, tri_up):
        w_in, halo, taps, heads, (norm_in, norm_gate, skip), (age, age_row) = prepared
        normed, raw, pre, dt_raw, cum, decay, state_in, mixer, gate, grad_gn, part, stats, w_z_all = saved
        pieces, length, model = hid.shape
        inner, channels, in_width, lead = mixer.shape[2], taps.shape[1], w_in.shape[1], HALO + length
        token = functools.partial(shaped, F32, pieces, length)
        token_low = functools.partial(shaped, BF16, pieces, length)
        square, token_wide, token_narrow = ((length, length), F32), ((length, inner), F32), ((length, inner), BF16)
        stats = lax.psum(stats, "tensor")
        grad_fed, grad_mix, grad_gate, grad_cum, grad_bc, grad_state, grad_wz, grad_wo, sums = call(
            functools.partial(backward_local, inner_all), pieces,
            [(mixer, by_piece), (gate, by_piece), (grad_gn, by_piece), (stats, by_piece), (pre, by_piece),
             (dt_raw, by_piece), (cum, by_piece), (age, by_piece), (age_row, by_piece), (state_in, by_piece),
             (normed, by_piece), (seed, by_piece), (norm_gate, fixed), (skip, fixed), (heads, fixed), (spread, fixed),
             (gather, fixed)],
            [(token(inner), by_piece), (token_low(inner), by_piece), (token_low(inner), by_piece),
             (token(LANES), by_piece), (token(2 * LANES), by_piece), (shaped(BF16, pieces, LANES, inner), by_piece),
             (shaped(BF16, model, inner), fixed), (shaped(BF16, model, inner), fixed), (shaped(F32, 8, inner), fixed)],
            [((2, 8, inner), F32), ((model, inner), F32), ((model, inner), F32), square, square, square, token_wide, token_wide, token_narrow,
             token_narrow], "backward_local",
        )
        grad_later = chain(grad_state, decay, -1)
        grad_normed, grad_halo, grad_w, conv_sums, head_sums, norm_sums = call(
            backward_finish, pieces,
            [(grad_later, by_piece), (state_in, by_piece), (pre, by_piece), (raw, by_piece), (dt_raw, by_piece),
             (cum, by_piece), (age, by_piece), (grad_fed, by_piece), (grad_mix, by_piece), (grad_cum, by_piece),
             (grad_bc, by_piece), (grad_gate, by_piece), (normed, by_piece), (hid, by_piece), (halo, by_piece),
             (w_in, fixed), w_z_all, (taps, fixed), (skip, fixed), (heads, fixed), (spread, fixed), (gather, fixed),
             (tri_up, fixed)],
            [(token_low(model), by_piece), (shaped(BF16, pieces, HALO, model), by_piece),
             (shaped(BF16, model, in_width), fixed), (shaped(F32, 8, channels), fixed), (shaped(F32, 8, LANES), fixed),
             (shaped(F32, 8, model), fixed)],
            [((5, 8, channels), F32), ((2, 8, LANES), F32), ((8, model), F32), ((model, in_width), F32), token_wide,
             token_wide, token_wide, token_narrow, token_narrow, token_narrow, ((lead + 8, channels), F32), ((3, lead + 8, LANES), F32),
             ((lead, in_width), BF16), ((lead, model), F32)],
            "backward_finish",
        )
        sums_zo = jnp.concatenate([scatter_rows(grad_wz), scatter_rows(grad_wo)], 1)
        mine, bc_width = lax.axis_index("tensor"), 2 * LANES
        grad_w = scatter_rows(grad_w)
        grad_w_bc = lax.psum_scatter(grad_w[:, :bc_width], "tensor", scatter_dimension=1, tiled=True)
        norm_sums, conv_bc = lax.psum((norm_sums, conv_sums[:, :bc_width]), ("shard", "context", "tensor"))
        conv_x, head_sums, sums = lax.psum((conv_sums[:, bc_width:], head_sums, sums), ("shard", "context"))
        conv_bc = lax.dynamic_slice_in_dim(conv_bc, mine * own_bc, own_bc, 1)
        sums_w = jnp.concatenate([grad_w_bc, grad_w[:, bc_width:]], 1)
        small = (jnp.concatenate([conv_bc, conv_x], 1), norm_sums, head_sums, sums)
        return stats, sums_zo, sums_w, small, exchange(part), exchange(grad_normed), exchange(passed_along(grad_halo, -1))

    def run(self, inner_all, hid, seed, prepared, w_z, w_out, own_bc, spread, gather, tri, tri_up):
        saved = self.forward(hid, seed, prepared, w_z, w_out, spread, tri)
        return self.backward(inner_all, hid, seed, prepared, saved, own_bc, spread, gather, tri_up)


class FourByFourByTwo:
    def prepare(self, hid, *parameters):
        return parameters

    def run(self, inner_all, hid, seed, prepared, w_z, w_out, own_bc, spread, gather, tri, tri_up):
        doc_start, norm_in, norm_gate, dt_bias, a_log, skip_d, w_bc, w_dt, w_x, conv_bc, conv_x = prepared
        pieces, length, model = hid.shape
        rows, inner = w_z.shape
        channels, in_width, lead = 2 * LANES + inner, 3 * LANES + inner, HALO + length
        width = in_width - own_bc

        def gradients(p, i):
            return (jnp.where(p == 2, i, jnp.where(p < 2, 0, pieces - 1)), 0, 0)

        def block_of(where):
            return lambda array: pl.BlockSpec((1,) + array.shape[1:], where)

        def once(array):
            return pl.BlockSpec(array.shape, lambda p, i: (0,) * array.ndim, pipeline_mode=pl.Buffered(1))

        kept = once

        def anywhere(array):
            return ANY

        def vmem(kind, *dims):
            return pltpu.VMEM(dims, kind)

        token_low, tail = shaped(BF16, pieces, length, model), shaped(BF16, pieces, HALO, model)
        stats = shaped(F32, pieces, 8, length)
        def in_smem(array):
            return pl.BlockSpec(memory_space=pltpu.SMEM)

        inputs = [(seed, block_of(gradients)), (hid, anywhere), (doc_start, once), (w_bc, once),
                  (w_dt.T, once), (w_x, once), (conv_bc, once), (conv_x, once), (norm_in, once), (norm_gate, once),
                  (dt_bias, in_smem), (a_log, in_smem), (skip_d, in_smem), (w_z, once), (w_out.T, once), (spread, once),
                  (gather, once), (tri, once), (tri_up, once)]
        outputs = [(stats, kept), (shaped(F32, rows, 2 * inner), kept), (shaped(F32, rows, width), kept),
                   (shaped(F32, 8, channels - own_bc), kept), (shaped(F32, 8, model), kept), (shaped(F32, 8, LANES), kept),
                   (shaped(F32, 8, inner), kept), (token_low, anywhere), (shaped(BF16, 1, *token_low.shape), anywhere),
                   (token_low, anywhere), (shaped(BF16, 1, *token_low.shape), anywhere), (tail, anywhere),
                   (shaped(BF16, 1, *tail.shape), anywhere)]
        state, square, low = vmem(BF16, pieces, LANES, inner), vmem(F32, length, length), vmem(BF16, length, inner)
        per_piece = DMA((pieces,))
        scratch = [
            vmem(BF16, *tail.shape), vmem(F32, *stats.shape), vmem(F32, pieces, length, LANES), vmem(F32, 8, inner),
            vmem(BF16, model, in_width),
            vmem(F32, 8, channels), vmem(F32, 8, LANES), vmem(BF16, rows, in_width), vmem(F32, LANES, rows),
            vmem(BF16, length, model),
            vmem(BF16, pieces, lead, model), vmem(BF16, pieces, length, channels), vmem(F32, pieces, length, LANES),
            vmem(BF16, pieces, length, 2 * inner), vmem(F32, pieces, length, inner), vmem(BF16, pieces, lead, in_width),
            state, state, state, vmem(F32, pieces, 8, inner), vmem(BF16, 16, rows, 2 * inner),
            vmem(F32, pieces, length, 2 * LANES), vmem(F32, pieces, length, LANES), vmem(F32, model, 2 * inner),
            vmem(BF16, rows, 2 * inner), vmem(BF16, 16, rows, 2 * inner), vmem(BF16, 16, rows, own_bc),
            vmem(BF16, 16, rows, own_bc), vmem(F32, length, inner), vmem(F32, length, inner), low, low, low,
            vmem(F32, lead + 8, channels), vmem(F32, 3, lead + 8, LANES), vmem(F32, lead, channels), square, square,
            square, vmem(F32, length, LANES), vmem(BF16, *tail.shape),
            vmem(F32, *stats.shape), vmem(F32, *stats.shape), vmem(F32, 6, 8, channels),
            vmem(F32, 5, 8, channels), vmem(F32, 5, 8, channels), vmem(F32, 2, 8, LANES), vmem(F32, 8, model),
            vmem(F32, 2, 8, inner), DMA((2, GATHER_COPIES)), DMA((2, 16)), DMA((3,)), DMA((3,)), DMA((GATHER_COPIES,)),
            DMA((16,)), DMA((2, pieces)), DMA((2, pieces)), DMA((8,)),
            DMA((8,)), per_piece, per_piece, per_piece, per_piece, per_piece, per_piece, DMA((2, pieces)),
            DMA((2, pieces)), DMA((2, pieces)),
        ]
        (stats, sums_zo, sums_w, conv_sums, norm_sums, head_sums, sums, own_part, other_part, own_grad, other_grad,
         own_tail, other_tail) = pl.pallas_call(
            functools.partial(block, inner_all),
            grid=(6, pieces),
            in_specs=[cut(array) for array, cut in inputs],
            out_specs=[cut(shape) for shape, cut in outputs],
            out_shape=[shape for shape, _ in outputs],
            scratch_shapes=scratch + scatter_scratch(rows, 2 * inner) + scatter_scratch(rows, width),
            compiler_params=pltpu.CompilerParams(
                collective_id=1, has_side_effects=True, vmem_limit_bytes=BLOCK_VMEM_BYTES
            ),
            name="block",
        )(*[array for array, _ in inputs])
        small = (conv_sums, norm_sums, head_sums, sums)
        return stats, sums_zo, sums_w, small, (own_part, other_part), (own_grad, other_grad), (own_tail, other_tail)


def links():
    sizes = tuple(lax.axis_size(axis) for axis in ("shard", "context", "tensor"))
    return FourByFourByTwo() if sizes == (4, 4, 2) else AnyMesh()


def shards(inner_all, hidden_in, out_grad, doc_start, norm_in, w_z, w_x, w_bc, w_dt, conv_x, conv_bc, dt_bias, a_log,
           skip_d, norm_gate, w_out):
    micro, per_device, length, model = hidden_in.shape
    pieces = micro * per_device
    inner = w_z.shape[1]
    head_count, own_bc = w_dt.shape[1], w_bc.shape[1]

    head_of = np.arange(inner) // HEAD
    slot = np.where(np.arange(LANES) < 3 * SLOTS, np.arange(LANES) % SLOTS, -1)
    gather = jnp.asarray(head_of[:, None] == np.arange(LANES)[None], BF16)
    spread = jnp.asarray(head_of[None] == slot[:, None], BF16)
    tri = jnp.asarray(np.tril(np.ones((length, length))), BF16)
    tri_up = jnp.asarray(np.triu(np.ones((length, length))), BF16)

    hid = hidden_in.reshape(pieces, length, model)
    seed = out_grad.reshape(pieces, length, model)
    between = links()
    prepared = between.prepare(
        hid, doc_start, norm_in, norm_gate, dt_bias, a_log, skip_d, w_bc, w_dt, w_x, conv_bc, conv_x
    )
    stats, sums_zo, sums_w, small, (own_part, other_part), (own_grad, other_grad), (own_tail, other_tail) = (
        between.run(inner_all, hid, seed, prepared, w_z, w_out, own_bc, spread, gather, tri, tri_up)
    )
    token_low = functools.partial(shaped, BF16, pieces, length)
    rows = w_z.shape[0]
    outputs = [shaped(F32, rows, inner), shaped(F32, rows, inner), shaped(F32, rows, own_bc),
               shaped(F32, head_count, rows), shaped(F32, rows, inner), shaped(F32, 5, inner), shaped(F32, 5, own_bc),
               shaped(F32, 1, head_count), shaped(F32, 1, head_count), shaped(F32, 1, head_count),
               shaped(F32, inner), shaped(F32, model)]
    (out, in_grad, grad_wz, grad_wx, grad_wbc, grad_wdt, grad_wo, grad_conv_x, grad_conv_bc, grad_dt_bias, grad_a_log,
     grad_skip, grad_norm_gate, grad_norm_in) = call(
        functools.partial(finish, inner_all), pieces // SPAN,
        [(hid, by_span), (seed, by_span), (stats, by_span), (norm_in, fixed), (own_part, by_span),
         (other_part, by_span_second), (own_grad, by_span), (other_grad, by_span_second), (own_tail, by_span),
         (other_tail, by_span_second), (sums_zo, fixed), (sums_w, fixed)] + [(array, fixed) for array in small]
        + [(gather, fixed)],
        [(token_low(model), by_span), (token_low(model), by_span)] + [(shape, fixed) for shape in outputs],
        [((length, model), F32)], "finish",
    )
    return (
        out.reshape(hidden_in.shape),
        in_grad.reshape(hidden_in.shape),
        grad_norm_in,
        grad_wz,
        grad_wx,
        grad_wbc,
        grad_wdt.T,
        grad_conv_x,
        grad_conv_bc,
        grad_dt_bias[0],
        grad_a_log[0],
        grad_skip[0],
        grad_norm_gate,
        grad_wo.T,
    )


def solution(mesh):
    whole = P(None, "shard", "context", None)
    rows = P(("shard", "context"), "tensor")
    lanes = P(None, "tensor")
    heads = P("tensor")
    w_out = P("tensor", ("shard", "context"))
    inputs = (whole, whole, P(None, "shard", "context"), P(), rows, rows, rows, rows, lanes, lanes, heads, heads, heads, heads, w_out)
    outputs = (whole, whole, P(), rows, rows, rows, rows, lanes, lanes, heads, heads, heads, heads, w_out)

    def placed(*arrays):
        inner_all = arrays[4].shape[1]
        return jax.shard_map(
            functools.partial(shards, inner_all), mesh=mesh, in_specs=inputs, out_specs=outputs, check_vma=False
        )(*arrays)

    return placed
```

```python
import functools

import jax
import jax.numpy as jnp
import numpy as np
from jax import lax
from jax.experimental import pallas as pl
from jax.experimental.pallas import tpu as pltpu
from jax.sharding import PartitionSpec as P

EPSILON = 1e-05
F32, BF16 = jnp.float32, jnp.bfloat16
HEAD = 64
LANES = 128
HALO = 16
ROWS = 64
GONE = -1e30
VMEM_BYTES = 60 * 1024 * 1024
BLOCK_VMEM_BYTES = 63 * 1024 * 1024


def mm(left, right):
    return jnp.dot(left, right, preferred_element_type=F32)


def mm_nt(left, right):
    return lax.dot_general(left, right, (((1,), (1,)), ((), ())), preferred_element_type=F32)


def mm_tn(left, right):
    return lax.dot_general(left, right, (((0,), (0,)), ((), ())), preferred_element_type=F32)


def parts_of(value, count):
    parts = []
    for _ in range(count - 1):
        parts.append(value.astype(BF16))
        value = value - parts[-1].astype(F32)
    return parts + [value.astype(BF16)]


def pick(value, ones, count=2):
    return sum(mm(part, ones) for part in parts_of(value, count))


def pick_left(ones, value, count=3):
    found = mm(ones, jnp.concatenate(parts_of(value, count), 1))
    width = value.shape[1]
    return sum(found[:, k * width : (k + 1) * width] for k in range(count))


SLOTS = 16


def three_parts(value):
    high = value.astype(BF16).astype(F32)
    middle = (value - high).astype(BF16).astype(F32)
    lane = lax.broadcasted_iota(jnp.int32, value.shape, 1)
    chosen = jnp.where(lane < SLOTS, high, jnp.where(lane < 2 * SLOTS, middle, value - high - middle))
    return jnp.where(lane < 3 * SLOTS, chosen, 0.0).astype(BF16)


def to_lanes(value, ones):
    return mm(three_parts(value), ones)


def folded(value):
    return jnp.sum(value.reshape(-1, 8, value.shape[1]), 0)


def to_rows(folds):
    rows = [jnp.sum(fold, 0, keepdims=True) for fold in folds]
    return jnp.concatenate(rows + [jnp.zeros_like(rows[0])] * (8 - len(rows)), 0)


def softplus(value):
    return jnp.maximum(value, 0.0) + jnp.log1p(jnp.exp(-jnp.abs(value)))


def sigmoid(value):
    return jax.nn.sigmoid(value)


def column_blocks(width):
    return [(at, min(LANES, width - at)) for at in range(0, width, LANES)]


def row_blocks(length):
    return [(at, min(ROWS, length - at)) for at in range(0, length, ROWS)]


def row_index(length):
    return lax.broadcasted_iota(jnp.int32, (length, LANES), 0).astype(F32)


def is_first_step():
    return pl.program_id(0) == 0


def is_last_step():
    return pl.program_id(0) == pl.num_programs(0) - 1


def half_masks(width):
    lane = lax.broadcasted_iota(jnp.int32, (1, width), 1)
    return [(lane // HEAD) == k for k in range(width // HEAD)]


def normalised(hidden, gain):
    scale = lax.rsqrt(jnp.mean(hidden * hidden, -1, keepdims=True) + EPSILON)
    return hidden * scale * gain, scale


def keep_masks(age, masks):
    for lag in range(1, 4):
        masks[lag - 1] = jnp.where(age[...] >= lag, 1.0, 0.0)


def normalise(hid, norm_in, normed):
    for at in range(0, hid.shape[0], 64):
        rows = slice(at, min(at + 64, hid.shape[0]))
        normed[rows] = normalised(hid[rows].astype(F32), norm_in[...])[0].astype(BF16)


def project(age, w_in, taps, heads, spread, tri,
            normed, raw_low, pre, dt_raw, cum, local, decay, act, masks, raw):
    length, channels = act.shape[0], taps.shape[1]
    bc_width = 2 * LANES
    raw[:, :bc_width] = mm(normed[...], w_in[:, :bc_width])
    raw[:, bc_width:] = mm(normed[...], w_in[:, bc_width + LANES :])
    raw_low[:, :bc_width] = raw[:, :bc_width].astype(BF16)
    raw_low[:, bc_width + LANES :] = raw[:, bc_width:].astype(BF16)
    dt_raw[...] = mm(normed[HALO:], w_in[:, bc_width : bc_width + LANES])
    keep_masks(age, masks)
    for at, width in column_blocks(channels):
        cols = slice(at, at + width)
        running = taps[4:5, cols] + taps[0:1, cols] * raw[HALO:, cols]
        for lag in range(1, 4):
            tapped = masks[lag - 1, :, :width] * raw[HALO - lag : HALO - lag + length, cols]
            running = running + taps[lag : lag + 1, cols] * tapped
        pre[:, cols] = running.astype(BF16)
        running = pre[:, cols].astype(F32)
        act[:, cols] = running * sigmoid(running)
    step = softplus(dt_raw[...] + heads[0:1])
    total = pick_left(tri[...], -jnp.exp(heads[1:2]) * step)
    cum[...] = total
    last, age_last = total[length - 1 :], age[length - 1 :]
    open_end = row_index(length) - (length - 1) + age_last >= 0
    weight = jnp.where(open_end, jnp.exp(last - total), 0.0) * step
    weighted = (act[:, bc_width:] * to_lanes(weight, spread[...])).astype(BF16)
    local[...] = mm_tn(act[:, :LANES].astype(BF16), weighted).astype(BF16)
    kept = jnp.where(age_last > length - 1, jnp.exp(last), 0.0)
    decay[...] = to_lanes(jnp.broadcast_to(kept, (8, LANES)), spread[...])


def activated(pre):
    value = pre[...].astype(F32)
    return (value * sigmoid(value)).astype(BF16)


def wide_mask(back, age):
    age = jnp.concatenate([age] * (back.shape[1] // LANES), 1) if age.shape[0] > 1 else age
    return jnp.where((back >= 0) & (back <= age), 0.0, GONE)


def gate_products(normed, out_grad, w_z, w_out_t, gate, grad_gn):
    gate[...] = mm(normed[HALO:], w_z()).astype(BF16)
    grad_gn[...] = mm(out_grad[...], w_out_t()).astype(BF16)


def mix_within(pre, dt_raw, cum, age, skip, heads, spread, near, seg, pair, step_x):
    length, inner = near.shape
    bc_width = 2 * LANES
    pair[...] = mm_nt(activated(pre.at[:, LANES:bc_width]), activated(pre.at[:, :LANES]))
    row = lax.broadcasted_iota(jnp.int32, (length, length), 0)
    col = lax.broadcasted_iota(jnp.int32, (length, length), 1)
    back = (row - col).astype(F32)
    seg[...] = wide_mask(back, age[...])
    total = cum[...]
    total_t = cum[...].T
    step_x[...] = to_lanes(softplus(dt_raw[...] + heads[0:1]), spread[...])
    for at, width in column_blocks(inner):
        cols = slice(at, at + width)
        x_pre = pre[:, bc_width + at : bc_width + at + width].astype(F32)
        values = x_pre * sigmoid(x_pre)
        fed = (values * step_x[:, cols]).astype(BF16)
        masks = half_masks(width)
        for start in range(0, length, LANES):
            stop = start + LANES
            mixing = []
            for head in range(at // HEAD, (at + width) // HEAD):
                spread_log = total[start:stop, head : head + 1] - total_t[head : head + 1, :stop]
                mixing.append((pair[start:stop, :stop] * jnp.exp(spread_log + seg[start:stop, :stop])).astype(BF16))
            fed_to = jnp.concatenate([jnp.where(mask, fed[:stop], 0) for mask in masks], 0)
            near[start:stop, cols] = skip[:, cols] * values[start:stop] + mm(jnp.concatenate(mixing, 1), fed_to)


def mix_states(pre, cum, age, state_in, near, gate, grad_gn, w_out_t, norm_gate, spread,
               mixer, part, stats, carried, gated_low):
    length, inner = near.shape
    open_start = age[...] > row_index(length)
    carried[...] = to_lanes(jnp.where(open_start, jnp.exp(cum[...]), 0.0), spread[...])
    carried[...] = carried[...] * mm(activated(pre.at[:, LANES : 2 * LANES]), state_in[...])
    squares, products = {}, {}
    for at, width in column_blocks(inner):
        cols = slice(at, at + width)
        mixed = near[:, cols] + carried[:, cols]
        mixer[:, cols] = mixed
        raw_gate = gate[:, cols].astype(F32)
        gated = mixed * (raw_gate * sigmoid(raw_gate))
        weighted = gated * norm_gate[:, cols]
        gated_low[:, cols] = weighted.astype(BF16)
        squares[width] = squares.get(width, 0.0) + gated * gated
        products[width] = products.get(width, 0.0) + grad_gn[:, cols].astype(F32) * weighted
    part[...] = mm_nt(gated_low[...], w_out_t()).astype(BF16)
    lane = lax.broadcasted_iota(jnp.int32, (length, LANES), 1)
    squares = sum(jnp.sum(found, 1, keepdims=True) for found in squares.values())
    products = sum(jnp.sum(found, 1, keepdims=True) for found in products.values())
    columns = jnp.where(lane == 0, squares, jnp.where(lane == 1, products, 0.0))
    stats[...] = columns.T[:8]


def forward_local(hid, halo, age, norm_in, w_in, taps, heads, spread, tri,
                  normed, raw, pre, dt_raw, cum, local, decay, act, masks, raw_wide):
    normalise(halo.at[0], norm_in, normed.at[0, :HALO])
    normalise(hid.at[0], norm_in, normed.at[0, HALO:])
    project(age.at[0], w_in, taps, heads, spread, tri, normed.at[0], raw.at[0],
            pre.at[0], dt_raw.at[0], cum.at[0], local.at[0], decay.at[0], act, masks, raw_wide)


def forward_mix(pre, dt_raw, cum, age, state_in, normed, out_grad, w_z, w_out_t, norm_gate, skip, heads, spread,
                mixer, gate, grad_gn, part, stats, near, seg, pair, carried, step_x, gated_low):
    w_z_all, w_out_all = (lambda: w_z[...]), (lambda: w_out_t[...])
    gate_products(normed.at[0], out_grad.at[0], w_z_all, w_out_all, gate.at[0], grad_gn.at[0])
    mix_within(pre.at[0], dt_raw.at[0], cum.at[0], age.at[0], skip, heads, spread, near, seg, pair, step_x)
    mix_states(pre.at[0], cum.at[0], age.at[0], state_in.at[0], near, gate.at[0], grad_gn.at[0], w_out_all, norm_gate,
               spread, mixer.at[0], part.at[0], stats.at[0], carried, gated_low)


def gate_back(inner_all, mixer, gate, grad_gn, stats, pre, cum, age, state_in, normed, out_grad, norm_gate,
              spread, grad_mix, grad_gate, grad_c, grad_state, sums, sum_z, sum_o,
              carried, gated_low, from_state):
    length, inner = mixer.shape
    bc_width = 2 * LANES
    open_start = age[...] > row_index(length)
    carried[...] = to_lanes(jnp.where(open_start, jnp.exp(cum[...]), 0.0), spread[...])
    means = stats[...].T / inner_all
    scale_all = jnp.broadcast_to(lax.rsqrt(means[:, :1] + EPSILON), (length, LANES))
    pull_all = scale_all * scale_all * scale_all * jnp.broadcast_to(means[:, 1:2], (length, LANES))
    for at, width in column_blocks(inner):
        cols = slice(at, at + width)
        scale, pull = scale_all[:, :width], pull_all[:, :width]
        mixed = mixer[:, cols]
        raw_gate = gate[:, cols].astype(F32)
        logistic = sigmoid(raw_gate)
        acted = raw_gate * logistic
        gated = mixed * acted
        grad_out = grad_gn[:, cols].astype(F32)
        gated_scaled = gated * scale
        gated_low[:, cols] = (gated_scaled * norm_gate[:, cols]).astype(BF16)
        grad_gated = scale * (grad_out * norm_gate[:, cols]) - gated * pull
        grad_gate[:, cols] = (grad_gated * mixed * (logistic * (1.0 + raw_gate * (1.0 - logistic)))).astype(BF16)
        mix_low = (grad_gated * acted).astype(BF16)
        grad_mix[:, cols] = mix_low
        sums[0, :, cols] += folded(grad_out * gated_scaled)
        from_state[:, cols] = (carried[:, cols] * mix_low.astype(F32)).astype(BF16)
    grad_state[...] = mm_tn(activated(pre.at[:, LANES:bc_width]), from_state[...]).astype(BF16)
    grad_c[...] = mm_nt(from_state[...], state_in[...])
    sum_z[...] += mm_tn(normed[HALO:], grad_gate[...])
    sum_o[...] += mm_tn(out_grad[...], gated_low[...])


def within_back(mixer, pre, dt_raw, cum, age_row, grad_mix, skip, heads, spread, gather, grad_fed, grad_cum, grad_bc,
                sums, seg, pair, grad_pair, step_x, high, low):
    length, inner = grad_mix.shape
    bc_width = 2 * LANES
    readout, inputs_b = activated(pre.at[:, LANES:bc_width]), activated(pre.at[:, :LANES])
    pair[...] = mm_nt(inputs_b, readout)
    grad_pair[...] = jnp.zeros_like(grad_pair)
    row = lax.broadcasted_iota(jnp.int32, (length, length), 0)
    col = lax.broadcasted_iota(jnp.int32, (length, length), 1)
    back = (col - row).astype(F32)
    seg[...] = wide_mask(back, age_row[:1])
    total = cum[...]
    total_t = cum[...].T
    step_x[...] = to_lanes(softplus(dt_raw[...] + heads[0:1]), spread[...])
    for at, width in column_blocks(inner):
        cols = slice(at, at + width)
        x_pre = pre[:, bc_width + at : bc_width + at + width].astype(F32)
        values = x_pre * sigmoid(x_pre)
        fed = (values * step_x[:, cols]).astype(BF16)
        mix_low = grad_mix[:, cols]
        mix_wide = mix_low.astype(F32)
        kept = mix_wide * (mixer[:, cols] - skip[:, cols] * values)
        masks = half_masks(width)
        for start in range(0, length, LANES):
            stop = start + LANES
            fed_from = jnp.concatenate([jnp.where(mask, fed[start:stop], 0) for mask in masks], 0)
            grad_mixing = mm_nt(fed_from, mix_low[start:])
            total_pair = grad_pair[start:stop, start:]
            mixing = []
            for k, head in enumerate(range(at // HEAD, (at + width) // HEAD)):
                spread_log = total_t[head : head + 1, start:] - total[start:stop, head : head + 1]
                decayed = jnp.exp(spread_log + seg[start:stop, start:])
                mixing.append((pair[start:stop, start:] * decayed).astype(BF16))
                total_pair = total_pair + grad_mixing[k * LANES : (k + 1) * LANES] * decayed
            grad_pair[start:stop, start:] = total_pair
            mix_to = jnp.concatenate([jnp.where(mask, mix_low[start:], 0) for mask in masks], 0)
            grad_fed[start:stop, cols] = mm(jnp.concatenate(mixing, 1), mix_to)
        sums[1, :, cols] += folded(mix_wide * values)
        kept = kept - grad_fed[:, cols] * fed.astype(F32)
        high[:, cols] = kept.astype(BF16)
        low[:, cols] = (kept - high[:, cols].astype(F32)).astype(BF16)
    grad_cum[...] = mm(high[...], gather[...]) + mm(low[...], gather[...])
    pair_low = grad_pair[...].astype(BF16)
    grad_bc[:, :LANES] = mm(pair_low, readout)
    grad_bc[:, LANES:] += mm_tn(pair_low, inputs_b)


def state_back(grad_later, state_in, pre, raw, dt_raw, cum, age, grad_fed, grad_mix, grad_cum, grad_bc, taps, skip,
               heads, spread, gather, tri_up, grad_in, conv_sums, head_sums,
               step_x, open_x, from_state, fed_state, met_state, met_all, slope, keep):
    length, inner = grad_fed.shape
    channels = taps.shape[1]
    bc_width = 2 * LANES
    lead = HALO + length
    grad_in[:HALO, bc_width : bc_width + LANES] = jnp.zeros((HALO, LANES), BF16)
    for lag in range(1, 4):
        keep[lag - 1, HALO - lag : lead - lag] = jnp.where(age[...] >= lag, 1.0, 0.0)
    total = cum[...]
    step_raw = dt_raw[...] + heads[0:1]
    step = softplus(step_raw)
    rate = -jnp.exp(heads[1:2])
    step_x[...] = to_lanes(step, spread[...])
    last, age_last = total[length - 1 :], age[length - 1 :]
    open_end = row_index(length) - (length - 1) + age_last >= 0
    open_x[...] = to_lanes(jnp.where(open_end, jnp.exp(last - total), 0.0), spread[...])
    from_state[...] = open_x[...] * mm(activated(pre.at[:, :LANES]), grad_later[...])
    for at, width in column_blocks(inner):
        cols = slice(at, at + width)
        x_pre = pre[:, bc_width + at : bc_width + at + width].astype(F32)
        logistic = sigmoid(x_pre)
        values = x_pre * logistic
        fed = values * step_x[:, cols]
        fed_state[:, cols] = (fed * open_x[:, cols]).astype(BF16)
        arrived = from_state[:, cols]
        grad = grad_fed[:, cols] + arrived
        met_state[:, cols] = (values * arrived).astype(BF16)
        met_all[:, cols] = (values * grad).astype(BF16)
        grad_values = grad * step_x[:, cols] + skip[:, cols] * grad_mix[:, cols].astype(F32)
        slope[HALO:lead, bc_width + at : bc_width + at + width] = grad_values * (
            logistic * (1.0 + x_pre * (1.0 - logistic))
        )
    for at, extra in ((0, mm_nt(fed_state[...], grad_later[...])), (LANES, 0.0)):
        cols = slice(at, at + LANES)
        bc_pre = pre[:, cols].astype(F32)
        logistic = sigmoid(bc_pre)
        slope[HALO:lead, cols] = (grad_bc[:, cols] + extra) * (logistic * (1.0 + bc_pre * (1.0 - logistic)))
    state_sum, step_sum = mm(met_state[...], gather[...]) * step, mm(met_all[...], gather[...])
    kept = jnp.where(age_last > length - 1, jnp.exp(last), 0.0)
    met = jnp.sum(grad_later[...].astype(F32) * state_in[...].astype(F32), 0, keepdims=True)
    met = pick(jnp.broadcast_to(met, (8, inner)), gather[...], 3)[:1]
    end = met * kept + jnp.sum(state_sum, 0, keepdims=True)
    grad_a = pick_left(tri_up[...], grad_cum[...] - state_sum) + end
    head_sums[1] += folded(grad_a * rate * step)
    grad_step = (step_sum + grad_a * rate) * sigmoid(step_raw)
    head_sums[0] += folded(grad_step)
    grad_in[HALO:, bc_width : bc_width + LANES] = grad_step.astype(BF16)
    for at, width in column_blocks(channels):
        cols = slice(at, at + width)
        shifted = at if at < bc_width else at + LANES
        for top, rows in row_blocks(lead):
            here = slice(top, top + rows)
            own, fed_in = slope[here, cols], raw[here, shifted : shifted + width].astype(F32)
            total_in = taps[0:1, cols] * own
            conv_sums[0, :, cols] += folded(own * fed_in)
            conv_sums[4, :, cols] += folded(own)
            for lag in range(1, 4):
                later = keep[lag - 1, here, :width] * slope[top + lag : top + rows + lag, cols]
                conv_sums[lag, :, cols] += folded(later * fed_in)
                total_in = total_in + taps[lag : lag + 1, cols] * later
            grad_in[here, shifted : shifted + width] = total_in.astype(BF16)


def clear_margins(slope, keep, length):
    slope[:HALO] = jnp.zeros((HALO, slope.shape[1]), F32)
    slope[HALO + length :] = jnp.zeros((8, slope.shape[1]), F32)
    keep[...] = jnp.zeros_like(keep)


def features_back(grad_in, grad_gate, w_in, w_z, grad_normed, grad_halo, wide):
    wide[...] = mm_nt(grad_in[...], w_in[...])
    wide[HALO:] += mm_nt(grad_gate[...], w_z())
    grad_halo[...] = wide[:HALO].astype(BF16)
    grad_normed[...] = wide[HALO:].astype(BF16)


def gain_back(weights, gradients, sums):
    for top in range(0, weights.shape[0], 2 * LANES):
        rows = slice(top, top + 2 * LANES)
        total = 0.0
        for at, width in column_blocks(weights.shape[1]):
            cols = slice(at, at + width)
            total = total + weights[rows, cols].astype(F32) * gradients[rows, cols]
        sums[:, rows] += folded(total.T)


def backward_local(inner_all, mixer, gate, grad_gn, stats, pre, dt_raw, cum, age, age_row, state_in, normed, out_grad,
                   norm_gate, skip, heads, spread, gather,
                   grad_fed, grad_mix, grad_gate, grad_cum, grad_bc, grad_state, grad_wz, grad_wo, sums_out,
                   sums, sum_z, sum_o, seg, pair, grad_pair, carried, step_x, gated_low, from_state):
    @pl.when(is_first_step())
    def _():
        sum_z[...] = jnp.zeros_like(sum_z)
        sum_o[...] = jnp.zeros_like(sum_o)
        sums[...] = jnp.zeros_like(sums)

    gate_back(inner_all, mixer.at[0], gate.at[0], grad_gn.at[0], stats.at[0], pre.at[0], cum.at[0], age.at[0],
              state_in.at[0], normed.at[0], out_grad.at[0], norm_gate, spread, grad_mix.at[0],
              grad_gate.at[0], grad_bc.at[0, :, LANES:], grad_state.at[0], sums, sum_z, sum_o,
              carried, gated_low, from_state)
    within_back(mixer.at[0], pre.at[0], dt_raw.at[0], cum.at[0], age_row.at[0], grad_mix.at[0], skip, heads, spread,
                gather, grad_fed.at[0], grad_cum.at[0], grad_bc.at[0], sums, seg, pair, grad_pair, step_x, gated_low,
                from_state)

    @pl.when(is_last_step())
    def _():
        grad_wz[...] = sum_z[...].astype(BF16)
        grad_wo[...] = sum_o[...].astype(BF16)
        sums_out[...] = to_rows([sums[0], sums[1]])


def backward_finish(grad_later, state_in, pre, raw, dt_raw, cum, age, grad_fed, grad_mix, grad_cum, grad_bc, grad_gate,
                    normed, hid, halo, w_in, w_z, taps, skip, heads, spread, gather, tri_up,
                    grad_normed, grad_halo, grad_w, conv_out, head_out, norm_out,
                    conv_sums, head_sums, norm_sums, sum_w, step_x, open_x, from_state, fed_state, met_state, met_all,
                    slope, keep, grad_in, wide):
    @pl.when(is_first_step())
    def _():
        for sums in (sum_w, conv_sums, head_sums, norm_sums):
            sums[...] = jnp.zeros_like(sums)
        clear_margins(slope, keep, hid.shape[1])

    state_back(grad_later.at[0], state_in.at[0], pre.at[0], raw.at[0], dt_raw.at[0], cum.at[0], age.at[0],
               grad_fed.at[0], grad_mix.at[0], grad_cum.at[0], grad_bc.at[0], taps, skip, heads, spread, gather, tri_up,
               grad_in, conv_sums, head_sums, step_x, open_x, from_state, fed_state, met_state, met_all, slope,
               keep)
    features_back(grad_in, grad_gate.at[0], w_in, lambda: w_z[...], grad_normed.at[0], grad_halo.at[0], wide)
    for rows, kept in ((slice(0, HALO), halo.at[0]), (slice(HALO, None), hid.at[0])):
        hidden = kept[...].astype(F32)
        norm_sums[...] += folded(wide[rows] * hidden * normalised(hidden, 1.0)[1])
    sum_w[...] += mm_tn(normed[0], grad_in[...])

    @pl.when(is_last_step())
    def _():
        grad_w[...] = sum_w[...].astype(BF16)
        conv_out[...] = to_rows([conv_sums[k] for k in range(5)])
        head_out[...] = to_rows([head_sums[0], head_sums[1]])
        norm_out[...] = to_rows([norm_sums[...]])


def finish(inner_all, hid, out_grad, stats, norm_in, own_part, other_part, own_grad, other_grad, own_tail, other_tail,
           sums_zo, sums_w, conv_sums, norm_sums, head_sums, inner_sums, gather,
           out, in_grad, grad_wz, grad_wx, grad_wbc, grad_wdt, grad_wo, grad_conv_x, grad_conv_bc, grad_dt_bias,
           grad_a_log, grad_skip, grad_norm_gate, grad_norm_in, total):
    length = hid.shape[1]
    gain = norm_in[...].reshape(1, -1)
    for i in range(hid.shape[0]):

        def added(own, others, rows, i=i):
            found = own[i, rows].astype(F32)
            for k in range(others.shape[0]):
                found = found + others[k, i, rows].astype(F32)
            return found

        total[...] = added(own_grad, other_grad, slice(None))
        total[length - HALO :] += added(own_tail, other_tail, slice(None))
        scales = lax.rsqrt(stats[i].T[:, :1] / inner_all + EPSILON)
        for at in range(0, length, 64):
            rows = slice(at, at + 64)
            hidden = hid[i, rows].astype(F32)
            out[i, rows] = (hidden + scales[rows] * added(own_part, other_part, rows)).astype(BF16)
            scale = normalised(hidden, 1.0)[1]
            weighted = total[rows] * gain
            inner_mean = jnp.mean(weighted * hidden, -1, keepdims=True)
            in_grad[i, rows] = (
                out_grad[i, rows].astype(F32) + scale * weighted - hidden * (scale * scale * scale * inner_mean)
            ).astype(BF16)

    @pl.when(is_last_step())
    def _():
        inner, own_bc, head_count = grad_wz.shape[1], grad_wbc.shape[1], grad_wdt.shape[0]
        grad_wz[...] = sums_zo[:, :inner]
        grad_wo[...] = sums_zo[:, inner:]
        grad_wbc[...] = sums_w[:, :own_bc]
        grad_wdt[...] = sums_w[:, own_bc : own_bc + LANES].T[:head_count]
        grad_wx[...] = sums_w[:, own_bc + LANES :]
        grad_conv_bc[...] = conv_sums[:5, :own_bc]
        grad_conv_x[...] = conv_sums[:5, own_bc:]
        grad_dt_bias[...] = head_sums[0:1, :head_count]
        grad_a_log[...] = head_sums[1:2, :head_count]
        grad_norm_in[...] = norm_sums[0:1].reshape(-1)
        grad_norm_gate[...] = inner_sums[0:1].reshape(-1)
        grad_skip[...] = pick(inner_sums[...], gather[...], 3)[1:2, :head_count]


def by_piece(array):
    rest = array.shape[1:]
    return pl.BlockSpec((1,) + rest, lambda i: (i,) + (0,) * len(rest))


SPAN = 2


def by_span(array):
    rest = array.shape[1:]
    return pl.BlockSpec((SPAN,) + rest, lambda i: (i,) + (0,) * len(rest))


def by_span_second(array):
    rest = array.shape[2:]
    return pl.BlockSpec((array.shape[0], SPAN) + rest, lambda i: (0, i) + (0,) * len(rest))


def fixed(array):
    return pl.BlockSpec(array.shape, lambda i: (0,) * len(array.shape))


def call(kernel, pieces, inputs, outputs, scratch, name):
    return pl.pallas_call(
        kernel,
        grid=(pieces,),
        in_specs=[cut(array) for array, cut in inputs],
        out_specs=[cut(shape) for shape, cut in outputs],
        out_shape=[shape for shape, _ in outputs],
        scratch_shapes=[pltpu.VMEM(shape, kind) for shape, kind in scratch],
        compiler_params=pltpu.CompilerParams(vmem_limit_bytes=VMEM_BYTES),
        name=name,
    )(*[array for array, _ in inputs])


def shaped(kind, *dims):
    return jax.ShapeDtypeStruct(dims, kind)


MESH = pl.DeviceIdType.MESH
UP, DOWN, NEXT_X, NEXT_Y = range(4)


def coordinates():
    return lax.axis_index("shard"), lax.axis_index("context"), lax.axis_index("tensor")


def greet(partners):
    barrier = pltpu.get_barrier_semaphore()
    count = 0
    for there, device in partners:
        if there is True:
            pl.semaphore_signal(barrier, inc=1, device_id=device, device_id_type=MESH)
            count = count + 1
        else:
            pl.when(there)(
                functools.partial(pl.semaphore_signal, barrier, inc=1, device_id=device, device_id_type=MESH)
            )
            count = count + there.astype(jnp.int32)
    pl.semaphore_wait(barrier, count)


def neighbours(place):
    shard, context, _ = place
    count = lax.axis_size("context")
    return [
        (context + 1 < count, {"context": context + 1}),
        (context > 0, {"context": context - 1}),
        (True, {"shard": shard ^ 1}),
        (True, {"shard": shard ^ 2}),
    ]


def gather_step(step, start, arrived, stage, out, received):
    place = shard, context, _ = coordinates()
    count = lax.axis_size("context")
    up, down, next_x, next_y = neighbours(place)
    mine, beside_x, beside_y, across = [(shard ^ k) * count for k in (0, 1, 2, 3)]

    def pass_on(number, source, slot, to, there=True):
        if to[0] is not True:
            there = to[0] if there is True else there & to[0]
        start(number, source, out(slot), received.at[slot], to[1], there)

    def both_ways(distance):
        found = [(context - distance, context >= distance, up),
                 (context + distance, context + distance < count, down)]
        return [(jnp.clip(at, 0, count - 1), there, to) for at, there, to in found[: 2 if distance else 1]]

    if step == 0:
        for k, to in enumerate((up, down, next_x, next_y)):
            pass_on(k, stage, mine + context, to)
    elif step < count:
        for k, (at, there, to) in enumerate(both_ways(step)):
            slot = mine + at
            arrived(out(slot), received.at[slot], there)
            for m, target in enumerate((to, next_x, next_y)):
                pass_on(4 + (step - 1) * 6 + k * 3 + m, out(slot), slot, target, there)
    elif step < 2 * count:
        for k, (at, there, _) in enumerate(both_ways(step - count)):
            number = 4 + (count - 1) * 6 + (step - count) * 4 + k * 2
            slot_x, slot_y = beside_x + at, beside_y + at
            arrived(out(slot_x), received.at[slot_x], there)
            pass_on(number, out(slot_x), slot_x, next_y, there & (at < count // 2))
            arrived(out(slot_y), received.at[slot_y], there)
            pass_on(number + 1, out(slot_y), slot_y, next_x, there & (at >= count // 2))
    else:
        for at in range(count):
            arrived(out(across + at), received.at[across + at], True)


def gather_steps():
    return 2 * lax.axis_size("context") + 1


GATHER_COPIES = 40


class Numbered:
    def __init__(self, send):
        self.send = send

    def copy(self, number, source, target, received, device):
        return pltpu.make_async_remote_copy(
            src_ref=source, dst_ref=target, send_sem=self.send.at[number], recv_sem=received,
            device_id=device, device_id_type=MESH,
        )

    def when(self, there, action):
        if there is True:
            action()
        else:
            pl.when(there)(action)

    def start(self, number, source, target, received, device, there=True):
        self.when(there, self.copy(number, source, target, received, device).start)

    def sent(self, number, source, target, received, device, there=True):
        self.when(there, self.copy(number, source, target, received, device).wait_send)

    def arrived(self, target, received, there=True):
        other = {"tensor": 1 - lax.axis_index("tensor")}
        self.when(there, self.copy(0, target, target, received, other).wait_recv)

    def nothing(self, *_):
        pass


def scatter_scratch(rows, width):
    return [pltpu.VMEM((4, rows, width), BF16) for _ in range(4)] + [DMA((4, 4)), DMA((SCATTER_COPIES,))]


SCATTER_COPIES = 16


def scatter_steps():
    return 2 + lax.axis_size("context") // 2 + lax.axis_size("context")


def scatter_step(step, start, arrived, blocks, out, first, from_x, from_y, along, received, add=True):
    shard, context, _ = coordinates()
    count = lax.axis_size("context")
    half = count // 2
    _, _, next_x, next_y = neighbours(coordinates())
    mine, beside_x, beside_y, across = [(shard ^ k) * count for k in (0, 1, 2, 3)]
    if step == 0:
        for k in range(count):
            start(k, blocks.at[across + k], first.at[k], received.at[0, k], (next_y if k < half else next_x)[1], True)
        for k in (0, count - 1, *range(1, count - 1)):
            beside, target, row, to = (beside_y, from_y, 2, next_y) if k < half else (beside_x, from_x, 1, next_x)
            start(count + k, blocks.at[beside + k], target.at[k], received.at[row, k], to[1], True)
    elif step <= half:
        for k in (step - 1, count - step):
            beside, target, row, to = (beside_x, from_x, 1, next_x) if k < half else (beside_y, from_y, 2, next_y)
            arrived(first.at[k], received.at[0, k], True)
            if add:
                blocks[beside + k] = (blocks[beside + k].astype(F32) + first[k].astype(F32)).astype(BF16)
            start(2 * count + k, blocks.at[beside + k], target.at[k], received.at[row, k], to[1], True)
    elif step <= half + count:
        at = step - half - 1
        k = at // 2 if at % 2 == 0 else count - 1 - at // 2
        arrived(from_x.at[k], received.at[1, k], True)
        arrived(from_y.at[k], received.at[2, k], True)
        if add:
            found = blocks[mine + k].astype(F32) + from_x[k].astype(F32) + from_y[k].astype(F32)
            blocks[mine + k] = found.astype(BF16)

            @pl.when(context == k)
            def _():
                out[...] = found

        there = context != k
        start(3 * count + k, blocks.at[mine + k], along.at[context], received.at[3, context], {"context": k}, there)
    else:
        for k in range(count):

            @pl.when(context != k)
            def _(k=k):
                arrived(along.at[k], received.at[3, k], True)
                out[...] += along[k].astype(F32)


GATHER_TURNS = (0, 0, 1, 3, 2, 4, 6, 8, 10)
OUTER_TURNS = (24, 28, 29, 33, 33, 34, 34, 38)
OUTER_END = 39
SMALL_TURNS = (5, 6, 7)
UP_TURNS = ((4, 6, 8, 11, 14, 16, 18, 19), (7, 10, 12, 15, 17, 18, 20, 21))
DOWN_TURNS = ((20, 21, 22, 23, 24, 26, 28, 30), (22, 23, 24, 25, 27, 29, 31, 33))


def block(inner_all, out_grad, hid_all, doc_start, w_bc, w_dt_t, w_x, conv_bc, conv_x, norm_in_all, norm_gate_all,
          dt_bias, a_log, skip_d, w_z, w_out_t, spread, gather, tri, tri_up,
          stats_out, sums_zo, sums_w, conv_out, norm_out, head_out, inner_out, own_part, other_part, own_grad,
          other_grad, own_tail, other_tail,
          halo, ages, age_lanes, vectors, w_in, taps, heads, stage_w, dt_rows, out_grad_last,
          normed, pre, cum, gates, near, inputs, state_in, leaving, arrived, decay, both, grad_bc, grad_cum, sum_all,
          stage_in, stage, half_out, half_in, carried, step_x, low_a, low_b, low_c, slope, keep, wide, seg, pair,
          grad_pair, step_raw, tails, stats, stats_in, small, seen, conv_sums, head_sums, norm_sums,
          inner_sums,
          send_w, received_w, others_sent, others, send_in, received, states_up, states_down, send, got, grad_send, grad_got, stats_send, stats_got,
          part_send, part_got, stores, tail_send, tail_got, *buffers):
    outer, last_ones = buffers[:6], buffers[6:]
    shard, context, tensor = coordinates()
    phase, i = pl.program_id(0), pl.program_id(1)
    pieces = pl.num_programs(1)
    turn = phase * pieces + i
    count = lax.axis_size("context")
    length = hid_all.shape[1]
    model, inner = sum_all.shape[0], w_z.shape[1]
    in_width, channels = w_in.shape[1], taps.shape[1]
    lead = HALO + length
    bc_width = 2 * LANES
    own_bc = bc_width // 2
    rows = stage.shape[1]
    partner = {"tensor": 1 - tensor}
    below, above = context > 0, context < count - 1
    cols = pl.ds(pl.multiple_of(tensor * own_bc, LANES), own_bc)
    other_cols = pl.ds(pl.multiple_of((1 - tensor) * own_bc, LANES), own_bc)
    norm_in, norm_gate, skip = [vectors.at[k : k + 1] for k in range(3)]
    numbered, misc = Numbered(send_in), Numbered(send)
    act, features = wide.at[:length], wide.at[:, :model]

    def piece(array, k=i):
        return array.at[k]

    def link(number, source, target, device):
        return misc.copy(number, source, target, got.at[number], device)

    def half_link():
        return link(0, half_out, half_in, partner)

    def tail_link(k):
        return pltpu.make_async_remote_copy(
            src_ref=tails.at[k], dst_ref=own_tail.at[k], send_sem=tail_send.at[0, k], recv_sem=tail_got.at[0, k],
            device_id={"context": context - 1}, device_id_type=MESH,
        )

    def tail_partner_link(k):
        return to_partner(own_tail.at[k], other_tail.at[0, k], tail_send.at[1, k], tail_got.at[1, k])

    def tail_blanks(k):
        targets = (own_tail.at[k], other_tail.at[0, k])
        return [pltpu.make_async_copy(arrived.at[k, :HALO], target, tail_got.at[n, k]) for n, target in enumerate(targets)]

    def small_link(k):
        to = [partner, {"shard": shard ^ 1}, {"shard": shard ^ 2}, {"context": context ^ 1}, {"context": context ^ 2}]
        return link(3 + k, small.at[k], seen.at[k], to[k])

    def to_partner(source, target, sent, arrives):
        return pltpu.make_async_remote_copy(
            src_ref=source, dst_ref=target, send_sem=sent, recv_sem=arrives, device_id=partner, device_id_type=MESH
        )

    def stats_link(k):
        return to_partner(stats.at[k], stats_in.at[k], stats_send.at[k], stats_got.at[k])

    def part_link(k):
        return to_partner(low_c, other_part.at[0, k], part_send.at[k], part_got.at[k])

    def part_store(k):
        return pltpu.make_async_copy(low_c, own_part.at[k], stores.at[0, k])

    def grad_link(k):
        return to_partner(gates.at[k, :, :inner], other_grad.at[0, k], grad_send.at[k], grad_got.at[k])

    def grad_store(k):
        return pltpu.make_async_copy(gates.at[k, :, :inner], own_grad.at[k], stores.at[1, k])

    def passed(c, target, semaphores, by):
        return pltpu.make_async_remote_copy(
            src_ref=leaving.at[c], dst_ref=target.at[c], send_sem=semaphores.at[1, c], recv_sem=semaphores.at[0, c],
            device_id={"context": context + by}, device_id_type=MESH,
        )

    def up(c):
        return passed(c, state_in, states_up, 1)

    def down(c):
        return passed(c, arrived, states_down, -1)

    def pass_on(c, target, copy):
        copy.wait_recv()
        leaving[c] = (decay[c, :1] * target[c].astype(F32) + leaving[c].astype(F32)).astype(BF16)
        copy.start()

    def step_sizes(k):
        return step_raw.at[k]

    def age_of(k):
        return age_lanes.at[k]

    middle = below & above
    hops = count - 1 - context

    def fetch_features(k):
        return pltpu.make_async_copy(hid_all.at[k], gates.at[k, :, :model], stores.at[0, k])

    def w_in_block(slot):
        return w_in.at[pl.ds(pl.multiple_of(slot * rows, HALO), rows)]

    def both_block(slot):
        return both.at[slot]

    @pl.when(turn == 0)
    def _():
        for k in range(pieces_of(gates)):
            fetch_features(k).start()
        head_count = w_dt_t.shape[0]
        dt_rows[...] = jnp.zeros_like(dt_rows)
        for copy in range(3):
            dt_rows[copy * SLOTS : copy * SLOTS + head_count] = w_dt_t[...].astype(F32)
        stage_w[:, bc_width : bc_width + LANES] = dt_rows[...].T.astype(BF16)
        stage_w[:, bc_width + LANES :] = w_x[...]
        stage_w[:, cols] = w_bc[...]
        taps[...] = jnp.zeros_like(taps)
        taps[:5, cols] = conv_bc[...]
        taps[:5, bc_width:] = conv_x[...]
        greet([(True, partner), (True, {"shard": shard ^ 1}), (True, {"shard": shard ^ 2})]
              + [(True, {"context": context ^ k}) for k in range(1, count)])
        first_links = Numbered(others_sent)
        tail = pl.ds(length - HALO, HALO)
        first_copies = [(0, stage_w.at[:, cols], stage_w.at[:, cols], others.at[0], partner, True),
                        (1, taps.at[:, cols], taps.at[:, cols], others.at[1], partner, True),
                        (2, hid_all.at[:, tail], halo, others.at[2], {"context": context + 1}, above)]
        for copy in first_copies:
            first_links.start(*copy)
        first_links.arrived(stage_w.at[:, other_cols], others.at[0])
        half = in_width // 2 // LANES * LANES
        halves = []
        for k, cut in enumerate((slice(0, half), slice(half, in_width))):
            to = functools.partial(lambda slot, cut: w_in_block(slot).at[:, cut], cut=cut)
            halves.append((Numbered(send_w.at[k]), stage_w.at[:, cut], to, received_w.at[k]))
        for numbered_w, *refs in halves:
            gather_step(0, numbered_w.start, numbered_w.arrived, *refs)
        stage_in[:, :inner] = w_z[...]
        stage_in[:, inner:] = w_out_t[...]
        gather_step(0, numbered.start, numbered.arrived, stage_in, both_block, received)
        w_in_block(shard * count + context)[...] = stage_w[...]
        both[shard * count + context] = stage_in[...]
        lane = lax.broadcasted_iota(jnp.int32, (1, LANES), 1)
        slot = jnp.where(lane < 3 * SLOTS, lane % SLOTS, -1)
        lane_x = lax.broadcasted_iota(jnp.int32, (1, inner), 1)
        head_rows = [jnp.zeros((1, LANES), F32) for _ in range(8)]
        skips = jnp.zeros((1, inner), F32)
        for head in range(head_count):
            head_rows[0] = jnp.where(slot == head, dt_bias[head], head_rows[0])
            head_rows[1] = jnp.where(slot == head, a_log[head], head_rows[1])
            skips = jnp.where(lane_x // HEAD == head, skip_d[head], skips)
        heads[...] = jnp.concatenate(head_rows, 0)
        vectors[0:1] = norm_in_all[...].reshape(1, -1)
        vectors[1:2] = norm_gate_all[...].reshape(1, -1)
        vectors[2:3] = skips
        position = context * length + lax.broadcasted_iota(jnp.int32, (1, length), 1)
        for k in range(pieces_of(gates)):
            at = divmod(k, doc_start.shape[1])
            age = (position - doc_start[at[0], at[1] : at[1] + 1]).astype(F32)
            ages[k] = jnp.broadcast_to(age, (8, length))
        for k in range(pieces_of(gates)):
            fetch_features(k).wait()

        def one(k, carry):
            normalise(gates.at[k, :, :model], norm_in, normed.at[k, HALO:])
            return carry

        lax.fori_loop(0, pieces_of(gates), one, 0)
        for step in range(1, gather_steps()):
            for numbered_w, *refs in halves:
                gather_step(step, numbered_w.start, numbered_w.arrived, *refs)
        for step in range(gather_steps()):
            for numbered_w, *refs in halves:
                gather_step(step, numbered_w.sent, numbered_w.nothing, *refs)
        first_links.arrived(taps.at[:, other_cols], others.at[1])
        first_links.arrived(halo, others.at[2], below)
        for copy in first_copies:
            first_links.sent(*copy)

        @pl.when(jnp.logical_not(below))
        def _():
            halo[...] = jnp.zeros_like(halo)

        for sums in (sum_all, conv_sums, head_sums, norm_sums, inner_sums):
            sums[...] = jnp.zeros_like(sums)

    for c in range(len(UP_TURNS[0])):

        @pl.when((turn == jnp.where(context == 1, UP_TURNS[0][c], UP_TURNS[1][c])) & middle)
        def _(c=c):
            pass_on(c, state_in, up(c))

        @pl.when((turn == jnp.where(hops == 1, DOWN_TURNS[0][c], DOWN_TURNS[1][c])) & middle)
        def _(c=c):
            pass_on(c, arrived, down(c))

    @pl.when(phase == 0)
    def _():
        age_lanes[i] = jnp.broadcast_to(ages[i].T[:, :1], (length, LANES))
        age = age_of(i)
        normalise(halo.at[i], norm_in, normed.at[i, :HALO])
        project(age, w_in, taps, heads, spread, tri, normed.at[i], inputs.at[i],
                pre.at[i], step_raw.at[i], cum.at[i], leaving.at[i], decay.at[i], act, keep.at[:, :length], slope.at[:lead])

        @pl.when(jnp.logical_not(below))
        def _():
            state_in[i] = jnp.zeros(state_in.shape[1:], BF16)
            up(i).start()

    @pl.when(turn < 2 * pieces)
    def _():
        for step in range(1, gather_steps()):

            @pl.when(turn == GATHER_TURNS[step])
            def _(step=step):
                gather_step(step, numbered.start, numbered.arrived, stage_in, both_block, received)

        @pl.when(turn == 2 * pieces - 1)
        def _():
            for step in range(gather_steps()):
                gather_step(step, numbered.sent, numbered.nothing, stage_in, both_block, received)

    def w_z_all():
        return both[:, :, :inner].reshape(-1, inner)

    def w_out_all():
        return both[:, :, inner:].reshape(-1, inner)

    def gate_parts(k):
        return gates.at[k, :, :inner], gates.at[k, :, inner:]

    @pl.when(phase == 1)
    def _():
        mix_within(pre.at[i], step_sizes(i), cum.at[i], age_of(i), skip, heads, spread, near.at[i], seg, pair, step_x)

    @pl.when(phase == 2)
    def _():
        gate_products(normed.at[i], out_grad.at[0], w_z_all, w_out_all, *gate_parts(i))

        @pl.when(jnp.logical_not(above))
        def _():
            up(i).wait_recv()

        @pl.when(i >= 1)
        def _():
            part_link(i - 1).wait_send()
            part_store(i - 1).wait()

        mix_states(pre.at[i], cum.at[i], age_of(i), state_in.at[i], near.at[i], *gate_parts(i), w_out_all, norm_gate, spread,
                   near.at[i], low_c, stats.at[i], carried, low_a)
        stats_link(i).start()
        part_link(i).start()
        part_store(i).start()

        @pl.when(above)
        def _():
            up(i).wait_send()

    @pl.when((turn > 2 * pieces) & (turn <= 3 * pieces))
    def _():
        k = turn - 2 * pieces - 1
        stats_link(k).wait_recv()
        stats_out[k] = stats[k] + stats_in[k]
        gate, grad_gn = gate_parts(k)
        gate_back(inner_all, near.at[k], gate, grad_gn, stats_out.at[k], pre.at[k], cum.at[k], age_of(k), state_in.at[k],
                  normed.at[k], out_grad_last, norm_gate, spread, grad_gn, gate, grad_bc.at[k, :, LANES:],
                  leaving.at[k], inner_sums, sum_all.at[:, :inner], sum_all.at[:, inner:], carried, low_a, low_b)

        @pl.when(jnp.logical_not(above))
        def _():
            arrived[k] = jnp.zeros(arrived.shape[1:], BF16)
            down(k).start()

    @pl.when(phase == 2)
    def _():
        out_grad_last[...] = out_grad[0]

    @pl.when(turn == 3 * pieces)
    def _():
        part_link(pieces - 1).wait_send()
        part_store(pieces - 1).wait()
        gain_back(w_z_all(), sum_all.at[:, :inner], norm_sums)
        stage[...] = sum_all[...].reshape(stage.shape).astype(BF16)

    outer_links = Numbered(outer[5])

    @pl.when((turn >= OUTER_TURNS[0]) & (turn <= OUTER_END))
    def _():
        for step, when in enumerate(OUTER_TURNS):

            @pl.when(turn == when)
            def _(step=step):
                scatter_step(step, outer_links.start, outer_links.arrived, stage, sums_zo, *outer[:5])

        @pl.when(turn == OUTER_END)
        def _():
            for step in range(scatter_steps() - 1):
                scatter_step(step, outer_links.sent, outer_links.nothing, stage, sums_zo, *outer[:5], add=False)

    @pl.when(phase == 3)
    def _():
        within_back(near.at[i], pre.at[i], step_sizes(i), cum.at[i], ages.at[i], gates.at[i, :, inner:], skip, heads, spread, gather,
                    near.at[i], grad_cum.at[i], grad_bc.at[i], inner_sums, seg, pair, grad_pair, step_x, low_a,
                    low_b)

    @pl.when(phase == 4)
    def _():
        @pl.when(i == 0)
        def _():
            sum_all[...] = jnp.zeros_like(sum_all)
            clear_margins(slope, keep, length)

        @pl.when(jnp.logical_not(below))
        def _():
            down(i).wait_recv()

        state_back(arrived.at[i], state_in.at[i], pre.at[i], inputs.at[i], step_sizes(i), cum.at[i], age_of(i), near.at[i],
                   gates.at[i, :, inner:], grad_cum.at[i], grad_bc.at[i], taps, skip, heads, spread, gather, tri_up,
                   inputs.at[i], conv_sums, head_sums, step_x, carried, wide.at[:length, :inner], low_a, low_b, low_c,
                   slope, keep)
        sum_all[:, :in_width] += mm_tn(normed[i, HALO:], inputs[i, HALO:])

        @pl.when(below)
        def _():
            down(i).wait_send()

    last_stage = stage.at[:, :, : in_width - own_bc]
    last_links = Numbered(last_ones[5])

    def last_step(step):
        scatter_step(step, last_links.start, last_links.arrived, last_stage, sums_w, *last_ones[:5])

    @pl.when(turn == 5 * pieces - 1)
    def _():
        small[0] = to_rows([conv_sums[k] for k in range(5)])
        small[0, 5:6, model : model + LANES] = jnp.sum(head_sums[0], 0, keepdims=True)
        small[0, 5:6, model + LANES :] = jnp.sum(head_sums[1], 0, keepdims=True)
        small[0, 6:8, :inner] = to_rows([inner_sums[0], inner_sums[1]])[:2]
        small[0, 6:8, inner:] = jnp.zeros((2, channels - inner), F32)
        sum_all[:, :in_width] += mm_tn(
            normed[:, :HALO].reshape(-1, model), inputs[:, :HALO].reshape(-1, in_width)
        )
        half_out[...] = sum_all[:, other_cols].reshape(half_out.shape).astype(BF16)
        half_link().start()
        stage[:, :, own_bc : in_width - own_bc] = (
            sum_all[:, bc_width:in_width].reshape(16, rows, in_width - bc_width).astype(BF16)
        )
        gain_back(w_in, sum_all, norm_sums)
        small[0, 5:6, :model] = jnp.sum(norm_sums[...], 0, keepdims=True) / norm_in[...]
        small_link(0).start()

    def small_step(k):
        row = lax.broadcasted_iota(jnp.int32, small.shape[1:], 0)
        lane = lax.broadcasted_iota(jnp.int32, small.shape[1:], 1)
        shared = ((row < 5) & (lane < bc_width)) | ((row == 5) & (lane < model))
        small_link(k).wait_recv()
        small[k + 1] = small[k] + (jnp.where(shared, seen[k], 0.0) if k == 0 else seen[k])
        if k < 4:
            small_link(k + 1).start()

    for k, at in enumerate(SMALL_TURNS):
        pl.when(turn == 5 * pieces + at)(functools.partial(small_step, k))

    @pl.when(phase == 5)
    def _():
        features_back(inputs.at[i], gates.at[i, :, :inner], w_in, w_z_all, gates.at[i, :, :inner], tails.at[i], features)
        grad_link(i).start()
        grad_store(i).start()
        pl.when(below)(tail_link(i).start)

        @pl.when(jnp.logical_not(above))
        def _():
            for copy in tail_blanks(i):
                copy.start()

        @pl.when(above & (i >= 2))
        def _():
            tail_link(i - 2).wait_recv()
            tail_partner_link(i - 2).start()

        @pl.when(i == 0)
        def _():
            half_link().wait_recv()
            own_half = sum_all[:, cols].reshape(half_in.shape) + half_in[...].astype(F32)
            stage[:, :, :own_bc] = own_half.astype(BF16)
            last_step(0)

        @pl.when(i == 4)
        def _():
            last_step(1)

        @pl.when(i == 5)
        def _():
            last_step(2)

    @pl.when(turn == 6 * pieces - 1)
    def _():
        for k in (pieces_of(gates) - 2, pieces_of(gates) - 1):

            @pl.when(above)
            def _(k=k):
                tail_link(k).wait_recv()
                tail_partner_link(k).start()

        for step in range(3, scatter_steps()):
            last_step(step)
            if step in (5, 6):
                small_step(step - 2)
        total = small.at[5]
        conv_out[:, :own_bc] = total[:, cols]
        conv_out[:, own_bc:] = total[:, bc_width:]
        norm_out[...] = jnp.broadcast_to(total[5:6, :model], norm_out.shape)
        head_out[...] = jnp.zeros_like(head_out)
        head_out[0:1] = total[5:6, model : model + LANES]
        head_out[1:2] = total[5:6, model + LANES : model + 2 * LANES]
        inner_out[...] = jnp.zeros_like(inner_out)
        inner_out[0:2] = total[6:8, :inner]
        for k in range(pieces_of(gates)):

            @pl.when(above)
            def _(k=k):
                tail_partner_link(k).wait_recv()
                tail_partner_link(k).wait_send()

            @pl.when(jnp.logical_not(above))
            def _(k=k):
                for copy in tail_blanks(k):
                    copy.wait()

            pl.when(below)(tail_link(k).wait_send)
            grad_link(k).wait_recv()
            grad_link(k).wait_send()
            grad_store(k).wait()
            part_link(k).wait_recv()
            stats_link(k).wait_send()
        half_link().wait_send()
        for k in range(5):
            small_link(k).wait_send()
        for step in range(scatter_steps() - 1):
            scatter_step(step, last_links.sent, last_links.nothing, last_stage, sums_w, *last_ones[:5], add=False)


def pieces_of(array):
    return array.shape[0]


ANY = pl.BlockSpec(memory_space=pl.ANY)
IN_VMEM = pl.BlockSpec(memory_space=pltpu.VMEM)
DMA = pltpu.SemaphoreType.DMA


def gather_rows(rows):
    return lax.all_gather(rows, ("shard", "context"), axis=0, tiled=True)


def scatter_rows(rows):
    return lax.psum_scatter(rows.astype(F32), ("shard", "context"), scatter_dimension=0, tiled=True)


def passed_along(value, by):
    length = lax.axis_size("context")
    return lax.ppermute(value, "context", [(i, i + by) for i in range(length) if 0 <= i + by < length])


def chain(local, decay, by):
    arrived = jnp.zeros_like(local)
    for _ in range(lax.axis_size("context") - 1):
        leaving = decay[:, :1] * arrived.astype(F32) + local.astype(F32)
        arrived = passed_along(leaving.astype(BF16), by)
    return arrived


def exchange(value):
    everything = lax.all_gather(value, "tensor")
    return everything[0], everything[1:]


def part_of(width, at):
    return lambda array: pl.BlockSpec((array.shape[0], width), lambda i: (0, at))


class AnyMesh:
    def prepare(self, hid, doc_start, norm_in, norm_gate, dt_bias, a_log, skip_d, w_bc, w_dt, w_x, conv_bc, conv_x):
        pieces, length, _ = hid.shape
        head_count = w_dt.shape[1]

        def head_row(row):
            return jnp.pad(jnp.tile(jnp.pad(row, (0, SLOTS - head_count)), 3), (0, LANES - 3 * SLOTS))

        heads = jnp.stack([head_row(dt_bias), head_row(a_log)] + [jnp.zeros((LANES,), F32)] * 6)
        vectors = (norm_in[None], norm_gate[None], jnp.repeat(skip_d, HEAD)[None])
        position = lax.axis_index("context") * length + jnp.arange(length, dtype=jnp.int32)
        ages = (position - doc_start.reshape(pieces, length)).astype(F32)
        age = jnp.broadcast_to(ages[:, :, None], (pieces, length, LANES))
        age_row = jnp.broadcast_to(ages[:, None, :], (pieces, 8, length))
        conv_bc_all = lax.all_gather(conv_bc, "tensor", axis=1, tiled=True)
        taps = jnp.pad(jnp.concatenate([conv_bc_all, conv_x], 1), ((0, 3), (0, 0)))
        w_bc_all = lax.all_gather(w_bc, "tensor", axis=1, tiled=True)
        w_dt_wide = jnp.pad(jnp.tile(jnp.pad(w_dt, ((0, 0), (0, SLOTS - w_dt.shape[1]))), (1, 3)), ((0, 0), (0, LANES - 3 * SLOTS)))
        w_in = gather_rows(jnp.concatenate([w_bc_all, w_dt_wide, w_x], 1))
        return w_in, passed_along(hid[:, length - HALO :], 1), taps, heads, vectors, (age, age_row)

    def forward(self, hid, seed, prepared, w_z, w_out, spread, tri):
        w_in, halo, taps, heads, (norm_in, norm_gate, skip), (age, _) = prepared
        pieces, length, model = hid.shape
        inner, channels = w_z.shape[1], taps.shape[1]
        token = functools.partial(shaped, F32, pieces, length)
        token_low = functools.partial(shaped, BF16, pieces, length)
        normed, raw, pre, dt_raw, cum, local, decay = call(
            forward_local, pieces,
            [(hid, by_piece), (halo, by_piece), (age, by_piece), (norm_in, fixed), (w_in, fixed), (taps, fixed),
             (heads, fixed), (spread, fixed), (tri, fixed)],
            [(shaped(BF16, pieces, HALO + length, model), by_piece),
             (shaped(BF16, pieces, HALO + length, w_in.shape[1]), by_piece), (token_low(channels), by_piece),
             (token(LANES), by_piece), (token(LANES), by_piece), (shaped(BF16, pieces, LANES, inner), by_piece),
             (shaped(F32, pieces, 8, inner), by_piece)],
            [((length, channels), F32), ((3, length, LANES), F32), ((HALO + length, channels), F32)], "forward_local",
        )
        state_in = chain(local, decay, 1)
        w_z_all, w_out_t = gather_rows(w_z), gather_rows(w_out.T)
        square = ((length, length), F32)
        token_wide = ((length, inner), F32)
        mixer, gate, grad_gn, part, stats = call(
            forward_mix, pieces,
            [(pre, by_piece), (dt_raw, by_piece), (cum, by_piece), (age, by_piece), (state_in, by_piece),
             (normed, by_piece), (seed, by_piece), (w_z_all, fixed), (w_out_t, fixed), (norm_gate, fixed),
             (skip, fixed), (heads, fixed), (spread, fixed)],
            [(token(inner), by_piece), (token_low(inner), by_piece), (token_low(inner), by_piece),
             (token_low(model), by_piece), (shaped(F32, pieces, 8, length), by_piece)],
            [token_wide, square, square, token_wide, token_wide, ((length, inner), BF16)], "forward_mix",
        )
        return normed, raw, pre, dt_raw, cum, decay, state_in, mixer, gate, grad_gn, part, stats, (w_z_all, fixed)

    def backward(self, inner_all, hid, seed, prepared, saved, own_bc, spread, gather, tri_up):
        w_in, halo, taps, heads, (norm_in, norm_gate, skip), (age, age_row) = prepared
        normed, raw, pre, dt_raw, cum, decay, state_in, mixer, gate, grad_gn, part, stats, w_z_all = saved
        pieces, length, model = hid.shape
        inner, channels, in_width, lead = mixer.shape[2], taps.shape[1], w_in.shape[1], HALO + length
        token = functools.partial(shaped, F32, pieces, length)
        token_low = functools.partial(shaped, BF16, pieces, length)
        square, token_wide, token_narrow = ((length, length), F32), ((length, inner), F32), ((length, inner), BF16)
        stats = lax.psum(stats, "tensor")
        grad_fed, grad_mix, grad_gate, grad_cum, grad_bc, grad_state, grad_wz, grad_wo, sums = call(
            functools.partial(backward_local, inner_all), pieces,
            [(mixer, by_piece), (gate, by_piece), (grad_gn, by_piece), (stats, by_piece), (pre, by_piece),
             (dt_raw, by_piece), (cum, by_piece), (age, by_piece), (age_row, by_piece), (state_in, by_piece),
             (normed, by_piece), (seed, by_piece), (norm_gate, fixed), (skip, fixed), (heads, fixed), (spread, fixed),
             (gather, fixed)],
            [(token(inner), by_piece), (token_low(inner), by_piece), (token_low(inner), by_piece),
             (token(LANES), by_piece), (token(2 * LANES), by_piece), (shaped(BF16, pieces, LANES, inner), by_piece),
             (shaped(BF16, model, inner), fixed), (shaped(BF16, model, inner), fixed), (shaped(F32, 8, inner), fixed)],
            [((2, 8, inner), F32), ((model, inner), F32), ((model, inner), F32), square, square, square, token_wide, token_wide, token_narrow,
             token_narrow], "backward_local",
        )
        grad_later = chain(grad_state, decay, -1)
        grad_normed, grad_halo, grad_w, conv_sums, head_sums, norm_sums = call(
            backward_finish, pieces,
            [(grad_later, by_piece), (state_in, by_piece), (pre, by_piece), (raw, by_piece), (dt_raw, by_piece),
             (cum, by_piece), (age, by_piece), (grad_fed, by_piece), (grad_mix, by_piece), (grad_cum, by_piece),
             (grad_bc, by_piece), (grad_gate, by_piece), (normed, by_piece), (hid, by_piece), (halo, by_piece),
             (w_in, fixed), w_z_all, (taps, fixed), (skip, fixed), (heads, fixed), (spread, fixed), (gather, fixed),
             (tri_up, fixed)],
            [(token_low(model), by_piece), (shaped(BF16, pieces, HALO, model), by_piece),
             (shaped(BF16, model, in_width), fixed), (shaped(F32, 8, channels), fixed), (shaped(F32, 8, LANES), fixed),
             (shaped(F32, 8, model), fixed)],
            [((5, 8, channels), F32), ((2, 8, LANES), F32), ((8, model), F32), ((model, in_width), F32), token_wide,
             token_wide, token_wide, token_narrow, token_narrow, token_narrow, ((lead + 8, channels), F32), ((3, lead + 8, LANES), F32),
             ((lead, in_width), BF16), ((lead, model), F32)],
            "backward_finish",
        )
        sums_zo = jnp.concatenate([scatter_rows(grad_wz), scatter_rows(grad_wo)], 1)
        mine, bc_width = lax.axis_index("tensor"), 2 * LANES
        grad_w = scatter_rows(grad_w)
        grad_w_bc = lax.psum_scatter(grad_w[:, :bc_width], "tensor", scatter_dimension=1, tiled=True)
        norm_sums, conv_bc = lax.psum((norm_sums, conv_sums[:, :bc_width]), ("shard", "context", "tensor"))
        conv_x, head_sums, sums = lax.psum((conv_sums[:, bc_width:], head_sums, sums), ("shard", "context"))
        conv_bc = lax.dynamic_slice_in_dim(conv_bc, mine * own_bc, own_bc, 1)
        sums_w = jnp.concatenate([grad_w_bc, grad_w[:, bc_width:]], 1)
        small = (jnp.concatenate([conv_bc, conv_x], 1), norm_sums, head_sums, sums)
        return stats, sums_zo, sums_w, small, exchange(part), exchange(grad_normed), exchange(passed_along(grad_halo, -1))

    def run(self, inner_all, hid, seed, prepared, w_z, w_out, own_bc, spread, gather, tri, tri_up):
        saved = self.forward(hid, seed, prepared, w_z, w_out, spread, tri)
        return self.backward(inner_all, hid, seed, prepared, saved, own_bc, spread, gather, tri_up)


class FourByFourByTwo:
    def prepare(self, hid, *parameters):
        return parameters

    def run(self, inner_all, hid, seed, prepared, w_z, w_out, own_bc, spread, gather, tri, tri_up):
        doc_start, norm_in, norm_gate, dt_bias, a_log, skip_d, w_bc, w_dt, w_x, conv_bc, conv_x = prepared
        pieces, length, model = hid.shape
        rows, inner = w_z.shape
        channels, in_width, lead = 2 * LANES + inner, 3 * LANES + inner, HALO + length
        width = in_width - own_bc

        def gradients(p, i):
            return (jnp.where(p == 2, i, jnp.where(p < 2, 0, pieces - 1)), 0, 0)

        def block_of(where):
            return lambda array: pl.BlockSpec((1,) + array.shape[1:], where)

        def once(array):
            return pl.BlockSpec(array.shape, lambda p, i: (0,) * array.ndim, pipeline_mode=pl.Buffered(1))

        kept = once

        def anywhere(array):
            return ANY

        def vmem(kind, *dims):
            return pltpu.VMEM(dims, kind)

        token_low, tail = shaped(BF16, pieces, length, model), shaped(BF16, pieces, HALO, model)
        stats = shaped(F32, pieces, 8, length)
        def in_smem(array):
            return pl.BlockSpec(memory_space=pltpu.SMEM)

        inputs = [(seed, block_of(gradients)), (hid, anywhere), (doc_start, once), (w_bc, once),
                  (w_dt.T, once), (w_x, once), (conv_bc, once), (conv_x, once), (norm_in, once), (norm_gate, once),
                  (dt_bias, in_smem), (a_log, in_smem), (skip_d, in_smem), (w_z, once), (w_out.T, once), (spread, once),
                  (gather, once), (tri, once), (tri_up, once)]
        outputs = [(stats, kept), (shaped(F32, rows, 2 * inner), kept), (shaped(F32, rows, width), kept),
                   (shaped(F32, 8, channels - own_bc), kept), (shaped(F32, 8, model), kept), (shaped(F32, 8, LANES), kept),
                   (shaped(F32, 8, inner), kept), (token_low, anywhere), (shaped(BF16, 1, *token_low.shape), anywhere),
                   (token_low, anywhere), (shaped(BF16, 1, *token_low.shape), anywhere), (tail, anywhere),
                   (shaped(BF16, 1, *tail.shape), anywhere)]
        state, square, low = vmem(BF16, pieces, LANES, inner), vmem(F32, length, length), vmem(BF16, length, inner)
        per_piece = DMA((pieces,))
        scratch = [
            vmem(BF16, *tail.shape), vmem(F32, *stats.shape), vmem(F32, pieces, length, LANES), vmem(F32, 8, inner),
            vmem(BF16, model, in_width),
            vmem(F32, 8, channels), vmem(F32, 8, LANES), vmem(BF16, rows, in_width), vmem(F32, LANES, rows),
            vmem(BF16, length, model),
            vmem(BF16, pieces, lead, model), vmem(BF16, pieces, length, channels), vmem(F32, pieces, length, LANES),
            vmem(BF16, pieces, length, 2 * inner), vmem(F32, pieces, length, inner), vmem(BF16, pieces, lead, in_width),
            state, state, state, vmem(F32, pieces, 8, inner), vmem(BF16, 16, rows, 2 * inner),
            vmem(F32, pieces, length, 2 * LANES), vmem(F32, pieces, length, LANES), vmem(F32, model, 2 * inner),
            vmem(BF16, rows, 2 * inner), vmem(BF16, 16, rows, 2 * inner), vmem(BF16, 16, rows, own_bc),
            vmem(BF16, 16, rows, own_bc), vmem(F32, length, inner), vmem(F32, length, inner), low, low, low,
            vmem(F32, lead + 8, channels), vmem(F32, 3, lead + 8, LANES), vmem(F32, lead, channels), square, square,
            square, vmem(F32, pieces, length, LANES), vmem(BF16, *tail.shape),
            vmem(F32, *stats.shape), vmem(F32, *stats.shape), vmem(F32, 6, 8, channels),
            vmem(F32, 5, 8, channels), vmem(F32, 5, 8, channels), vmem(F32, 2, 8, LANES), vmem(F32, 8, model),
            vmem(F32, 2, 8, inner), DMA((2, GATHER_COPIES)), DMA((2, 16)), DMA((3,)), DMA((3,)), DMA((GATHER_COPIES,)),
            DMA((16,)), DMA((2, pieces)), DMA((2, pieces)), DMA((8,)),
            DMA((8,)), per_piece, per_piece, per_piece, per_piece, per_piece, per_piece, DMA((2, pieces)),
            DMA((2, pieces)), DMA((2, pieces)),
        ]
        (stats, sums_zo, sums_w, conv_sums, norm_sums, head_sums, sums, own_part, other_part, own_grad, other_grad,
         own_tail, other_tail) = pl.pallas_call(
            functools.partial(block, inner_all),
            grid=(6, pieces),
            in_specs=[cut(array) for array, cut in inputs],
            out_specs=[cut(shape) for shape, cut in outputs],
            out_shape=[shape for shape, _ in outputs],
            scratch_shapes=scratch + scatter_scratch(rows, 2 * inner) + scatter_scratch(rows, width),
            compiler_params=pltpu.CompilerParams(
                collective_id=1, has_side_effects=True, vmem_limit_bytes=BLOCK_VMEM_BYTES
            ),
            name="block",
        )(*[array for array, _ in inputs])
        small = (conv_sums, norm_sums, head_sums, sums)
        return stats, sums_zo, sums_w, small, (own_part, other_part), (own_grad, other_grad), (own_tail, other_tail)


def links():
    sizes = tuple(lax.axis_size(axis) for axis in ("shard", "context", "tensor"))
    return FourByFourByTwo() if sizes == (4, 4, 2) else AnyMesh()


def shards(inner_all, hidden_in, out_grad, doc_start, norm_in, w_z, w_x, w_bc, w_dt, conv_x, conv_bc, dt_bias, a_log,
           skip_d, norm_gate, w_out):
    micro, per_device, length, model = hidden_in.shape
    pieces = micro * per_device
    inner = w_z.shape[1]
    head_count, own_bc = w_dt.shape[1], w_bc.shape[1]

    head_of = np.arange(inner) // HEAD
    slot = np.where(np.arange(LANES) < 3 * SLOTS, np.arange(LANES) % SLOTS, -1)
    gather = jnp.asarray(head_of[:, None] == np.arange(LANES)[None], BF16)
    spread = jnp.asarray(head_of[None] == slot[:, None], BF16)
    tri = jnp.asarray(np.tril(np.ones((length, length))), BF16)
    tri_up = jnp.asarray(np.triu(np.ones((length, length))), BF16)

    hid = hidden_in.reshape(pieces, length, model)
    seed = out_grad.reshape(pieces, length, model)
    between = links()
    prepared = between.prepare(
        hid, doc_start, norm_in, norm_gate, dt_bias, a_log, skip_d, w_bc, w_dt, w_x, conv_bc, conv_x
    )
    stats, sums_zo, sums_w, small, (own_part, other_part), (own_grad, other_grad), (own_tail, other_tail) = (
        between.run(inner_all, hid, seed, prepared, w_z, w_out, own_bc, spread, gather, tri, tri_up)
    )
    token_low = functools.partial(shaped, BF16, pieces, length)
    rows = w_z.shape[0]
    outputs = [shaped(F32, rows, inner), shaped(F32, rows, inner), shaped(F32, rows, own_bc),
               shaped(F32, head_count, rows), shaped(F32, rows, inner), shaped(F32, 5, inner), shaped(F32, 5, own_bc),
               shaped(F32, 1, head_count), shaped(F32, 1, head_count), shaped(F32, 1, head_count),
               shaped(F32, inner), shaped(F32, model)]
    (out, in_grad, grad_wz, grad_wx, grad_wbc, grad_wdt, grad_wo, grad_conv_x, grad_conv_bc, grad_dt_bias, grad_a_log,
     grad_skip, grad_norm_gate, grad_norm_in) = call(
        functools.partial(finish, inner_all), pieces // SPAN,
        [(hid, by_span), (seed, by_span), (stats, by_span), (norm_in, fixed), (own_part, by_span),
         (other_part, by_span_second), (own_grad, by_span), (other_grad, by_span_second), (own_tail, by_span),
         (other_tail, by_span_second), (sums_zo, fixed), (sums_w, fixed)] + [(array, fixed) for array in small]
        + [(gather, fixed)],
        [(token_low(model), by_span), (token_low(model), by_span)] + [(shape, fixed) for shape in outputs],
        [((length, model), F32)], "finish",
    )
    return (
        out.reshape(hidden_in.shape),
        in_grad.reshape(hidden_in.shape),
        grad_norm_in,
        grad_wz,
        grad_wx,
        grad_wbc,
        grad_wdt.T,
        grad_conv_x,
        grad_conv_bc,
        grad_dt_bias[0],
        grad_a_log[0],
        grad_skip[0],
        grad_norm_gate,
        grad_wo.T,
    )


def solution(mesh):
    whole = P(None, "shard", "context", None)
    rows = P(("shard", "context"), "tensor")
    lanes = P(None, "tensor")
    heads = P("tensor")
    w_out = P("tensor", ("shard", "context"))
    inputs = (whole, whole, P(None, "shard", "context"), P(), rows, rows, rows, rows, lanes, lanes, heads, heads, heads, heads, w_out)
    outputs = (whole, whole, P(), rows, rows, rows, rows, lanes, lanes, heads, heads, heads, heads, w_out)

    def placed(*arrays):
        inner_all = arrays[4].shape[1]
        return jax.shard_map(
            functools.partial(shards, inner_all), mesh=mesh, in_specs=inputs, out_specs=outputs, check_vma=False
        )(*arrays)

    return placed
```
